32 devices in a mesh: dp: 16 (over z, y, x), mp: 2 (over core).
Axes of the slice: x: 2, y: 2, z: 4, core: 2. Of those that a mesh axis runs over, the one named last changes fastest.
Arguments:
- tokens: bfloat16 [16384, 768], P(('dp', 'mp')), may hold values from -6 to 6
- seg_ids: int32 [32, 512], P('dp'), may hold values from 0 to 3, never falling along the last dimension, each value on 1 to 256 neighbouring positions
- fill_len: int32 [32], P('dp'), may hold values from 256 to 512, as said below
- qkv_weight: bfloat16 [768, 3, 768], P(None, None, 'mp'), may hold values from -0.21875 to 0.21875
- qv_bias: float32 [2, 768], P(None, 'mp'), may hold values from -3 to 3
- out_weight: bfloat16 [768, 768], replicated, may hold values from -0.875 to 0.875
- out_bias: float32 [768], replicated, may hold values from -2 to 2
- norm1_gain: float32 [768], replicated, may hold values from 0.1 to 1.9
- norm1_bias: float32 [768], replicated, may hold values from -2 to 2
- in_weight: bfloat16 [768, 3072], replicated, may hold values from -0.21875 to 0.21875
- in_bias: float32 [3072], replicated, may hold values from -3 to 3
- down_weight: bfloat16 [3072, 768], replicated, may hold values from -0.15625 to 0.15625
- down_bias: float32 [768], replicated, may hold values from -2 to 2
- norm2_gain: float32 [768], replicated, may hold values from 0.1 to 1.9
- norm2_bias: float32 [768], replicated, may hold values from -2 to 2
- act_range: float32 [4], replicated, may hold values from 1.5 to 3
- cotangent: bfloat16 [16384, 768], P(('dp', 'mp')), may hold values from -6 to 6
Outputs:
- layer_out: bfloat16 [16384, 768], P(('dp', 'mp'))
- grad_tokens: float32 [16384, 768], P(('dp', 'mp'))
- grad_qkv_weight: float32 [768, 3, 768], P(None, None, ('mp', 'dp'))
- grad_qv_bias: float32 [2, 768], P(None, ('mp', 'dp'))
- grad_out_weight: float32 [768, 768], P(('dp', 'mp'))
- grad_out_bias: float32 [768], P(('dp', 'mp'))
- grad_norm1_gain: float32 [768], P(('dp', 'mp'))
- grad_norm1_bias: float32 [768], P(('dp', 'mp'))
- grad_in_weight: float32 [768, 3072], P(('dp', 'mp'))
- grad_in_bias: float32 [3072], P(('dp', 'mp'))
- grad_down_weight: float32 [3072, 768], P(('dp', 'mp'))
- grad_down_bias: float32 [768], P(('dp', 'mp'))
- grad_norm2_gain: float32 [768], P(('dp', 'mp'))
- grad_norm2_bias: float32 [768], P(('dp', 'mp'))
- new_range: float32 [4], replicated
The draws below stay inside these ranges and needn't reach their ends.
Inputs may be any that keep to these rules, and one draw needn't show every extreme that they name: `seg_ids`: within a packed row the document numbers never fall; each document covers 1 to 256 positions and some document covers exactly that many. `fill_len`: some packed row is full in every draw.
All inputs are finite; a program needn't handle non-finite values.
Results may differ from the reference program's by a relative error of at most 0.012.
Values may be sent and summed in bfloat16 or wider, within the bound.
A program may use at most 192 MiB of HBM per device.

```python
import math
import jax
import jax.numpy as jnp
import numpy as np
from jax import lax

D = 768
HEADS = 12
HD = 64
FF = 3072
SEQ = 512
DOCS = 4
ROWS = 32
TOKENS = 16384


def draw_fill_len(key, part):
    key = jax.random.fold_in(key, 11)
    base_key, pick_key = jax.random.split(key)
    lengths = jax.random.randint(base_key, (ROWS,), SEQ // 2, SEQ + 1)
    chosen = jax.random.randint(pick_key, (), 0, ROWS)
    return jnp.where(jnp.arange(ROWS) == chosen, SEQ, lengths).astype(jnp.int32)


def shard_levels(stream_key, dims, shards, least, high):
    level, own = 1.0, jax.random.fold_in(stream_key, 6)
    for dim, shards_of in shards:
        heights = jnp.exp(jax.random.uniform(jax.random.fold_in(own, dim), (shards_of,), jnp.float32, least / len(shards), high / len(shards)))
        level = level * jnp.repeat(heights, dims[dim] // shards_of).reshape([-1 if axis == dim else 1 for axis in range(len(dims))])
    return level


def length_profile(count, total, most, lean):
    loads = [(1 << 20) // math.isqrt(rank ** lean) + 1 for rank in range(2, count + 1)]
    rest, counts = total - most - (count - 1), [1] * (count - 1)
    while rest > 0:
        candidates = [i for i in range(count - 1) if counts[i] < most]
        whole, left = sum([loads[i] for i in candidates]), rest
        for i in candidates:
            extra = min(most - counts[i], max(1, left * loads[i] // whole), rest)
            counts[i] = counts[i] + extra
            rest = rest - extra
    return np.array([most] + counts)


def uneven_parts(rng, amount, total, limit, skew):
    if amount == 2:
        one = jax.random.randint(rng, (), max(1, total - limit), min(limit, total - 1) + 1)
        return jnp.stack([one, total - one])
    tallies = jnp.asarray(length_profile(amount, total, limit, skew), jnp.int32)
    couples = (amount - 1) // 2
    giver, sink = tallies[1:1 + 2 * couples:2], tallies[2:2 + 2 * couples:2]
    slack = jnp.minimum(giver - 1, limit - sink)
    shifted = jax.random.randint(jax.random.fold_in(rng, 1), (couples,), 0, 1 << 20) % (slack + 1)
    tallies = tallies.at[1:1 + 2 * couples:2].set(giver - shifted).at[2:2 + 2 * couples:2].set(sink + shifted)
    return tallies[jax.random.permutation(jax.random.fold_in(rng, 2), amount)]


def gaussian(own_key, dims, scale, limit, cuts=(), kind=jnp.bfloat16):
    entries = scale * jax.random.normal(own_key, dims, jnp.float32)
    if cuts:
        entries = entries * shard_levels(own_key, dims, cuts, -0.22, 0.18)
    return jnp.clip(entries, -limit, limit).astype(kind)


def setup_inputs(seed: int = 0) -> dict:
    key_list = jax.random.split(jax.random.key(seed), 18)
    return {
        "tokens": gaussian(key_list[0], (TOKENS, D), 1.0, 6.0, ((0, 32),)),
        "seg_ids": jax.vmap(lambda own: jnp.searchsorted(jnp.cumsum(uneven_parts(own, DOCS, SEQ, SEQ // 2, 0)), jnp.arange(SEQ), side="right"))(jax.random.split(key_list[1], ROWS)).reshape((ROWS, SEQ)).astype(jnp.int32),
        "fill_len": draw_fill_len(jax.random.fold_in(key_list[17], 71), 0),
        "qkv_weight": gaussian(key_list[3], (D, 3, D), D ** -0.5, 0.21875, ((2, 2),)),
        "qv_bias": gaussian(key_list[4], (2, D), 0.5, 3.0, ((1, 2),), jnp.float32),
        "out_weight": gaussian(key_list[5], (D, D), (D // 16) ** -0.5, 0.875),
        "out_bias": gaussian(key_list[6], (D,), 0.3, 2.0, (), jnp.float32),
        "norm1_gain": jnp.clip(1.0 + 0.18 * jax.random.normal(key_list[7], (D,), jnp.float32), 0.1, 1.9),
        "norm1_bias": gaussian(key_list[8], (D,), 0.3, 2.0, (), jnp.float32),
        "in_weight": gaussian(key_list[9], (D, FF), D ** -0.5, 0.21875),
        "in_bias": gaussian(key_list[10], (FF,), 0.5, 3.0, (), jnp.float32),
        "down_weight": gaussian(key_list[11], (FF, D), (FF // 2) ** -0.5, 0.15625),
        "down_bias": gaussian(key_list[12], (D,), 0.3, 2.0, (), jnp.float32),
        "norm2_gain": jnp.clip(1.0 + 0.18 * jax.random.normal(key_list[13], (D,), jnp.float32), 0.1, 1.9),
        "norm2_bias": gaussian(key_list[14], (D,), 0.3, 2.0, (), jnp.float32),
        "act_range": jnp.clip(jax.random.uniform(key_list[15], (4,), jnp.float32, 1.5, 3.0), 1.5, 3.0),
        "cotangent": gaussian(key_list[16], (TOKENS, D), 1.0, 6.0, ((0, 32),)),
    }


EPSILON = 1e-06
MOMENTUM = 0.9

@jax.custom_vjp
def low(v):
    return lax.optimization_barrier(v.astype(jnp.bfloat16)).astype(jnp.float32)

@jax.custom_vjp
def low_back(v):
    return v

def low_keep(v):
    return (low(v), None)

def low_pass(kept, grad):
    return (grad,)

def back_keep(v):
    return (v, None)

def back_low(kept, grad):
    return (low(grad),)
low.defvjp(low_keep, low_pass)
low_back.defvjp(back_keep, back_low)

def both_round(values_in):
    return low_back(low(values_in))

def soft_clip(values_in, clip_limit):
    return clip_limit * jnp.tanh(values_in / clip_limit)

def layer_norm(hidden, norm_gain, norm_shift):
    center = hidden - lax.optimization_barrier(jnp.mean(hidden, axis=-1, keepdims=True))
    inv_std = lax.rsqrt(lax.optimization_barrier(jnp.mean(center * center, axis=-1, keepdims=True)) + EPSILON)
    return center * inv_std * norm_gain + norm_shift

def attend_mask(seg_rows, fill_rows):
    positions = jnp.arange(seg_rows.shape[1], dtype=jnp.int32)
    same_doc = seg_rows[:, :, None] == seg_rows[:, None, :]
    live_key = positions[None, None, :] < fill_rows[:, None, None]
    diagonal = positions[:, None] == positions[None, :]
    return same_doc & (live_key | diagonal[None])

def group_layer(weights, act_range, x_rows, seg_rows, fill_rows):
    qkv_weight, qv_bias, out_weight, out_bias, norm1_gain, norm1_bias, in_weight, in_bias, down_weight, down_bias, norm2_gain, norm2_bias = weights
    n_rows = seg_rows.shape[0]
    highest = lax.Precision.HIGHEST
    clip_in = low(soft_clip(x_rows, act_range[0]))
    packed = jnp.dot(clip_in, qkv_weight.reshape(D, 3 * D), precision=highest)
    head_shape = (n_rows, SEQ, HEADS, HD)
    queries = both_round(packed[:, :D] + qv_bias[0]).reshape(head_shape)
    key_rows = both_round(packed[:, D:2 * D]).reshape(head_shape)
    value_rows = both_round(packed[:, 2 * D:] + qv_bias[1]).reshape(head_shape)
    scores = jnp.einsum('rqhd,rkhd->rhqk', queries, key_rows, precision=highest) * HD ** (-0.5)
    scores = low_back(scores)
    key_mask = attend_mask(seg_rows, fill_rows)[:, None]
    row_max = lax.optimization_barrier(jnp.max(jnp.where(key_mask, scores, -1e+30), axis=-1, keepdims=True))
    unnormed = jnp.where(key_mask, jnp.exp(jnp.where(key_mask, scores - row_max, -80.0)), 0.0)
    probs = low(unnormed / lax.optimization_barrier(jnp.sum(unnormed, axis=-1, keepdims=True)))
    context = jnp.einsum('rhqk,rkhd->rqhd', probs, value_rows, precision=highest)
    context = low_back(context).reshape(n_rows * SEQ, D)
    mixed = both_round(soft_clip(context, act_range[1]))
    attn_out = low_back(jnp.dot(mixed, out_weight, precision=highest) + out_bias)
    normed = layer_norm(x_rows + attn_out, norm1_gain, norm1_bias)
    clip_mid = low(soft_clip(normed, act_range[2]))
    pre_act = low_back(jnp.dot(clip_mid, in_weight, precision=highest) + in_bias)
    activated = jax.nn.gelu(pre_act, approximate=False)
    clip_act = low(soft_clip(activated, act_range[3]))
    branch = low_back(jnp.dot(clip_act, down_weight, precision=highest) + down_bias)
    result = layer_norm(normed + branch, norm2_gain, norm2_bias)
    peaks = jnp.stack([jnp.max(jnp.abs(x_rows)), jnp.max(jnp.abs(context)), jnp.max(jnp.abs(normed)), jnp.max(jnp.abs(activated))])
    return (result, peaks)

def reference(tokens, seg_ids, fill_len, qkv_weight, qv_bias, out_weight, out_bias, norm1_gain, norm1_bias, in_weight, in_bias, down_weight, down_bias, norm2_gain, norm2_bias, act_range, cotangent):
    group_rows = math.gcd(ROWS, max(1, 4096 // SEQ))
    group_count = ROWS // group_rows
    weights = tuple((item.astype(jnp.float32) for item in (qkv_weight, qv_bias, out_weight, out_bias, norm1_gain, norm1_bias, in_weight, in_bias, down_weight, down_bias, norm2_gain, norm2_bias)))
    x_float = tokens.astype(jnp.float32).reshape(group_count, group_rows * SEQ, D)
    seg_groups = seg_ids.reshape(group_count, group_rows, SEQ)
    fill_groups = fill_len.reshape(group_count, group_rows)
    checked = jax.checkpoint(group_layer)

    def forward(x_all, *params):

        def scan_step(carry, pieces):
            x_rows, seg_rows, fill_rows = pieces
            result, peaks = checked(params, act_range, x_rows, seg_rows, fill_rows)
            return (carry, (result, peaks))
        carry_end, (results, peaks) = lax.scan(scan_step, jnp.zeros((), jnp.float32), (x_all, seg_groups, fill_groups))
        return (results, lax.optimization_barrier(jnp.max(peaks, axis=0)))
    results, pullback, peaks = jax.vjp(forward, x_float, *weights, has_aux=True)
    gradients = pullback(cotangent.astype(jnp.float32).reshape(group_count, group_rows * SEQ, D))
    new_range = MOMENTUM * act_range + (1.0 - MOMENTUM) * peaks
    layer_out = results.reshape(TOKENS, D).astype(jnp.bfloat16)
    return (layer_out, gradients[0].reshape(TOKENS, D), gradients[1], gradients[2], gradients[3], gradients[4], gradients[5], gradients[6], gradients[7], gradients[8], gradients[9], gradients[10], gradients[11], gradients[12], new_range)
```

```python
import functools
import math

import jax
import jax.numpy as jnp
from jax import lax
from jax.experimental import pallas as pl
from jax.experimental.pallas import tpu as pltpu
from jax.sharding import PartitionSpec as P

HD = 64
EPSILON = 1e-06
MOMENTUM = 0.9
SQRT_HALF = math.sqrt(0.5)
INV_SQRT_2PI = 1.0 / math.sqrt(2.0 * math.pi)
LOW = jnp.bfloat16
WIDE = jnp.float32
MESH = pl.DeviceIdType.MESH

ORDER_A, ORDER_B, ORDER_C = (0, 1, 2, 3), (1, 0, 2, 3), (2, 3, 0, 1)
MESSAGES = (
    ("down", 0, ORDER_A),
    ("down", 1, ORDER_B),
    ("down", 2, ORDER_C),
    ("wide", 0, ORDER_A),
    ("wide", 1, ORDER_B),
    ("wide", 2, ORDER_A),
    ("wide", 3, ORDER_B),
    ("wide", 4, ORDER_C),
    ("wide", 5, ORDER_A),
    ("wide", 6, ORDER_B),
    ("wide", 7, ORDER_A),
)
N_MSG = len(MESSAGES)
DOWN0, IN0, OUT0, QKV0 = 0, 3, 7, 8


def dot(a, b):
    return lax.dot_general(a, b, (((1,), (0,)), ((), ())), preferred_element_type=WIDE)


def dot_nt(a, b):
    return lax.dot_general(a, b, (((1,), (1,)), ((), ())), preferred_element_type=WIDE)


def dot_tn(a, b):
    return lax.dot_general(a, b, (((0,), (0,)), ((), ())), preferred_element_type=WIDE)


def place(chunk, order):
    spot = 0
    for bit in order:
        spot = spot * 2 + (chunk >> bit) % 2
    return spot


class Scatter:
    def __init__(self, n_low, acc, csend, crecv, recvs, send_sem, recv_sem):
        self.acc, self.csend, self.crecv, self.recvs = acc, csend, crecv, recvs
        self.send_sem, self.recv_sem = send_sem, recv_sem
        self.dp, self.mp = lax.axis_index("dp"), lax.axis_index("mp")
        self.n_low = n_low
        self.slot_user = {}
        self.pending = []
        self.next = {}

    def bit(self, bit):
        return (self.dp // (self.n_low << bit)) % 2

    def partner(self, bit):
        return (self.dp + (self.n_low << bit) * (1 - 2 * self.bit(bit)), self.mp)

    def slot(self, m):
        group, index, _ = MESSAGES[m]
        return self.csend[group].at[index % 2]

    def core_copy(self, m):
        group, index, _ = MESSAGES[m]
        return pltpu.make_async_remote_copy(
            src_ref=self.slot(m),
            dst_ref=self.crecv[group].at[index],
            send_sem=self.send_sem.at[m, 0],
            recv_sem=self.recv_sem.at[m, 0],
            device_id=(self.dp, 1 - self.mp),
            device_id_type=MESH,
        )

    def base(self, m, stage):
        order = MESSAGES[m][2]
        spot = 0
        for k in range(stage):
            spot = spot + self.bit(order[k]) * (8 >> k)
        return spot

    def copy(self, m, stage):
        group, index, order = MESSAGES[m]
        count = 16 >> stage
        bit = order[stage - 1]
        start = self.base(m, stage - 1) + (1 - self.bit(bit)) * count
        return pltpu.make_async_remote_copy(
            src_ref=self.acc[group].at[index, pl.ds(start, count)],
            dst_ref=self.recvs[group][stage - 1].at[index],
            send_sem=self.send_sem.at[m, stage],
            recv_sem=self.recv_sem.at[m, stage],
            device_id=self.partner(bit),
            device_id_type=MESH,
        )

    def slot_free(self, m):
        group, index, _ = MESSAGES[m]
        old = self.slot_user.get((group, index % 2))
        if old is not None:
            self.core_copy(old).wait_send()
            self.pending.remove((old, 0))
        self.slot_user[(group, index % 2)] = m

    def send_core(self, m):
        self.core_copy(m).start()
        self.pending.append((m, 0))
        self.next[m] = 0

    def add(self, m, received, from_, start, count):
        group, index, _ = MESSAGES[m]
        acc = self.acc[group]
        here = pl.ds(start, count)
        acc[index, here] = acc[index, here] + received[index, pl.ds(from_, count)]

    def step(self, m, stage, out=None):
        group, index, order = MESSAGES[m]
        assert self.next[m] == stage
        self.next[m] = stage + 1
        (self.core_copy(m) if stage == 0 else self.copy(m, stage)).wait_recv()
        if stage == 4:
            total = self.acc[group][index, self.base(m, 4)].astype(WIDE) + self.recvs[group][3][index, 0].astype(WIDE)
            out(total)
            return
        received = self.crecv[group] if stage == 0 else self.recvs[group][stage - 1]
        count = 8 >> stage
        base = self.base(m, stage)
        mine = self.bit(order[stage])
        self.add(m, received, (1 - mine) * count, base + (1 - mine) * count, count)
        self.copy(m, stage + 1).start()
        self.pending.append((m, stage + 1))
        self.add(m, received, mine * count, base + mine * count, count)

    def finish(self):
        for m, stage in self.pending:
            (self.core_copy(m) if stage == 0 else self.copy(m, stage)).wait_send()


def store_down(ref, first, result, order):
    for chunk in range(16):
        ref[(*first, place(chunk, order))] = result[32 * chunk : 32 * chunk + 32].astype(LOW)


def store_wide(ref, first, result, order):
    half = result.shape[1] // 2
    for chunk in range(16):
        rows = result[24 * chunk : 24 * chunk + 24]
        ref[(*first, place(chunk, order))] = jnp.concatenate([rows[:, :half], rows[:, half:]], axis=0).astype(LOW)


def interleave(ref, values):
    for part in range(2):
        flipped = values(part).T
        for core in range(2):
            groups = [flipped[24 * i : 24 * i + 24] for i in range(core, 16, 2)]
            ref[core, 192 * part : 192 * part + 192, :] = jnp.concatenate(groups, axis=0).astype(LOW)


def kernel(
    n_dp, n_low, upto,
    tok_h, seg_v, fill_s, qkvw_h, qvb_v, outw_h, outb_v, g1_v, b1_v, inw_h, inb_v, downw_h, downb_v, g2_v, b2_v, act_v, cot_h,
    lay_h, gtok_h, gqkv, gout, gin, gdown, small_o,
    tok, cot, wqkv, qvb, wout, win, wdown, clip_in, qkv, bias, ctx, stats, mixed_t, xhat1, clip_mid, clip_mid_t, clip_act_t, slope_f, h2, d_h1, sm, sm_r,
    acc_d, acc_w, cs_d, cs_w, cr_d, cr_w, rd1, rd2, rd3, rd4, rw1, rw2, rw3, rw4,
    loc_sem, wsend, wrecv, msend, mrecv, ssend, srecv,
):
    dp, mp = lax.axis_index("dp"), lax.axis_index("mp")
    n_bits = n_dp.bit_length() - 1
    tokens, width = tok.shape
    hidden = win.shape[1]
    half = width // 2
    other = 1 - mp
    core_id = (dp, other)

    local = [
        pltpu.make_async_copy(src, dst, loc_sem.at[i])
        for i, (src, dst) in enumerate(
            ((tok_h, tok), (qkvw_h, wqkv.at[mp]), (outw_h, wout), (inw_h, win), (downw_h, wdown), (cot_h, cot))
        )
    ]
    for copy in local[:2]:
        copy.start()

    def dp_partner(b):
        return (dp + (1 << b) * (1 - 2 * ((dp // (1 << b)) % 2)), mp)

    barrier = pltpu.get_barrier_semaphore()
    partners = [core_id] + [dp_partner(b) for b in range(n_bits)]
    for there in partners:
        pl.semaphore_signal(barrier, inc=1, device_id=there, device_id_type=MESH)
    for copy in local[2:]:
        copy.start()

    r0, r1, r2, r3 = (act_v[0:1, i : i + 1] for i in range(4))
    i0, i1, i2, i3 = (1.0 / r for r in (r0, r1, r2, r3))

    row = jnp.sum(jnp.where(lax.broadcasted_iota(jnp.int32, seg_v.shape, 0) == mp, seg_v[...], 0), axis=0, keepdims=True).astype(WIDE)
    fill = fill_s[mp]
    seg_col = jnp.broadcast_to(row, (128, tokens)).T[:, 0:1]
    blk = 128

    for i in range(tokens // blk):
        kpos = lax.broadcasted_iota(jnp.int32, (blk, tokens), 1)
        qpos = lax.broadcasted_iota(jnp.int32, (blk, tokens), 0) + i * blk
        live = (kpos < fill) | (kpos == qpos)
        same = seg_col[i * blk : i * blk + blk] == row
        bias[i * blk : i * blk + blk, :] = jnp.where(same & live, 0.0, -1e30)

    pl.semaphore_wait(barrier, len(partners))
    weight_copies = [
        pltpu.make_async_remote_copy(
            src_ref=src, dst_ref=dst, send_sem=wsend.at[i], recv_sem=wrecv.at[i], device_id=core_id, device_id_type=MESH
        )
        for i, (src, dst) in enumerate(((qkvw_h, wqkv.at[mp]), (qvb_v, qvb.at[mp])))
    ]
    for copy in weight_copies:
        copy.start()
    qvb[mp] = qvb_v[...]

    local[0].wait()
    rb = 64
    def rows_at(i, size=rb):
        return pl.ds(pl.multiple_of(i * size, size), size)

    def clip_rows(i, peak):
        v = tok[rows_at(i), :].astype(WIDE)
        clip_in[rows_at(i), :] = (r0 * jnp.tanh(v * i0)).astype(LOW)
        return jnp.maximum(peak, jnp.max(jnp.abs(v), axis=0, keepdims=True))

    peak0 = lax.fori_loop(0, tokens // rb, clip_rows, jnp.zeros((1, width), WIDE))
    stats[...] = jnp.zeros_like(stats)
    lane = lax.broadcasted_iota(jnp.int32, (1, 128), 1)
    in_head = [lane < HD, lane >= HD]
    qb = 256

    def project(part):
        for j in range(3):
            out = dot(clip_in[...], wqkv[part, j])
            if j == 0:
                out = (out + qvb[part, 0:1, :]).astype(LOW).astype(WIDE) * (HD ** -0.5)
            elif j == 2:
                out = out + qvb[part, 1:2, :]
            qkv[j, part] = out.astype(LOW)

    def attend(part):
        def pair(t, carry):
            at = pl.ds(pl.multiple_of(t * 128, 128), 128)
            k, v = qkv[1, part, :, at], qkv[2, part, :, at]
            for i in range(tokens // qb):
                rows = pl.ds(i * qb, qb)
                q = qkv[0, part, rows, at]
                total = jnp.zeros((qb, 128), WIDE)
                found = stats[rows, :]
                for h in range(2):
                    kz = jnp.where(in_head[h], k, jnp.zeros_like(k))
                    vz = jnp.where(in_head[h], v, jnp.zeros_like(v))
                    s = dot_nt(q, kz) + bias[rows, :]
                    top = jnp.max(s, axis=-1, keepdims=True)
                    e = jnp.exp(s - top)
                    norm = jnp.sum(e, axis=-1, keepdims=True)
                    total = total + dot(e.astype(LOW), vz) * (1.0 / norm)
                    found = jnp.where(lane == (part * 6 + t * 2 + h), top + jnp.log(norm), found)
                stats[rows, :] = found
                ctx[rows, pl.ds(pl.multiple_of(part * half + t * 128, 128), 128)] = total
            return carry

        lax.fori_loop(0, half // 128, pair, 0)

    local[1].wait()
    project(mp)
    attend(mp)
    for copy in weight_copies:
        copy.wait()
    project(other)
    attend(other)

    local[2].wait()

    def mix_rows(i, peak):
        c = ctx[rows_at(i), :]
        clip_mid[rows_at(i), :] = (r1 * jnp.tanh(c * i1)).astype(LOW)
        return jnp.maximum(peak, jnp.max(jnp.abs(c), axis=0, keepdims=True))

    peak1 = lax.fori_loop(0, tokens // rb, mix_rows, jnp.zeros((1, width), WIDE))
    interleave(mixed_t, lambda part: clip_mid[:, half * part : half * part + half].astype(WIDE))
    h2[...] = dot(clip_mid[...], wout[...])

    def norm(v):
        center = v - jnp.mean(v, axis=-1, keepdims=True)
        inv = lax.rsqrt(jnp.mean(center * center, axis=-1, keepdims=True) + EPSILON)
        return center * inv, inv

    def norm1_rows(i, peak):
        rows = rows_at(i)
        xhat, inv = norm(tok[rows, :].astype(WIDE) + (h2[rows, :] + outb_v[...]))
        xhat1[rows, :] = xhat
        stats[rows, :] = jnp.where(lane == 127, inv, stats[rows, :])
        normed = xhat * g1_v[...] + b1_v[...]
        h2[rows, :] = normed + downb_v[...]
        clip_mid[rows, :] = (r2 * jnp.tanh(normed * i2)).astype(LOW)
        return jnp.maximum(peak, jnp.max(jnp.abs(normed), axis=0, keepdims=True))

    peak2 = lax.fori_loop(0, tokens // rb, norm1_rows, jnp.zeros((1, width), WIDE))
    interleave(clip_mid_t, lambda part: clip_mid[:, half * part : half * part + half].astype(WIDE))

    local[3].wait()
    local[4].wait()
    fb = 256

    def feed(b, peak):
        cols = pl.ds(pl.multiple_of(b * fb, fb), fb)
        pre = dot(clip_mid[...], win[:, cols]) + inb_v[:, cols]
        u = jnp.abs(pre)
        bell = jnp.exp(pre * pre * -0.5)
        t = 1.0 / (1.0 + (0.3275911 * SQRT_HALF) * u)
        poly = ((((1.061405429 * t - 1.453152027) * t + 1.421413741) * t - 0.284496736) * t + 0.254829592) * t
        tail = 0.5 * poly * bell
        phi_cdf = jnp.where(pre < 0, tail, 1.0 - tail)
        act = pre * phi_cdf
        th = jnp.tanh(act * i3)
        out = (r3 * th).astype(LOW)
        slope_f[:, cols] = ((1.0 - th * th) * (phi_cdf + pre * bell * INV_SQRT_2PI)).astype(LOW)
        flipped = out.T
        for i in range(fb // 32):
            group = b * (fb // 32) + i
            owner = group // 3
            clip_act_t[owner % 2, group % 3, owner // 2] = flipped[32 * i : 32 * i + 32]
        h2[...] += dot(out, wdown[pl.ds(pl.multiple_of(b * fb, fb), fb), :])
        return jnp.maximum(peak, jnp.max(jnp.abs(act), axis=0, keepdims=True))

    peak3 = lax.fori_loop(0, hidden // fb, feed, jnp.zeros((1, fb), WIDE))

    local[5].wait()
    zero_row = jnp.zeros((1, width), WIDE)

    def norm2_rows(i, sums):
        rows = rows_at(i)
        xhat, inv = norm(h2[rows, :])
        e = cot[rows, :].astype(WIDE)
        clip_in_row = (xhat * g2_v[...] + b2_v[...]).astype(LOW)
        clip_mid[rows, :] = clip_in_row
        w = e * g2_v[...]
        d = inv * (w - jnp.mean(w, axis=-1, keepdims=True) - xhat * jnp.mean(w * xhat, axis=-1, keepdims=True))
        h2[rows, :] = d
        low = d.astype(LOW)
        cot[rows, :] = low
        return (
            sums[0] + jnp.sum(e * xhat, axis=0, keepdims=True),
            sums[1] + jnp.sum(e, axis=0, keepdims=True),
            sums[2] + jnp.sum(low.astype(WIDE), axis=0, keepdims=True),
        )

    gain2, shift2, down_bias = lax.fori_loop(0, tokens // rb, norm2_rows, (zero_row, zero_row, zero_row))
    lay_copy = pltpu.make_async_copy(clip_mid, lay_h, loc_sem.at[6])
    lay_copy.start()

    sm[...] = jnp.zeros_like(sm)
    sm[7:8, :] = down_bias
    sm[8:9, :] = gain2
    sm[9:10, :] = shift2
    lane_w = lax.broadcasted_iota(jnp.int32, (1, width), 1)
    peaks = zero_row
    for i, peak in enumerate((peak0, peak1, peak2, peak3)):
        peaks = jnp.where(lane_w == i, jnp.max(peak, axis=-1, keepdims=True), peaks)
    sm[12:13, :] = peaks

    scatter = Scatter(
        n_low,
        {"down": acc_d, "wide": acc_w},
        {"down": cs_d, "wide": cs_w},
        {"down": cr_d, "wide": cr_w},
        {"down": (rd1, rd2, rd3, rd4), "wide": (rw1, rw2, rw3, rw4)},
        msend,
        mrecv,
    )

    def out_down(index):
        def write(total):
            gdown[32 * index : 32 * index + 32, :] = total
        return write

    def out_wide(ref, at):
        def write(total):
            both = jnp.concatenate([total[:24], total[24:]], axis=1)
            if ref is gqkv:
                ref[at] = both
            else:
                ref[:, width * at : width * at + width] = both
        return write

    outs = [out_down(i) for i in range(3)] + [out_wide(gin, i) for i in range(4)] + [out_wide(gout, 0)] + [out_wide(gqkv, i) for i in range(3)]

    def step(m, stage):
        scatter.step(m, stage, outs[m])

    def drain():
        for stage in (0, 1, 2, 3, 4):
            for m in range(N_MSG):
                if scatter.next.get(m) == stage:
                    step(m, stage)
        scatter.finish()

    if upto >= 1:
        for i in range(3):
            m = DOWN0 + i
            order = MESSAGES[m][2]
            scatter.slot_free(m)
            store_down(cs_d, (i % 2,), dot(clip_act_t[other, i].reshape(16 * 32, tokens), cot[...]), order)
            scatter.send_core(m)
            store_down(acc_d, (i,), dot(clip_act_t[mp, i].reshape(16 * 32, tokens), cot[...]), order)
            step(m, 0)

    d_in_bias = []
    if upto >= 2:
        for i in range(4):
            m = IN0 + i
            order = MESSAGES[m][2]
            cols = slice(width * i, width * i + width)
            d_pre = (dot_nt(cot[...], wdown[cols, :]) * slope_f[:, cols].astype(WIDE)).astype(LOW)
            sm[3 + i : 4 + i, :] = jnp.sum(d_pre.astype(WIDE), axis=0, keepdims=True)
            scatter.slot_free(m)
            store_wide(cs_w, (i % 2,), dot(clip_mid_t[other], d_pre), order)
            scatter.send_core(m)
            store_wide(acc_w, (i,), dot(clip_mid_t[mp], d_pre), order)
            back = dot_nt(d_pre, win[:, cols])
            if i == 0:
                d_h1[...] = back
            else:
                d_h1[...] += back
            step(m, 0)

    if upto >= 3:
        lay_copy.wait()
        step(DOWN0, 1)

        def norm1_back(i, sums):
            rows = rows_at(i)
            xhat = xhat1[rows, :]
            inv = stats[rows, 127:128]
            th = jnp.tanh((xhat * g1_v[...] + b1_v[...]) * i2)
            e = h2[rows, :] + d_h1[rows, :] * (1.0 - th * th)
            w = e * g1_v[...]
            d = inv * (w - jnp.mean(w, axis=-1, keepdims=True) - xhat * jnp.mean(w * xhat, axis=-1, keepdims=True))
            d_h1[rows, :] = d
            low = d.astype(LOW)
            cot[rows, :] = low
            return (
                sums[0] + jnp.sum(e * xhat, axis=0, keepdims=True),
                sums[1] + jnp.sum(e, axis=0, keepdims=True),
                sums[2] + jnp.sum(low.astype(WIDE), axis=0, keepdims=True),
            )

        gain1, shift1, out_bias = lax.fori_loop(0, tokens // rb, norm1_back, (zero_row, zero_row, zero_row))
        sm[0:1, :] = out_bias
        sm[1:2, :] = gain1
        sm[2:3, :] = shift1
        order = MESSAGES[OUT0][2]
        scatter.slot_free(OUT0)
        store_wide(cs_w, (0,), dot(mixed_t[other], cot[...]), order)
        scatter.send_core(OUT0)
        store_wide(acc_w, (4,), dot(mixed_t[mp], cot[...]), order)
        h2[...] = dot_nt(cot[...], wout[...])

        def context_rows(i, carry):
            rows = rows_at(i)
            th = jnp.tanh(ctx[rows, :] * i1)
            clip_mid[rows, :] = (h2[rows, :].astype(LOW).astype(WIDE) * (1.0 - th * th)).astype(LOW)
            return carry

        lax.fori_loop(0, tokens // rb, context_rows, 0)
        step(OUT0, 0)

    def attend_back(part):
        def pair(t, carry):
            at = pl.ds(pl.multiple_of(t * 128, 128), 128)
            wide_at = pl.ds(pl.multiple_of(part * half + t * 128, 128), 128)
            k, v = qkv[1, part, :, at], qkv[2, part, :, at]
            d_k, d_v = jnp.zeros((tokens, 128), WIDE), jnp.zeros((tokens, 128), WIDE)
            for i in range(tokens // qb):
                rows = pl.ds(i * qb, qb)
                q = qkv[0, part, rows, at]
                dc = clip_mid[rows, wide_at]
                prod = dc.astype(WIDE) * ctx[rows, wide_at]
                found = stats[rows, :]
                d_q = jnp.zeros((qb, 128), WIDE)
                for h in range(2):
                    kz = jnp.where(in_head[h], k, jnp.zeros_like(k))
                    vz = jnp.where(in_head[h], v, jnp.zeros_like(v))
                    qz = jnp.where(in_head[h], q, jnp.zeros_like(q))
                    dcz = jnp.where(in_head[h], dc, jnp.zeros_like(dc))
                    mean = jnp.sum(jnp.where(in_head[h], prod, 0.0), axis=-1, keepdims=True)
                    total = jnp.sum(jnp.where(lane == (part * 6 + t * 2 + h), found, 0.0), axis=-1, keepdims=True)
                    p = jnp.exp(dot_nt(q, kz) + bias[rows, :] - total)
                    d_s = (p * (dot_nt(dc, vz) - mean)).astype(LOW)
                    d_q = d_q + dot(d_s, kz)
                    d_k = d_k + dot_tn(d_s, qz)
                    d_v = d_v + dot_tn(p.astype(LOW), dcz)
                qkv[0, part, rows, at] = (d_q * (HD ** -0.5)).astype(LOW)
            qkv[1, part, :, at] = d_k.astype(LOW)
            qkv[2, part, :, at] = d_v.astype(LOW)
            return carry

        lax.fori_loop(0, half // 128, pair, 0)

    if upto >= 4:
        step(DOWN0 + 1, 1)
        step(DOWN0 + 2, 1)
        attend_back(other)
        for i in range(2):
            m = QKV0 + i
            scatter.slot_free(m)
            store_wide(cs_w, ((5 + i) % 2,), dot_tn(qkv[i, other], clip_in[...]), MESSAGES[m][2])
            scatter.send_core(m)
        step(IN0, 1)
        step(IN0 + 1, 1)
        attend_back(mp)
        for i in range(2):
            m = QKV0 + i
            store_wide(acc_w, (5 + i,), dot_tn(qkv[i, mp], clip_in[...]), MESSAGES[m][2])
            step(m, 0)
        m = QKV0 + 2
        scatter.slot_free(m)
        store_wide(cs_w, (7 % 2,), dot_tn(qkv[2, other], clip_in[...]), MESSAGES[m][2])
        scatter.send_core(m)
        store_wide(acc_w, (7,), dot_tn(qkv[2, mp], clip_in[...]), MESSAGES[m][2])
        step(m, 0)
        for r, j in ((10, 0), (11, 2)):
            for part in range(2):
                sm[r : r + 1, half * part : half * part + half] = jnp.sum(qkv[j, part].astype(WIDE), axis=0, keepdims=True)

    if upto >= 5:
        for n, (part, j) in enumerate([(part, j) for part in range(2) for j in range(3)]):
            back = dot_nt(qkv[j, part], wqkv[part, j])
            if n == 0:
                h2[...] = back
            else:
                h2[...] += back

        def token_rows(i, carry):
            rows = rows_at(i)
            th = jnp.tanh(tok[rows, :].astype(WIDE) * i0)
            d_h1[rows, :] += h2[rows, :] * (1.0 - th * th)
            return carry

        lax.fori_loop(0, tokens // rb, token_rows, 0)
        tok_copy = pltpu.make_async_copy(d_h1, gtok_h, loc_sem.at[7])
        tok_copy.start()

        is_peak = lax.broadcasted_iota(jnp.int32, sm.shape, 0) == 12

        def small_copy(k):
            return pltpu.make_async_remote_copy(
                src_ref=sm,
                dst_ref=sm_r.at[k],
                send_sem=ssend.at[k],
                recv_sem=srecv.at[k],
                device_id=partners[k],
                device_id_type=MESH,
            )

        def small_end(k):
            small_copy(k).wait()
            sm[...] = jnp.where(is_peak, jnp.maximum(sm[...], sm_r[k]), sm[...] + sm_r[k])
            if k + 1 < len(partners):
                small_copy(k + 1).start()

        small_copy(0).start()
        for k in range(len(partners)):
            small_end(k)
        drain()

        per = width // (2 * n_dp)
        me = dp * 2 + mp
        sums = sm[...]
        out = pltpu.roll(sums, (width - per * me) % width, 1)[:, :128]
        qv_out = pltpu.roll(sums, (width - (mp * half + per * dp)) % width, 1)[:, :128]
        wide_at = 4 * per * me
        in_rows = pltpu.roll(sums, (width - wide_at % width) % width, 1)[:, :128]
        r_iota = lax.broadcasted_iota(jnp.int32, out.shape, 0)
        in_row = jnp.sum(jnp.where(r_iota == 3 + wide_at // width, in_rows, 0.0), axis=0, keepdims=True)
        out = jnp.where((r_iota == 10) | (r_iota == 11), qv_out, out)
        out = jnp.where(r_iota == 3, in_row, out)
        small_o[...] = out
        small_o[12:13, 0:4] = MOMENTUM * act_v[...] + (1.0 - MOMENTUM) * sums[12:13, 0:4]
        tok_copy.wait()
    else:
        lay_copy.wait() if upto < 3 else None
        drain()


def per_device(n_dp, upto, tokens, seg_ids, fill_len, qkv_weight, qv_bias, out_weight, out_bias, norm1_gain, norm1_bias, in_weight, in_bias,
               down_weight, down_bias, norm2_gain, norm2_bias, act_range, cotangent):
    n_tok, width = tokens.shape
    hidden = in_weight.shape[1]
    half = width // 2
    n_low = max(1, n_dp // 16)
    any_, vmem = pl.BlockSpec(memory_space=pl.ANY), pl.BlockSpec(memory_space=pltpu.VMEM)
    smem = pl.BlockSpec(memory_space=pltpu.SMEM)
    chunk = width // 32
    shape = jax.ShapeDtypeStruct
    low = lambda *s: pltpu.VMEM(s, LOW)
    wide = lambda *s: pltpu.VMEM(s, WIDE)
    dma = lambda *s: pltpu.SemaphoreType.DMA(s)
    n_partners = n_dp.bit_length()
    n_wide = N_MSG - 3
    outs = pl.pallas_call(
        functools.partial(kernel, n_dp, n_low, upto),
        out_shape=(
            shape((n_tok, width), LOW),
            shape((n_tok, width), WIDE),
            shape((3, chunk, width), WIDE),
            shape((chunk, width), WIDE),
            shape((chunk, hidden), WIDE),
            shape((4 * chunk, width), WIDE),
            shape((16, 128), WIDE),
        ),
        in_specs=[any_, vmem, smem, any_, vmem, any_, vmem, vmem, vmem, any_, vmem, any_, vmem, vmem, vmem, vmem, any_],
        out_specs=(any_, any_, vmem, vmem, vmem, vmem, vmem),
        scratch_shapes=[
            low(n_tok, width), low(n_tok, width), low(2, 3, width, half), wide(2, 2, half), low(width, width), low(width, hidden), low(hidden, width),
            low(n_tok, width), low(3, 2, n_tok, half), wide(n_tok, n_tok), wide(n_tok, width), wide(n_tok, 128), low(2, half, n_tok),
            wide(n_tok, width), low(n_tok, width), low(2, half, n_tok), low(2, 3, 16, 32, n_tok), low(n_tok, hidden),
            wide(n_tok, width), wide(n_tok, width), wide(16, width), wide(n_partners, 16, width),
            low(3, 16, 32, width), low(n_wide, 16, 48, half), low(2, 16, 32, width), low(2, 16, 48, half), low(3, 16, 32, width), low(n_wide, 16, 48, half),
            *(low(3, 16 >> k, 32, width) for k in range(1, 5)), *(low(n_wide, 16 >> k, 48, half) for k in range(1, 5)),
            dma(8), dma(2), dma(2), dma(N_MSG, 5), dma(N_MSG, 5), dma(n_partners), dma(n_partners),
        ],
        compiler_params=pltpu.CompilerParams(collective_id=0, has_side_effects=True, vmem_limit_bytes=64 * 2**20 - 2**16),
        cost_estimate=pl.CostEstimate(flops=25_000_000_000, bytes_accessed=24_000_000, transcendentals=12_000_000),
    )(
        tokens, seg_ids, fill_len, jnp.transpose(qkv_weight, (1, 0, 2)), qv_bias, out_weight, out_bias.reshape(1, width), norm1_gain.reshape(1, width),
        norm1_bias.reshape(1, width), in_weight, in_bias.reshape(1, hidden), down_weight, down_bias.reshape(1, width), norm2_gain.reshape(1, width),
        norm2_bias.reshape(1, width), act_range.reshape(1, 4), cotangent,
    )
    layer_out, grad_tokens, qkv_sum, sum_out, sum_in, sum_down, small = outs
    if n_low > 1:
        groups = [[top * n_low + low_ for low_ in range(n_low)] for top in range(16)]
        moves = [((top * n_low + i) * 2 + core, n_low * (2 * top + core) + i) for top in range(16) for i in range(n_low) for core in range(2)]

        def spread(v, dim):
            return lax.psum_scatter(v, "dp", scatter_dimension=dim, axis_index_groups=groups, tiled=True)

        qkv_sum = spread(qkv_sum, 1)
        sum_out, sum_in, sum_down = (lax.ppermute(spread(v, 0), ("dp", "mp"), moves) for v in (sum_out, sum_in, sum_down))
    per = width // (2 * n_dp)
    row = lambda i: small[i, :per]
    return (
        layer_out,
        grad_tokens,
        jnp.transpose(qkv_sum, (2, 0, 1)),
        small[10:12, :per],
        sum_out,
        row(0),
        row(1),
        row(2),
        sum_in,
        small[3, : 4 * per],
        sum_down,
        row(7),
        row(8),
        row(9),
        small[12, :4],
    )


def solution(mesh, upto=5):
    n_dp = mesh.shape["dp"]
    both, copies = P(("dp", "mp")), P()
    rows = P(("dp", "mp"), None)
    return jax.shard_map(
        functools.partial(per_device, n_dp, upto),
        mesh=mesh,
        in_specs=(
            rows, P("dp", None), P("dp"), P(None, None, "mp"), P(None, "mp"),
            *([copies] * 11), rows,
        ),
        out_specs=(
            rows, rows, P(None, None, ("mp", "dp")), P(None, ("mp", "dp")), rows, both, both, both, rows, both, rows, both, both, both, copies,
        ),
        check_vma=False,
    )
```

```python
import functools
import math

import jax
import jax.numpy as jnp
from jax import lax
from jax.experimental import pallas as pl
from jax.experimental.pallas import tpu as pltpu
from jax.sharding import PartitionSpec as P

HD = 64
EPSILON = 1e-06
MOMENTUM = 0.9
SQRT_HALF = math.sqrt(0.5)
INV_SQRT_2PI = 1.0 / math.sqrt(2.0 * math.pi)
LOW = jnp.bfloat16
WIDE = jnp.float32
MESH = pl.DeviceIdType.MESH

MESSAGES = (
    ("down", 0, (0, 1, 2, 3)),
    ("down", 1, (2, 3, 0, 1)),
    ("down", 2, (1, 2, 0, 3)),
    ("wide", 0, (0, 2, 3, 1)),
    ("wide", 1, (1, 0, 2, 3)),
    ("wide", 2, (1, 0, 2, 3)),
    ("wide", 3, (1, 0, 2, 3)),
    ("wide", 4, (0, 2, 1, 3)),
    ("wide", 5, (1, 0, 2, 3)),
    ("wide", 6, (0, 1, 2, 3)),
    ("wide", 7, (2, 1, 0, 3)),
)
N_MSG = len(MESSAGES)
DOWN0, IN0, OUT0, QKV0 = 0, 3, 7, 8


SCHEDULE = (
    ("Dp", 0), ("Do", 0), ("Dp", 1), ("Do", 1), ("Dp", 2), (0, 0), ("Do", 2), ("Ip", 0), (1, 0), (2, 0), ("Io", 0), ("In", 0), (3, 0),
    ("Ip", 1), ("Io", 1), ("In", 1), ("Ip", 2), (4, 0), ("Io", 2), ("In", 2), (0, 1), (5, 0), ("Ip", 3), (1, 1), ("Io", 3), (2, 1),
    ("In", 3), (6, 0), ("LN", 0), ("Op", 0), ("Oo", 0), (3, 1), ("dm", 0), ("cx", 0), (7, 0), ("ab", 0), (4, 1), ("ab", 1), (2, 2),
    (1, 2), ("ab", 2), (0, 2), ("Qp", 0), (3, 2), ("Qp", 1), (7, 1), ("Qp", 2), ("am", 0), (0, 3), ("am", 1), (4, 2), (5, 1), ("am", 2),
    (2, 3), (3, 3), (7, 2), (1, 3), ("Qo", 0), (8, 0), ("Qo", 1), (9, 0), ("Qo", 2), (10, 0), (0, 4), (4, 3), (6, 1), ("dc", 0), (5, 2),
    (3, 4), ("sm", 0), (7, 3), (2, 4), (1, 4), ("tk", 0), (9, 1), (10, 1), (4, 4), (8, 1), (5, 3), (6, 2), ("sm", 1), (7, 4), (9, 2),
    (5, 4), (6, 3), (8, 2), (9, 3), (10, 2), ("sm", 2), (6, 4), (8, 3), (10, 3), ("sm", 3), (9, 4), (8, 4), (10, 4), ("sm", 4),
)


def dot(a, b):
    return lax.dot_general(a, b, (((1,), (0,)), ((), ())), preferred_element_type=WIDE)


def dot_nt(a, b):
    return lax.dot_general(a, b, (((1,), (1,)), ((), ())), preferred_element_type=WIDE)


def dot_tn(a, b):
    return lax.dot_general(a, b, (((0,), (0,)), ((), ())), preferred_element_type=WIDE)


def place(chunk, order):
    spot = 0
    for bit in order:
        spot = spot * 2 + (chunk >> bit) % 2
    return spot


class Scatter:
    def __init__(self, n_low, acc, csend, crecv, recvs, send_sem, recv_sem):
        self.acc, self.csend, self.crecv, self.recvs = acc, csend, crecv, recvs
        self.send_sem, self.recv_sem = send_sem, recv_sem
        self.dp, self.mp = lax.axis_index("dp"), lax.axis_index("mp")
        self.n_low = n_low
        self.slot_user = {}
        self.pending = []
        self.next = {}

    def bit(self, bit):
        return (self.dp // (self.n_low << bit)) % 2

    def partner(self, bit):
        return (self.dp + (self.n_low << bit) * (1 - 2 * self.bit(bit)), self.mp)

    def slot(self, m):
        group, index, _ = MESSAGES[m]
        return self.csend[group].at[index % 2]

    def core_copy(self, m):
        group, index, _ = MESSAGES[m]
        return pltpu.make_async_remote_copy(
            src_ref=self.slot(m),
            dst_ref=self.crecv[group].at[index],
            send_sem=self.send_sem.at[m, 0],
            recv_sem=self.recv_sem.at[m, 0],
            device_id=(self.dp, 1 - self.mp),
            device_id_type=MESH,
        )

    def base(self, m, stage):
        order = MESSAGES[m][2]
        spot = 0
        for k in range(stage):
            spot = spot + self.bit(order[k]) * (8 >> k)
        return spot

    def copy(self, m, stage):
        group, index, order = MESSAGES[m]
        count = 16 >> stage
        bit = order[stage - 1]
        start = self.base(m, stage - 1) + (1 - self.bit(bit)) * count
        return pltpu.make_async_remote_copy(
            src_ref=self.acc[group].at[index, pl.ds(start, count)],
            dst_ref=self.recvs[group][stage - 1].at[index],
            send_sem=self.send_sem.at[m, stage],
            recv_sem=self.recv_sem.at[m, stage],
            device_id=self.partner(bit),
            device_id_type=MESH,
        )

    def slot_free(self, m):
        group, index, _ = MESSAGES[m]
        old = self.slot_user.get((group, index % 2))
        if old is not None:
            self.core_copy(old).wait_send()
            self.pending.remove((old, 0))
        self.slot_user[(group, index % 2)] = m

    def send_core(self, m):
        self.core_copy(m).start()
        self.pending.append((m, 0))
        self.next[m] = 0

    def add(self, m, received, from_, start, count):
        group, index, _ = MESSAGES[m]
        acc = self.acc[group]
        here = pl.ds(start, count)
        acc[index, here] = acc[index, here] + received[index, pl.ds(from_, count)]

    def step(self, m, stage, out=None):
        group, index, order = MESSAGES[m]
        assert self.next[m] == stage
        self.next[m] = stage + 1
        (self.core_copy(m) if stage == 0 else self.copy(m, stage)).wait_recv()
        if stage == 4:
            total = self.acc[group][index, self.base(m, 4)].astype(WIDE) + self.recvs[group][3][index, 0].astype(WIDE)
            out(total)
            return
        received = self.crecv[group] if stage == 0 else self.recvs[group][stage - 1]
        count = 8 >> stage
        base = self.base(m, stage)
        mine = self.bit(order[stage])
        self.add(m, received, (1 - mine) * count, base + (1 - mine) * count, count)
        self.copy(m, stage + 1).start()
        self.pending.append((m, stage + 1))
        self.add(m, received, mine * count, base + mine * count, count)

    def finish(self):
        for m, stage in self.pending:
            (self.core_copy(m) if stage == 0 else self.copy(m, stage)).wait_send()


def store_down(ref, first, result, order):
    for chunk in range(16):
        ref[(*first, place(chunk, order))] = result[32 * chunk : 32 * chunk + 32].astype(LOW)


def store_wide(ref, first, result, order):
    half = result.shape[1] // 2
    for chunk in range(16):
        rows = result[24 * chunk : 24 * chunk + 24]
        ref[(*first, place(chunk, order))] = jnp.concatenate([rows[:, :half], rows[:, half:]], axis=0).astype(LOW)


def interleave(ref, values):
    for part in range(2):
        flipped = values(part).T
        for core in range(2):
            groups = [flipped[24 * i : 24 * i + 24] for i in range(core, 16, 2)]
            ref[core, 192 * part : 192 * part + 192, :] = jnp.concatenate(groups, axis=0).astype(LOW)


def kernel(
    n_dp, n_low,
    tok_h, seg_v, fill_s, qkvw_h, qvb_v, outw_h, outb_v, g1_v, b1_v, inw_h, inb_v, downw_h, downb_v, g2_v, b2_v, act_v, cot_h,
    lay_h, gtok_h, gqkv, gout, gin, gdown, small_o,
    tok, cot, wqkv, qvb, wout, win, wdown, clip_in, qkv, bias, ctx, stats, mixed_t, xhat1, clip_mid, clip_mid_t, clip_act_t, slope_f, h2, d_h1, pre_s, act_s, d_pre, sm, sm_r,
    acc_d, acc_w, cs_d, cs_w, cr_d, cr_w, rd1, rd2, rd3, rd4, rw1, rw2, rw3, rw4,
    loc_sem, wsend, wrecv, msend, mrecv, ssend, srecv,
):
    dp, mp = lax.axis_index("dp"), lax.axis_index("mp")
    outb_v, g1_v, b1_v, downb_v, g2_v, b2_v = (v[...].reshape(1, -1) for v in (outb_v, g1_v, b1_v, downb_v, g2_v, b2_v))
    n_bits = n_dp.bit_length() - 1
    tokens, width = tok.shape
    hidden = win.shape[1]
    half = width // 2
    other = 1 - mp
    core_id = (dp, other)

    local = [
        pltpu.make_async_copy(src, dst, loc_sem.at[i])
        for i, (src, dst) in enumerate(
            ((tok_h, tok), (qkvw_h, wqkv.at[mp]), (outw_h, wout), (inw_h, win), (downw_h, wdown), (cot_h, cot))
        )
    ]
    for copy in local[:2]:
        copy.start()
    open_ = dict(enumerate(local))
    def take(i):
        open_.pop(i).wait()

    def dp_partner(b):
        return (dp + (1 << b) * (1 - 2 * ((dp // (1 << b)) % 2)), mp)

    barrier = pltpu.get_barrier_semaphore()
    partners = [core_id] + [dp_partner(b) for b in range(n_bits)]
    for there in partners:
        pl.semaphore_signal(barrier, inc=1, device_id=there, device_id_type=MESH)

    r0, r1, r2, r3 = (act_v[0:1, i : i + 1] for i in range(4))
    i0, i1, i2, i3 = (1.0 / r for r in (r0, r1, r2, r3))

    qvb[mp] = qvb_v[...]
    take(0)
    rb = 64
    def rows_at(i, size=rb):
        return pl.ds(pl.multiple_of(i * size, size), size)

    def clip_rows(i, peak):
        v = tok[rows_at(i), :].astype(WIDE)
        clip_in[rows_at(i), :] = (r0 * jnp.tanh(v * i0)).astype(LOW)
        return jnp.maximum(peak, jnp.max(jnp.abs(v), axis=0, keepdims=True))

    peak0 = lax.fori_loop(0, tokens // rb, clip_rows, jnp.zeros((1, width), WIDE), unroll=4)
    stats[...] = jnp.zeros_like(stats)
    lane = lax.broadcasted_iota(jnp.int32, (1, 128), 1)
    in_head = [lane < HD, lane >= HD]
    qb = 256

    def project(part):
        for j in range(3):
            out = dot(clip_in[...], wqkv[part, j])
            if j == 0:
                out = (out + qvb[part, 0:1, :]).astype(LOW).astype(WIDE) * (HD ** -0.5)
            elif j == 2:
                out = out + qvb[part, 1:2, :]
            qkv[j, part] = out.astype(LOW)

    def attend(part):
        def pair(t, carry):
            at = pl.ds(pl.multiple_of(t * 128, 128), 128)
            k, v = qkv[1, part, :, at], qkv[2, part, :, at]
            nil, one = jnp.zeros_like(v), jnp.ones_like(v)
            kz = [jnp.where(m, k, nil) for m in in_head]
            vz = [jnp.concatenate([jnp.where(m, v, nil), jnp.where(m, one, nil)], axis=1) for m in in_head]
            vz = jnp.concatenate(vz, axis=0)
            head = part * 6 + t * 2
            for i in range(tokens // qb):
                rows = pl.ds(i * qb, qb)
                q = qkv[0, part, rows, at]
                es, tops = [], []
                for h in range(2):
                    s = dot_nt(q, kz[h]) + bias[rows, :]
                    tops.append(jnp.max(s, axis=-1, keepdims=True))
                    es.append(jnp.exp(s - tops[h]).astype(LOW))
                both = dot(jnp.concatenate(es, axis=1), vz)
                norm = both[:, 128:]
                ctx[rows, pl.ds(pl.multiple_of(part * half + t * 128, 128), 128)] = both[:, :128] / norm
                total = jnp.where(in_head[0], tops[0], tops[1]) + jnp.log(norm)
                found = jnp.where(lane == head, total[:, 0:1], stats[rows, :])
                stats[rows, :] = jnp.where(lane == head + 1, total[:, HD : HD + 1], found)
            return carry

        lax.fori_loop(0, half // 128, pair, 0, unroll=True)

    take(1)
    project(mp)
    pl.semaphore_wait(barrier, len(partners))
    weight_copies = [
        pltpu.make_async_remote_copy(
            src_ref=src, dst_ref=dst, send_sem=wsend.at[i], recv_sem=wrecv.at[i], device_id=core_id, device_id_type=MESH
        )
        for i, (src, dst) in enumerate(((qkvw_h, wqkv.at[mp]), (qvb_v, qvb.at[mp])))
    ]
    for copy in weight_copies:
        copy.start()
    open_["w0"], open_["w1"] = weight_copies
    for copy in local[2:]:
        copy.start()
    row = jnp.sum(jnp.where(lax.broadcasted_iota(jnp.int32, seg_v.shape, 0) == mp, seg_v[...], 0), axis=0, keepdims=True).astype(WIDE)
    fill = fill_s[mp]
    seg_col = jnp.broadcast_to(row, (128, tokens)).T[:, 0:1]
    blk = 128

    for i in range(tokens // blk):
        kpos = lax.broadcasted_iota(jnp.int32, (blk, tokens), 1)
        qpos = lax.broadcasted_iota(jnp.int32, (blk, tokens), 0) + i * blk
        live = (kpos < fill) | (kpos == qpos)
        same = seg_col[i * blk : i * blk + blk] == row
        bias[i * blk : i * blk + blk, :] = jnp.where(same & live, 0.0, -1e30)

    attend(mp)
    take("w0")
    take("w1")
    project(other)
    attend(other)

    take(2)

    def mix_rows(i, peak):
        c = ctx[rows_at(i), :]
        clip_mid[rows_at(i), :] = (r1 * jnp.tanh(c * i1)).astype(LOW)
        return jnp.maximum(peak, jnp.max(jnp.abs(c), axis=0, keepdims=True))

    peak1 = lax.fori_loop(0, tokens // rb, mix_rows, jnp.zeros((1, width), WIDE), unroll=4)
    interleave(mixed_t, lambda part: clip_mid[:, half * part : half * part + half].astype(WIDE))
    h2[...] = dot(clip_mid[...], wout[...])

    def norm(v):
        center = v - jnp.mean(v, axis=-1, keepdims=True)
        inv = lax.rsqrt(jnp.mean(center * center, axis=-1, keepdims=True) + EPSILON)
        return center * inv, inv

    def norm1_rows(i, peak):
        rows = rows_at(i)
        xhat, inv = norm(tok[rows, :].astype(WIDE) + (h2[rows, :] + outb_v))
        xhat1[rows, :] = xhat
        stats[rows, :] = jnp.where(lane == 127, inv, stats[rows, :])
        normed = xhat * g1_v + b1_v
        h2[rows, :] = normed + downb_v
        clip_mid[rows, :] = (r2 * jnp.tanh(normed * i2)).astype(LOW)
        return jnp.maximum(peak, jnp.max(jnp.abs(normed), axis=0, keepdims=True))

    peak2 = lax.fori_loop(0, tokens // rb, norm1_rows, jnp.zeros((1, width), WIDE), unroll=4)
    interleave(clip_mid_t, lambda part: clip_mid[:, half * part : half * part + half].astype(WIDE))

    take(3)
    take(4)
    fb, fr = pre_s.shape[2], 32
    n_fb = hidden // fb

    def feed_in(b):
        pre_s[b % 2] = dot(clip_mid[...], win[:, fb * b : fb * b + fb])

    def feed_act(b, peak):
        cols = slice(fb * b, fb * b + fb)
        for r in range(0, tokens, fr):
            rows = slice(r, r + fr)
            pre = pre_s[b % 2, rows, :] + inb_v[:, cols]
            cdf = 0.5 + 0.5 * lax.erf(pre * SQRT_HALF)
            act = pre * cdf
            th = jnp.tanh(act * i3)
            act_s[b % 2, rows, :] = (r3 * th).astype(LOW)
            bell = jnp.exp(pre * pre * -0.5) * INV_SQRT_2PI
            slope_f[rows, cols] = ((1.0 - th * th) * (cdf + pre * bell)).astype(LOW)
            peak = jnp.maximum(peak, jnp.max(jnp.abs(act), axis=0, keepdims=True))
        return peak

    def feed_out(b):
        out = act_s[b % 2]
        flipped = out.T
        for i in range(fb // 32):
            group = b * (fb // 32) + i
            owner = group // 3
            clip_act_t[owner % 2, group % 3, owner // 2] = flipped[32 * i : 32 * i + 32]
        h2[...] += dot(out, wdown[fb * b : fb * b + fb, :])

    peak3 = jnp.zeros((1, fb), WIDE)
    feed_in(0)
    for b in range(n_fb):
        if b + 1 < n_fb:
            feed_in(b + 1)
        peak3 = feed_act(b, peak3)
        if b > 0:
            feed_out(b - 1)
    feed_out(n_fb - 1)

    take(5)
    zero_row = jnp.zeros((1, width), WIDE)

    def norm2_rows(i, sums):
        rows = rows_at(i)
        xhat, inv = norm(h2[rows, :])
        e = cot[rows, :].astype(WIDE)
        clip_in_row = (xhat * g2_v + b2_v).astype(LOW)
        clip_mid[rows, :] = clip_in_row
        w = e * g2_v
        d = inv * (w - jnp.mean(w, axis=-1, keepdims=True) - xhat * jnp.mean(w * xhat, axis=-1, keepdims=True))
        h2[rows, :] = d
        low = d.astype(LOW)
        cot[rows, :] = low
        return (
            sums[0] + jnp.sum(e * xhat, axis=0, keepdims=True),
            sums[1] + jnp.sum(e, axis=0, keepdims=True),
            sums[2] + jnp.sum(low.astype(WIDE), axis=0, keepdims=True),
        )

    gain2, shift2, down_bias = lax.fori_loop(0, tokens // rb, norm2_rows, (zero_row, zero_row, zero_row), unroll=4)
    lay_copy = pltpu.make_async_copy(clip_mid, lay_h, loc_sem.at[6])
    lay_copy.start()

    sm[...] = jnp.zeros_like(sm)
    sm[7:8, :] = down_bias
    sm[8:9, :] = gain2
    sm[9:10, :] = shift2
    lane_w = lax.broadcasted_iota(jnp.int32, (1, width), 1)
    peaks = zero_row
    for i, peak in enumerate((peak0, peak1, peak2, peak3)):
        peaks = jnp.where(lane_w == i, jnp.max(peak, axis=-1, keepdims=True), peaks)
    sm[12:13, :] = peaks

    scatter = Scatter(
        n_low,
        {"down": acc_d, "wide": acc_w},
        {"down": cs_d, "wide": cs_w},
        {"down": cr_d, "wide": cr_w},
        {"down": (rd1, rd2, rd3, rd4), "wide": (rw1, rw2, rw3, rw4)},
        msend,
        mrecv,
    )

    def out_down(index):
        def write(total):
            gdown[32 * index : 32 * index + 32, :] = total
        return write

    def out_wide(ref, at):
        def write(total):
            both = jnp.concatenate([total[:24], total[24:]], axis=1)
            if ref is gqkv:
                ref[at] = both
            else:
                ref[:, width * at : width * at + width] = both
        return write

    outs = [out_down(i) for i in range(3)] + [out_wide(gin, i) for i in range(4)] + [out_wide(gout, 0)] + [out_wide(gqkv, i) for i in range(3)]

    def step(m, stage):
        scatter.step(m, stage, outs[m])

    def send_part(m, result):
        group, index, order = MESSAGES[m]
        scatter.slot_free(m)
        (store_down if group == "down" else store_wide)((cs_d if group == "down" else cs_w), (index % 2,), result, order)
        scatter.send_core(m)

    def own_part(m, result):
        group, index, order = MESSAGES[m]
        (store_down if group == "down" else store_wide)((acc_d if group == "down" else acc_w), (index,), result, order)

    def down_send(i):
        send_part(DOWN0 + i, dot(clip_act_t[other, i].reshape(16 * 32, tokens), cot[...]))

    def down_own(i):
        own_part(DOWN0 + i, dot(clip_act_t[mp, i].reshape(16 * 32, tokens), cot[...]))

    def in_send(i):
        if i == 0:
            lay_copy.wait()
        cols = slice(width * i, width * i + width)
        d_pre[...] = (dot_nt(cot[...], wdown[cols, :]) * slope_f[:, cols].astype(WIDE)).astype(LOW)
        send_part(IN0 + i, dot(clip_mid_t[other], d_pre[...]))

    def in_own(i):
        own_part(IN0 + i, dot(clip_mid_t[mp], d_pre[...]))
        sm[3 + i : 4 + i, :] = jnp.sum(d_pre[...].astype(WIDE), axis=0, keepdims=True)

    def in_back(i):
        back = dot_nt(d_pre[...], win[:, width * i : width * i + width])
        if i == 0:
            d_h1[...] = back
        else:
            d_h1[...] += back

    def norm1_back(_):
        def some(i, sums):
            rows = rows_at(i)
            xhat = xhat1[rows, :]
            inv = stats[rows, 127:128]
            th = jnp.tanh((xhat * g1_v + b1_v) * i2)
            e = h2[rows, :] + d_h1[rows, :] * (1.0 - th * th)
            w = e * g1_v
            d = inv * (w - jnp.mean(w, axis=-1, keepdims=True) - xhat * jnp.mean(w * xhat, axis=-1, keepdims=True))
            d_h1[rows, :] = d
            low = d.astype(LOW)
            cot[rows, :] = low
            return (
                sums[0] + jnp.sum(e * xhat, axis=0, keepdims=True),
                sums[1] + jnp.sum(e, axis=0, keepdims=True),
                sums[2] + jnp.sum(low.astype(WIDE), axis=0, keepdims=True),
            )

        gain1, shift1, out_bias = lax.fori_loop(0, tokens // rb, some, (zero_row, zero_row, zero_row), unroll=4)
        sm[0:1, :] = out_bias
        sm[1:2, :] = gain1
        sm[2:3, :] = shift1

    def out_send(_):
        send_part(OUT0, dot(mixed_t[other], cot[...]))

    def out_own(_):
        own_part(OUT0, dot(mixed_t[mp], cot[...]))

    def mixed_back(_):
        h2[...] = dot_nt(cot[...], wout[...])

    def context_back(_):
        def some(i, carry):
            rows = rows_at(i)
            th = jnp.tanh(ctx[rows, :] * i1)
            clip_mid[rows, :] = (h2[rows, :].astype(LOW).astype(WIDE) * (1.0 - th * th)).astype(LOW)
            return carry

        lax.fori_loop(0, tokens // rb, some, 0, unroll=4)

    def attend_back(part, t):
        at = slice(t * 128, t * 128 + 128)
        wide_at = pl.ds(pl.multiple_of(part * half + t * 128, 128), 128)
        k, v = qkv[1, part, :, at], qkv[2, part, :, at]
        split = lambda v: [jnp.where(m, v, jnp.zeros_like(v)) for m in in_head]
        kz, vz = split(k), split(v)
        d_k, d_v = jnp.zeros((tokens, 128), WIDE), jnp.zeros((tokens, 128), WIDE)
        for i in range(tokens // qb):
            rows = pl.ds(i * qb, qb)
            q = qkv[0, part, rows, at]
            dc = clip_mid[rows, wide_at]
            prod = dc.astype(WIDE) * ctx[rows, wide_at]
            found = stats[rows, :]
            ps, ds = [], []
            for h in range(2):
                mean = jnp.sum(jnp.where(in_head[h], prod, 0.0), axis=-1, keepdims=True)
                total = jnp.sum(jnp.where(lane == (part * 6 + t * 2 + h), found, 0.0), axis=-1, keepdims=True)
                p = jnp.exp(dot_nt(q, kz[h]) + bias[rows, :] - total)
                ds.append((p * (dot_nt(dc, vz[h]) - mean)).astype(LOW))
                ps.append(p.astype(LOW))
            d_q = dot(jnp.concatenate(ds, axis=1), jnp.concatenate(kz, axis=0))
            d_k = d_k + dot_tn(jnp.concatenate(ds, axis=0), jnp.concatenate(split(q), axis=0))
            d_v = d_v + dot_tn(jnp.concatenate(ps, axis=0), jnp.concatenate(split(dc), axis=0))
            qkv[0, part, rows, at] = (d_q * (HD ** -0.5)).astype(LOW)
        qkv[1, part, :, at] = d_k.astype(LOW)
        qkv[2, part, :, at] = d_v.astype(LOW)

    def qkv_send(j):
        send_part(QKV0 + j, dot_tn(qkv[j, other], clip_in[...]))

    def qkv_own(j):
        own_part(QKV0 + j, dot_tn(qkv[j, mp], clip_in[...]))

    def in_tokens(_):
        for r, j in ((10, 0), (11, 2)):
            for part in range(2):
                sm[r : r + 1, half * part : half * part + half] = jnp.sum(qkv[j, part].astype(WIDE), axis=0, keepdims=True)
        small_copy(0).start()
        for n, (part, j) in enumerate([(part, j) for part in range(2) for j in range(3)]):
            back = dot_nt(qkv[j, part], wqkv[part, j])
            if n == 0:
                h2[...] = back
            else:
                h2[...] += back

    def token_grad(_):
        def some(i, carry):
            rows = rows_at(i)
            th = jnp.tanh(tok[rows, :].astype(WIDE) * i0)
            d_h1[rows, :] += h2[rows, :] * (1.0 - th * th)
            return carry

        lax.fori_loop(0, tokens // rb, some, 0, unroll=4)
        tok_copy.start()

    tok_copy = pltpu.make_async_copy(d_h1, gtok_h, loc_sem.at[7])
    is_peak = lax.broadcasted_iota(jnp.int32, sm.shape, 0) == 12

    def small_copy(k):
        return pltpu.make_async_remote_copy(
            src_ref=sm,
            dst_ref=sm_r.at[k],
            send_sem=ssend.at[k],
            recv_sem=srecv.at[k],
            device_id=partners[k],
            device_id_type=MESH,
        )

    def small_end(k):
        small_copy(k).wait()
        sm[...] = jnp.where(is_peak, jnp.maximum(sm[...], sm_r[k]), sm[...] + sm_r[k])
        if k + 1 < len(partners):
            small_copy(k + 1).start()

    parts = {
        "Dp": down_send, "Do": down_own, "Ip": in_send, "Io": in_own, "In": in_back, "LN": norm1_back, "Op": out_send, "Oo": out_own,
        "dm": mixed_back, "cx": context_back, "ab": lambda t: attend_back(other, t), "am": lambda t: attend_back(mp, t),
        "Qp": qkv_send, "Qo": qkv_own, "dc": in_tokens, "tk": token_grad, "sm": small_end,
    }
    for name, n in SCHEDULE:
        if isinstance(name, str):
            parts[name](n)
        else:
            step(name, n)
    for k in range(5, len(partners)):
        small_end(k)
    scatter.finish()

    per = width // (2 * n_dp)
    me = dp * 2 + mp
    sums = sm[...]
    out = pltpu.roll(sums, (width - per * me) % width, 1)[:, :128]
    qv_out = pltpu.roll(sums, (width - (mp * half + per * dp)) % width, 1)[:, :128]
    wide_at = 4 * per * me
    in_rows = pltpu.roll(sums, (width - wide_at % width) % width, 1)[:, :128]
    r_iota = lax.broadcasted_iota(jnp.int32, out.shape, 0)
    in_row = jnp.sum(jnp.where(r_iota == 3 + wide_at // width, in_rows, 0.0), axis=0, keepdims=True)
    out = jnp.where((r_iota == 10) | (r_iota == 11), qv_out, out)
    out = jnp.where(r_iota == 3, in_row, out)
    small_o[...] = out
    small_o[12:13, 0:4] = MOMENTUM * act_v[...] + (1.0 - MOMENTUM) * sums[12:13, 0:4]
    tok_copy.wait()


def hand_out(per, *refs):
    big, small, outs, held, sem = refs[:6], refs[6], refs[7:22], refs[22:28], refs[28]
    ins = [pltpu.make_async_copy(src, mid, sem.at[0, i]) for i, (src, mid) in enumerate(zip(big, held))]
    away = [pltpu.make_async_copy(mid, dst, sem.at[1, i]) for i, (mid, dst) in enumerate(zip(held, outs))]
    for copy in ins:
        copy.start()
    outs[6][...] = small[10:12, :per]
    for ref, row in zip(outs[7:], (0, 1, 2, 3, 7, 8, 9, 12)):
        ref[...] = small[row, : ref.shape[0]]
    for here, there in zip(ins, away):
        here.wait()
        there.start()
    for copy in away:
        copy.wait()


def per_device(n_dp, tokens, seg_ids, fill_len, qkv_weight, qv_bias, out_weight, out_bias, norm1_gain, norm1_bias, in_weight, in_bias,
               down_weight, down_bias, norm2_gain, norm2_bias, act_range, cotangent):
    n_tok, width = tokens.shape
    hidden = in_weight.shape[1]
    half = width // 2
    n_low = max(1, n_dp // 16)
    any_, vmem = pl.BlockSpec(memory_space=pl.ANY), pl.BlockSpec(memory_space=pltpu.VMEM)
    smem = pl.BlockSpec(memory_space=pltpu.SMEM)
    chunk = width // 32
    shape = jax.ShapeDtypeStruct
    low = lambda *s: pltpu.VMEM(s, LOW)
    wide = lambda *s: pltpu.VMEM(s, WIDE)
    dma = lambda *s: pltpu.SemaphoreType.DMA(s)
    n_partners = n_dp.bit_length()
    n_wide = N_MSG - 3
    outs = pl.pallas_call(
        functools.partial(kernel, n_dp, n_low),
        out_shape=(
            shape((n_tok, width), LOW),
            shape((n_tok, width), WIDE),
            shape((3, chunk, width), WIDE),
            shape((chunk, width), WIDE),
            shape((chunk, hidden), WIDE),
            shape((4 * chunk, width), WIDE),
            shape((16, 128), WIDE),
        ),
        in_specs=[any_, vmem, smem, any_, vmem, any_, vmem, vmem, vmem, any_, vmem, any_, vmem, vmem, vmem, vmem, any_],
        out_specs=(any_, any_, vmem, vmem, vmem, vmem, vmem),
        scratch_shapes=[
            low(n_tok, width), low(n_tok, width), low(2, 3, width, half), wide(2, 2, half), low(width, width), low(width, hidden), low(hidden, width),
            low(n_tok, width), low(3, 2, n_tok, half), wide(n_tok, n_tok), wide(n_tok, width), wide(n_tok, 128), low(2, half, n_tok),
            wide(n_tok, width), low(n_tok, width), low(2, half, n_tok), low(2, 3, 16, 32, n_tok), low(n_tok, hidden),
            wide(n_tok, width), wide(n_tok, width), wide(2, n_tok, 512), low(2, n_tok, 512), low(n_tok, width), wide(16, width), wide(n_partners, 16, width),
            low(3, 16, 32, width), low(n_wide, 16, 48, half), low(2, 16, 32, width), low(2, 16, 48, half), low(3, 16, 32, width), low(n_wide, 16, 48, half),
            *(low(3, 16 >> k, 32, width) for k in range(1, 5)), *(low(n_wide, 16 >> k, 48, half) for k in range(1, 5)),
            dma(8), dma(2), dma(2), dma(N_MSG, 5), dma(N_MSG, 5), dma(n_partners), dma(n_partners),
        ],
        compiler_params=pltpu.CompilerParams(collective_id=0, has_side_effects=True, vmem_limit_bytes=64 * 2**20 - 2**16),
        cost_estimate=pl.CostEstimate(flops=25_000_000_000, bytes_accessed=24_000_000, transcendentals=12_000_000),
    )(
        tokens, seg_ids, fill_len, jnp.transpose(qkv_weight, (1, 0, 2)), qv_bias, out_weight, out_bias, norm1_gain,
        norm1_bias, in_weight, in_bias.reshape(1, hidden), down_weight, down_bias, norm2_gain,
        norm2_bias, act_range.reshape(1, 4), cotangent,
    )
    layer_out, grad_tokens, qkv_sum, sum_out, sum_in, sum_down, small = outs
    if n_low > 1:
        groups = [[top * n_low + low_ for low_ in range(n_low)] for top in range(16)]
        moves = [((top * n_low + i) * 2 + core, n_low * (2 * top + core) + i) for top in range(16) for i in range(n_low) for core in range(2)]

        def spread(v, dim):
            return lax.psum_scatter(v, "dp", scatter_dimension=dim, axis_index_groups=groups, tiled=True)

        qkv_sum = spread(qkv_sum, 1)
        sum_out, sum_in, sum_down = (lax.ppermute(spread(v, 0), ("dp", "mp"), moves) for v in (sum_out, sum_in, sum_down))
    per = width // (2 * n_dp)
    rows = (per, per, per, 4 * per, per, per, per)
    vectors = [shape((size,), WIDE) for size in rows]
    big = (layer_out, grad_tokens, qkv_sum, sum_out, sum_in, sum_down)
    done = pl.pallas_call(
        functools.partial(hand_out, per),
        out_shape=(*(shape(v.shape, v.dtype) for v in big), shape((2, per), WIDE), *vectors, shape((4,), WIDE)),
        in_specs=[any_] * len(big) + [vmem],
        out_specs=(*([any_] * len(big)), *([vmem] * 9)),
        scratch_shapes=[*(pltpu.VMEM(v.shape, v.dtype) for v in big), dma(2, len(big))],
        compiler_params=pltpu.CompilerParams(vmem_limit_bytes=64 * 2**20 - 2**16),
    )(*big, small)
    layer_out, grad_tokens, qkv_sum, sum_out, sum_in, sum_down, sum_qv, out_b, gain1, shift1, in_b, down_b, gain2, shift2, new_range = done
    qkv_sum = jnp.transpose(qkv_sum, (2, 0, 1))
    return (
        layer_out, grad_tokens, qkv_sum, sum_qv, sum_out, out_b, gain1, shift1, sum_in, in_b, sum_down, down_b, gain2, shift2, new_range,
    )


def solution(mesh):
    n_dp = mesh.shape["dp"]
    both, copies = P(("dp", "mp")), P()
    rows = P(("dp", "mp"), None)
    return jax.shard_map(
        functools.partial(per_device, n_dp),
        mesh=mesh,
        in_specs=(
            rows, P("dp", None), P("dp"), P(None, None, "mp"), P(None, "mp"),
            *([copies] * 11), rows,
        ),
        out_specs=(
            rows, rows, P(None, None, ("mp", "dp")), P(None, ("mp", "dp")), rows, both, both, both, rows, both, rows, both, both, both, copies,
        ),
        check_vma=False,
    )
```

```python
import functools
import math

import jax
import jax.numpy as jnp
from jax import lax
from jax.experimental import pallas as pl
from jax.experimental.pallas import tpu as pltpu
from jax.sharding import PartitionSpec as P

HD = 64
EPSILON = 1e-06
MOMENTUM = 0.9
SQRT_HALF = math.sqrt(0.5)
INV_SQRT_2PI = 1.0 / math.sqrt(2.0 * math.pi)
LOW = jnp.bfloat16
WIDE = jnp.float32
MESH = pl.DeviceIdType.MESH

MESSAGES = (
    ("down", 0, (2, 3, 1, 0)),
    ("down", 1, (1, 0, 2, 3)),
    ("down", 2, (0, 2, 3, 1)),
    ("wide", 0, (2, 0, 1, 3)),
    ("wide", 1, (1, 2, 0, 3)),
    ("wide", 2, (1, 2, 3, 0)),
    ("wide", 3, (1, 2, 3, 0)),
    ("wide", 4, (0, 1, 2, 3)),
    ("wide", 5, (0, 1, 2, 3)),
    ("wide", 6, (1, 2, 0, 3)),
    ("wide", 7, (0, 1, 2, 3)),
)
N_MSG = len(MESSAGES)
GROUPS = {"down": 0, "wide": 3}


SCHEDULE = (
    (("Dp", "Do"), 3, (
        (("Dp", 2), ((0, 0),)),
    )),
    (1, 0),
    (("Ip", "Io", "In"), 4, (
        (("Ip", 0), ((2, 0),)),
        (("Ip", 1), ((3, 0),)),
        (("Ip", 2), ((4, 0),)),
        (("Ip", 3), ((5, 0),)),
    )),
    ("LN", 0), (6, 0), (0, 1), (1, 1), ("Op", 0), (2, 1), ("Oo", 0), ("dm", 0), ("cx", 0), (7, 0),
    (("ab",), 3, (
        (("ab", 0), ((3, 1), (4, 1))),
    )),
    (("Qp",), 3, (
    )),
    (1, 2),
    (("am",), 3, (
        (("am", 0), ((5, 1), (2, 2), (0, 2))),
    )),
    (("Qo",), 3, (
        (("Qo", 0), ((8, 0),)),
        (("Qo", 1), ((9, 0), (7, 1))),
    )),
    (10, 0), ("dc", 0), (4, 2), ("sm", 0), (3, 2), (6, 1), (1, 3), ("tk", 0), (0, 3), (5, 2), (8, 1), (2, 3), (9, 1), (6, 2), (1, 4),
    (7, 2), (10, 1), (3, 3), (4, 3), (5, 3), ("sm", 1), (9, 2), (0, 4), (8, 2), (2, 4), (7, 3), (5, 4), (6, 3), (10, 2), (3, 4), (9, 3),
    ("sm", 2), (4, 4), (8, 3), (6, 4), (7, 4), (10, 3), ("sm", 3), (9, 4), (8, 4), (10, 4), ("sm", 4),
)


def dot(a, b):
    return lax.dot_general(a, b, (((1,), (0,)), ((), ())), preferred_element_type=WIDE)


def dot_nt(a, b):
    return lax.dot_general(a, b, (((1,), (1,)), ((), ())), preferred_element_type=WIDE)


def dot_tn(a, b):
    return lax.dot_general(a, b, (((0,), (0,)), ((), ())), preferred_element_type=WIDE)


def place(chunk, order):
    spot = 0
    for bit in order:
        spot = spot * 2 + (chunk >> bit) % 2
    return spot


class Scatter:
    def __init__(self, n_low, acc, csend, crecv, recvs, send_sem, recv_sem):
        self.acc, self.csend, self.crecv, self.recvs = acc, csend, crecv, recvs
        self.send_sem, self.recv_sem = send_sem, recv_sem
        self.dp, self.mp = lax.axis_index("dp"), lax.axis_index("mp")
        self.n_low = n_low
        self.pending = []
        self.next = dict.fromkeys(range(N_MSG), 0)

    def bit(self, bit):
        return (self.dp // (self.n_low << bit)) % 2

    def partner(self, bit):
        return (self.dp + (self.n_low << bit) * (1 - 2 * self.bit(bit)), self.mp)

    def core_copy(self, group, index):
        m = GROUPS[group] + index
        return pltpu.make_async_remote_copy(
            src_ref=self.csend[group].at[index % 2],
            dst_ref=self.crecv[group].at[index],
            send_sem=self.send_sem.at[m, 0],
            recv_sem=self.recv_sem.at[m, 0],
            device_id=(self.dp, 1 - self.mp),
            device_id_type=MESH,
        )

    def base(self, m, stage):
        order = MESSAGES[m][2]
        spot = 0
        for k in range(stage):
            spot = spot + self.bit(order[k]) * (8 >> k)
        return spot

    def copy(self, m, stage):
        group, index, order = MESSAGES[m]
        count = 16 >> stage
        bit = order[stage - 1]
        start = self.base(m, stage - 1) + (1 - self.bit(bit)) * count
        return pltpu.make_async_remote_copy(
            src_ref=self.acc[group].at[index, pl.ds(start, count)],
            dst_ref=self.recvs[group][stage - 1].at[index],
            send_sem=self.send_sem.at[m, stage],
            recv_sem=self.recv_sem.at[m, stage],
            device_id=self.partner(bit),
            device_id_type=MESH,
        )

    def slot_free(self, group, index):
        if isinstance(index, int):
            if index >= 2:
                self.core_copy(group, index - 2).wait_send()
        else:
            pl.when(index >= 2)(lambda: self.core_copy(group, index - 2).wait_send())

    def add(self, m, received, from_, start, count):
        group, index, _ = MESSAGES[m]
        acc = self.acc[group]
        here = pl.ds(start, count)
        acc[index, here] = acc[index, here] + received[index, pl.ds(from_, count)]

    def step(self, m, stage, out=None):
        group, index, order = MESSAGES[m]
        assert self.next[m] == stage
        self.next[m] = stage + 1
        (self.core_copy(group, index) if stage == 0 else self.copy(m, stage)).wait_recv()
        if stage == 4:
            total = self.acc[group][index, self.base(m, 4)].astype(WIDE) + self.recvs[group][3][index, 0].astype(WIDE)
            out(total)
            return
        received = self.crecv[group] if stage == 0 else self.recvs[group][stage - 1]
        count = 8 >> stage
        base = self.base(m, stage)
        mine = self.bit(order[stage])
        self.add(m, received, (1 - mine) * count, base + (1 - mine) * count, count)
        self.copy(m, stage + 1).start()
        self.pending.append((m, stage + 1))
        self.add(m, received, mine * count, base + mine * count, count)

    def finish(self):
        for group, count in (("down", 3), ("wide", N_MSG - 3)):
            for index in (count - 2, count - 1):
                self.core_copy(group, index).wait_send()
        for m, stage in self.pending:
            self.copy(m, stage).wait_send()


def spot_of(group, index, chunk):
    if isinstance(index, int):
        return place(chunk, MESSAGES[GROUPS[group] + index][2])
    spot = 0
    for other, number, order in MESSAGES:
        if other == group:
            spot = jnp.where(index == number, place(chunk, order), spot)
    return spot


def store_chunks(ref, slot, group, index, result):
    for chunk in range(16):
        if group == "down":
            piece = result[32 * chunk : 32 * chunk + 32]
        else:
            rows, half = result[24 * chunk : 24 * chunk + 24], result.shape[1] // 2
            piece = jnp.concatenate([rows[:, :half], rows[:, half:]], axis=0)
        ref[slot, spot_of(group, index, chunk)] = piece.astype(LOW)


def interleave(ref, values):
    for part in range(2):
        flipped = values(part).T
        for core in range(2):
            groups = [flipped[24 * i : 24 * i + 24] for i in range(core, 16, 2)]
            ref[core, 192 * part : 192 * part + 192, :] = jnp.concatenate(groups, axis=0).astype(LOW)


def kernel(
    n_dp, n_low,
    tok_h, seg_v, fill_s, qkvw_h, qvb_v, outw_h, outb_v, g1_v, b1_v, inw_h, inb_v, downw_h, downb_v, g2_v, b2_v, act_v, cot_h,
    lay_h, gtok_h, gqkv, gout, gin, gdown, small_o,
    tok, cot, wqkv, qvb, wout, win, wdown, clip_in, qkv, bias, ctx, stats, mixed_t, xhat1, clip_mid, clip_mid_t, clip_act_t, slope_f, h2, d_h1, pre_s, act_s, d_pre, sm, sm_r,
    acc_d, acc_w, cs_d, cs_w, cr_d, cr_w, rd1, rd2, rd3, rd4, rw1, rw2, rw3, rw4,
    loc_sem, wsend, wrecv, msend, mrecv, ssend, srecv,
):
    dp, mp = lax.axis_index("dp"), lax.axis_index("mp")
    outb_v, g1_v, b1_v, downb_v, g2_v, b2_v = (v[...].reshape(1, -1) for v in (outb_v, g1_v, b1_v, downb_v, g2_v, b2_v))
    n_bits = n_dp.bit_length() - 1
    tokens, width = tok.shape
    hidden = win.shape[1]
    half = width // 2
    other = 1 - mp
    core_id = (dp, other)

    local = [
        pltpu.make_async_copy(src, dst, loc_sem.at[i])
        for i, (src, dst) in enumerate(
            ((tok_h, tok), (qkvw_h, wqkv.at[mp]), (outw_h, wout), (inw_h, win), (downw_h, wdown), (cot_h, cot))
        )
    ]
    for copy in local[:2]:
        copy.start()
    open_ = dict(enumerate(local))
    def take(i):
        open_.pop(i).wait()

    def dp_partner(b):
        return (dp + (1 << b) * (1 - 2 * ((dp // (1 << b)) % 2)), mp)

    barrier = pltpu.get_barrier_semaphore()
    partners = [core_id] + [dp_partner(b) for b in range(n_bits)]
    for there in partners:
        pl.semaphore_signal(barrier, inc=1, device_id=there, device_id_type=MESH)

    r0, r1, r2, r3 = (act_v[0:1, i : i + 1] for i in range(4))
    i0, i1, i2, i3 = (1.0 / r for r in (r0, r1, r2, r3))

    qvb[mp] = qvb_v[...]
    take(0)
    rb = 64
    def rows_at(i, size=rb):
        return pl.ds(pl.multiple_of(i * size, size), size)

    def clip_rows(i, peak):
        v = tok[rows_at(i), :].astype(WIDE)
        clip_in[rows_at(i), :] = (r0 * jnp.tanh(v * i0)).astype(LOW)
        return jnp.maximum(peak, jnp.max(jnp.abs(v), axis=0, keepdims=True))

    peak0 = lax.fori_loop(0, tokens // rb, clip_rows, jnp.zeros((1, width), WIDE), unroll=4)
    stats[...] = jnp.zeros_like(stats)
    lane = lax.broadcasted_iota(jnp.int32, (1, 128), 1)
    in_head = [lane < HD, lane >= HD]
    qb = 256

    def project(part):
        for j in range(3):
            out = dot(clip_in[...], wqkv[part, j])
            if j == 0:
                out = (out + qvb[part, 0:1, :]).astype(LOW).astype(WIDE) * (HD ** -0.5)
            elif j == 2:
                out = out + qvb[part, 1:2, :]
            qkv[j, part] = out.astype(LOW)

    def attend(part):
        def pair(t, carry):
            at = pl.ds(pl.multiple_of(t * 128, 128), 128)
            k, v = qkv[1, part, :, at], qkv[2, part, :, at]
            nil, one = jnp.zeros_like(v), jnp.ones_like(v)
            kz = [jnp.where(m, k, nil) for m in in_head]
            vz = [jnp.concatenate([jnp.where(m, v, nil), jnp.where(m, one, nil)], axis=1) for m in in_head]
            vz = jnp.concatenate(vz, axis=0)
            head = part * 6 + t * 2
            for i in range(tokens // qb):
                rows = pl.ds(i * qb, qb)
                q = qkv[0, part, rows, at]
                es, tops = [], []
                for h in range(2):
                    s = dot_nt(q, kz[h]) + bias[rows, :]
                    tops.append(jnp.max(s, axis=-1, keepdims=True))
                    es.append(jnp.exp(s - tops[h]).astype(LOW))
                both = dot(jnp.concatenate(es, axis=1), vz)
                norm = both[:, 128:]
                ctx[rows, pl.ds(pl.multiple_of(part * half + t * 128, 128), 128)] = both[:, :128] / norm
                total = jnp.where(in_head[0], tops[0], tops[1]) + jnp.log(norm)
                found = jnp.where(lane == head, total[:, 0:1], stats[rows, :])
                stats[rows, :] = jnp.where(lane == head + 1, total[:, HD : HD + 1], found)
            return carry

        lax.fori_loop(0, half // 128, pair, 0, unroll=True)

    take(1)
    project(mp)
    pl.semaphore_wait(barrier, len(partners))
    weight_copies = [
        pltpu.make_async_remote_copy(
            src_ref=src, dst_ref=dst, send_sem=wsend.at[i], recv_sem=wrecv.at[i], device_id=core_id, device_id_type=MESH
        )
        for i, (src, dst) in enumerate(((qkvw_h, wqkv.at[mp]), (qvb_v, qvb.at[mp])))
    ]
    for copy in weight_copies:
        copy.start()
    open_["w0"], open_["w1"] = weight_copies
    for copy in local[2:]:
        copy.start()
    row = jnp.sum(jnp.where(lax.broadcasted_iota(jnp.int32, seg_v.shape, 0) == mp, seg_v[...], 0), axis=0, keepdims=True).astype(WIDE)
    fill = fill_s[mp]
    seg_col = jnp.broadcast_to(row, (128, tokens)).T[:, 0:1]
    blk = 128

    for i in range(tokens // blk):
        kpos = lax.broadcasted_iota(jnp.int32, (blk, tokens), 1)
        qpos = lax.broadcasted_iota(jnp.int32, (blk, tokens), 0) + i * blk
        live = (kpos < fill) | (kpos == qpos)
        same = seg_col[i * blk : i * blk + blk] == row
        bias[i * blk : i * blk + blk, :] = jnp.where(same & live, 0.0, -1e30)

    attend(mp)
    take("w0")
    take("w1")
    project(other)
    attend(other)

    take(2)

    def mix_rows(i, peak):
        c = ctx[rows_at(i), :]
        clip_mid[rows_at(i), :] = (r1 * jnp.tanh(c * i1)).astype(LOW)
        return jnp.maximum(peak, jnp.max(jnp.abs(c), axis=0, keepdims=True))

    peak1 = lax.fori_loop(0, tokens // rb, mix_rows, jnp.zeros((1, width), WIDE), unroll=4)
    interleave(mixed_t, lambda part: clip_mid[:, half * part : half * part + half].astype(WIDE))
    h2[...] = dot(clip_mid[...], wout[...])

    def norm(v):
        center = v - jnp.mean(v, axis=-1, keepdims=True)
        inv = lax.rsqrt(jnp.mean(center * center, axis=-1, keepdims=True) + EPSILON)
        return center * inv, inv

    def norm1_rows(i, peak):
        rows = rows_at(i)
        xhat, inv = norm(tok[rows, :].astype(WIDE) + (h2[rows, :] + outb_v))
        xhat1[rows, :] = xhat
        stats[rows, :] = jnp.where(lane == 127, inv, stats[rows, :])
        normed = xhat * g1_v + b1_v
        h2[rows, :] = normed + downb_v
        clip_mid[rows, :] = (r2 * jnp.tanh(normed * i2)).astype(LOW)
        return jnp.maximum(peak, jnp.max(jnp.abs(normed), axis=0, keepdims=True))

    peak2 = lax.fori_loop(0, tokens // rb, norm1_rows, jnp.zeros((1, width), WIDE), unroll=4)
    interleave(clip_mid_t, lambda part: clip_mid[:, half * part : half * part + half].astype(WIDE))

    take(3)
    take(4)
    fb, fr = pre_s.shape[2], 32
    n_fb = hidden // fb

    def feed_in(b):
        pre_s[b % 2] = dot(clip_mid[...], win[:, fb * b : fb * b + fb])

    def feed_act(b, peak):
        cols = slice(fb * b, fb * b + fb)
        for r in range(0, tokens, fr):
            rows = slice(r, r + fr)
            pre = pre_s[b % 2, rows, :] + inb_v[:, cols]
            cdf = 0.5 + 0.5 * lax.erf(pre * SQRT_HALF)
            act = pre * cdf
            th = jnp.tanh(act * i3)
            act_s[b % 2, rows, :] = (r3 * th).astype(LOW)
            bell = jnp.exp(pre * pre * -0.5) * INV_SQRT_2PI
            slope_f[rows, cols] = ((1.0 - th * th) * (cdf + pre * bell)).astype(LOW)
            peak = jnp.maximum(peak, jnp.max(jnp.abs(act), axis=0, keepdims=True))
        return peak

    def feed_out(b):
        out = act_s[b % 2]
        flipped = out.T
        for i in range(fb // 32):
            group = b * (fb // 32) + i
            owner = group // 3
            clip_act_t[owner % 2, group % 3, owner // 2] = flipped[32 * i : 32 * i + 32]
        h2[...] += dot(out, wdown[fb * b : fb * b + fb, :])

    peak3 = jnp.zeros((1, fb), WIDE)
    feed_in(0)
    for b in range(n_fb):
        if b + 1 < n_fb:
            feed_in(b + 1)
        peak3 = feed_act(b, peak3)
        if b > 0:
            feed_out(b - 1)
    feed_out(n_fb - 1)

    take(5)
    zero_row = jnp.zeros((1, width), WIDE)

    def norm2_rows(i, sums):
        rows = rows_at(i)
        xhat, inv = norm(h2[rows, :])
        e = cot[rows, :].astype(WIDE)
        clip_in_row = (xhat * g2_v + b2_v).astype(LOW)
        clip_mid[rows, :] = clip_in_row
        w = e * g2_v
        d = inv * (w - jnp.mean(w, axis=-1, keepdims=True) - xhat * jnp.mean(w * xhat, axis=-1, keepdims=True))
        h2[rows, :] = d
        low = d.astype(LOW)
        cot[rows, :] = low
        return (
            sums[0] + jnp.sum(e * xhat, axis=0, keepdims=True),
            sums[1] + jnp.sum(e, axis=0, keepdims=True),
            sums[2] + jnp.sum(low.astype(WIDE), axis=0, keepdims=True),
        )

    gain2, shift2, down_bias = lax.fori_loop(0, tokens // rb, norm2_rows, (zero_row, zero_row, zero_row), unroll=4)
    lay_copy = pltpu.make_async_copy(clip_mid, lay_h, loc_sem.at[6])
    lay_copy.start()

    sm[...] = jnp.zeros_like(sm)
    sm[7:8, :] = down_bias
    sm[8:9, :] = gain2
    sm[9:10, :] = shift2
    lane_w = lax.broadcasted_iota(jnp.int32, (1, width), 1)
    peaks = zero_row
    for i, peak in enumerate((peak0, peak1, peak2, peak3)):
        peaks = jnp.where(lane_w == i, jnp.max(peak, axis=-1, keepdims=True), peaks)
    sm[12:13, :] = peaks

    scatter = Scatter(
        n_low,
        {"down": acc_d, "wide": acc_w},
        {"down": cs_d, "wide": cs_w},
        {"down": cr_d, "wide": cr_w},
        {"down": (rd1, rd2, rd3, rd4), "wide": (rw1, rw2, rw3, rw4)},
        msend,
        mrecv,
    )

    def out_down(index):
        def write(total):
            gdown[32 * index : 32 * index + 32, :] = total
        return write

    def out_wide(ref, at):
        def write(total):
            both = jnp.concatenate([total[:24], total[24:]], axis=1)
            if ref is gqkv:
                ref[at] = both
            else:
                ref[:, width * at : width * at + width] = both
        return write

    outs = [out_down(i) for i in range(3)] + [out_wide(gin, i) for i in range(4)] + [out_wide(gout, 0)] + [out_wide(gqkv, i) for i in range(3)]

    def step(m, stage):
        scatter.step(m, stage, outs[m])

    def send_part(group, index, result):
        scatter.slot_free(group, index)
        store_chunks(cs_d if group == "down" else cs_w, index % 2, group, index, result)
        scatter.core_copy(group, index).start()

    def own_part(group, index, result):
        store_chunks(acc_d if group == "down" else acc_w, index, group, index, result)

    def down_send(i):
        send_part("down", i, dot(clip_act_t[other, i].reshape(16 * 32, tokens), cot[...]))

    def down_own(i):
        own_part("down", i, dot(clip_act_t[mp, i].reshape(16 * 32, tokens), cot[...]))

    def block(i):
        return pl.ds(pl.multiple_of(i * width, width), width)

    def in_send(i):
        d_pre[...] = (dot_nt(cot[...], wdown[block(i), :]) * slope_f[:, block(i)].astype(WIDE)).astype(LOW)
        send_part("wide", i, dot(clip_mid_t[other], d_pre[...]))

    def in_own(i):
        own_part("wide", i, dot(clip_mid_t[mp], d_pre[...]))
        sm[pl.ds(3 + i, 1), :] = jnp.sum(d_pre[...].astype(WIDE), axis=0, keepdims=True)

    def in_back(i):
        d_h1[...] += dot_nt(d_pre[...], win[:, block(i)])

    def norm1_back(_):
        def some(i, sums):
            rows = rows_at(i)
            xhat = xhat1[rows, :]
            inv = stats[rows, 127:128]
            th = jnp.tanh((xhat * g1_v + b1_v) * i2)
            e = h2[rows, :] + d_h1[rows, :] * (1.0 - th * th)
            w = e * g1_v
            d = inv * (w - jnp.mean(w, axis=-1, keepdims=True) - xhat * jnp.mean(w * xhat, axis=-1, keepdims=True))
            d_h1[rows, :] = d
            low = d.astype(LOW)
            cot[rows, :] = low
            return (
                sums[0] + jnp.sum(e * xhat, axis=0, keepdims=True),
                sums[1] + jnp.sum(e, axis=0, keepdims=True),
                sums[2] + jnp.sum(low.astype(WIDE), axis=0, keepdims=True),
            )

        gain1, shift1, out_bias = lax.fori_loop(0, tokens // rb, some, (zero_row, zero_row, zero_row), unroll=4)
        sm[0:1, :] = out_bias
        sm[1:2, :] = gain1
        sm[2:3, :] = shift1

    def out_send(_):
        send_part("wide", 4, dot(mixed_t[other], cot[...]))

    def out_own(_):
        own_part("wide", 4, dot(mixed_t[mp], cot[...]))

    def mixed_back(_):
        h2[...] = dot_nt(cot[...], wout[...])

    def context_back(_):
        lay_copy.wait()
        def some(i, carry):
            rows = rows_at(i)
            th = jnp.tanh(ctx[rows, :] * i1)
            clip_mid[rows, :] = (h2[rows, :].astype(LOW).astype(WIDE) * (1.0 - th * th)).astype(LOW)
            return carry

        lax.fori_loop(0, tokens // rb, some, 0, unroll=4)

    def attend_back(part, t):
        at = pl.ds(pl.multiple_of(t * 128, 128), 128)
        wide_at = pl.ds(pl.multiple_of(part * half + t * 128, 128), 128)
        k, v = qkv[1, part, :, at], qkv[2, part, :, at]
        split = lambda v: [jnp.where(m, v, jnp.zeros_like(v)) for m in in_head]
        kz, vz = split(k), split(v)
        d_k, d_v = jnp.zeros((tokens, 128), WIDE), jnp.zeros((tokens, 128), WIDE)
        for i in range(tokens // qb):
            rows = pl.ds(i * qb, qb)
            q = qkv[0, part, rows, at]
            dc = clip_mid[rows, wide_at]
            prod = dc.astype(WIDE) * ctx[rows, wide_at]
            found = stats[rows, :]
            ps, ds = [], []
            for h in range(2):
                mean = jnp.sum(jnp.where(in_head[h], prod, 0.0), axis=-1, keepdims=True)
                total = jnp.sum(jnp.where(lane == (part * 6 + t * 2 + h), found, 0.0), axis=-1, keepdims=True)
                p = jnp.exp(dot_nt(q, kz[h]) + bias[rows, :] - total)
                ds.append((p * (dot_nt(dc, vz[h]) - mean)).astype(LOW))
                ps.append(p.astype(LOW))
            d_q = dot(jnp.concatenate(ds, axis=1), jnp.concatenate(kz, axis=0))
            d_k = d_k + dot_tn(jnp.concatenate(ds, axis=0), jnp.concatenate(split(q), axis=0))
            d_v = d_v + dot_tn(jnp.concatenate(ps, axis=0), jnp.concatenate(split(dc), axis=0))
            qkv[0, part, rows, at] = (d_q * (HD ** -0.5)).astype(LOW)
        qkv[1, part, :, at] = d_k.astype(LOW)
        qkv[2, part, :, at] = d_v.astype(LOW)

    def qkv_send(j):
        send_part("wide", 5 + j, dot_tn(qkv[j, other], clip_in[...]))

    def qkv_own(j):
        own_part("wide", 5 + j, dot_tn(qkv[j, mp], clip_in[...]))

    def in_tokens(_):
        for r, j in ((10, 0), (11, 2)):
            for part in range(2):
                sm[r : r + 1, half * part : half * part + half] = jnp.sum(qkv[j, part].astype(WIDE), axis=0, keepdims=True)
        small_copy(0).start()
        h2[...] = jnp.zeros_like(h2)

        def some(n, carry):
            h2[...] += dot_nt(qkv[n % 3, n // 3], wqkv[n // 3, n % 3])
            return carry

        lax.fori_loop(0, 6, some, 0)

    def token_grad(_):
        def some(i, carry):
            rows = rows_at(i)
            th = jnp.tanh(tok[rows, :].astype(WIDE) * i0)
            d_h1[rows, :] += h2[rows, :] * (1.0 - th * th)
            return carry

        lax.fori_loop(0, tokens // rb, some, 0, unroll=4)
        tok_copy.start()

    tok_copy = pltpu.make_async_copy(d_h1, gtok_h, loc_sem.at[7])
    is_peak = lax.broadcasted_iota(jnp.int32, sm.shape, 0) == 12

    def small_copy(k):
        return pltpu.make_async_remote_copy(
            src_ref=sm,
            dst_ref=sm_r.at[k],
            send_sem=ssend.at[k],
            recv_sem=srecv.at[k],
            device_id=partners[k],
            device_id_type=MESH,
        )

    def small_end(k):
        small_copy(k).wait()
        sm[...] = jnp.where(is_peak, jnp.maximum(sm[...], sm_r[k]), sm[...] + sm_r[k])
        if k + 1 < len(partners):
            small_copy(k + 1).start()

    parts = {
        "Dp": down_send, "Do": down_own, "Ip": in_send, "Io": in_own, "In": in_back, "LN": norm1_back, "Op": out_send, "Oo": out_own,
        "dm": mixed_back, "cx": context_back, "ab": lambda t: attend_back(other, t), "am": lambda t: attend_back(mp, t),
        "Qp": qkv_send, "Qo": qkv_own, "dc": in_tokens, "tk": token_grad, "sm": small_end,
    }
    d_h1[...] = jnp.zeros_like(d_h1)

    def loop(names, count, after):
        def round_(i, carry):
            for name in names:
                parts[name](i)
                for k in range(count):
                    todo = after.get((name, k), ())
                    if todo:
                        pl.when(i == k)(lambda todo=todo: [step(*which) for which in todo] and None)
            return carry

        lax.fori_loop(0, count, round_, 0)

    for entry in SCHEDULE:
        if len(entry) == 3:
            loop(entry[0], entry[1], dict(entry[2]))
        elif isinstance(entry[0], str):
            parts[entry[0]](entry[1])
        else:
            step(*entry)
    for k in range(5, len(partners)):
        small_end(k)
    scatter.finish()

    per = width // (2 * n_dp)
    me = dp * 2 + mp
    sums = sm[...]
    out = pltpu.roll(sums, (width - per * me) % width, 1)[:, :128]
    qv_out = pltpu.roll(sums, (width - (mp * half + per * dp)) % width, 1)[:, :128]
    wide_at = 4 * per * me
    in_rows = pltpu.roll(sums, (width - wide_at % width) % width, 1)[:, :128]
    r_iota = lax.broadcasted_iota(jnp.int32, out.shape, 0)
    in_row = jnp.sum(jnp.where(r_iota == 3 + wide_at // width, in_rows, 0.0), axis=0, keepdims=True)
    out = jnp.where((r_iota == 10) | (r_iota == 11), qv_out, out)
    out = jnp.where(r_iota == 3, in_row, out)
    small_o[...] = out
    small_o[12:13, 0:4] = MOMENTUM * act_v[...] + (1.0 - MOMENTUM) * sums[12:13, 0:4]
    tok_copy.wait()


def hand_out(per, *refs):
    big, small, outs, held, sem = refs[:6], refs[6], refs[7:22], refs[22:28], refs[28]
    ins = [pltpu.make_async_copy(src, mid, sem.at[0, i]) for i, (src, mid) in enumerate(zip(big, held))]
    away = [pltpu.make_async_copy(mid, dst, sem.at[1, i]) for i, (mid, dst) in enumerate(zip(held, outs))]
    for copy in ins:
        copy.start()
    outs[6][...] = small[10:12, :per]
    for ref, row in zip(outs[7:], (0, 1, 2, 3, 7, 8, 9, 12)):
        ref[...] = small[row, : ref.shape[0]]
    for here, there in zip(ins, away):
        here.wait()
        there.start()
    for copy in away:
        copy.wait()


def per_device(n_dp, tokens, seg_ids, fill_len, qkv_weight, qv_bias, out_weight, out_bias, norm1_gain, norm1_bias, in_weight, in_bias,
               down_weight, down_bias, norm2_gain, norm2_bias, act_range, cotangent):
    n_tok, width = tokens.shape
    hidden = in_weight.shape[1]
    half = width // 2
    n_low = max(1, n_dp // 16)
    any_, vmem = pl.BlockSpec(memory_space=pl.ANY), pl.BlockSpec(memory_space=pltpu.VMEM)
    smem = pl.BlockSpec(memory_space=pltpu.SMEM)
    chunk = width // 32
    shape = jax.ShapeDtypeStruct
    low = lambda *s: pltpu.VMEM(s, LOW)
    wide = lambda *s: pltpu.VMEM(s, WIDE)
    dma = lambda *s: pltpu.SemaphoreType.DMA(s)
    n_partners = n_dp.bit_length()
    n_wide = N_MSG - 3
    outs = pl.pallas_call(
        functools.partial(kernel, n_dp, n_low),
        out_shape=(
            shape((n_tok, width), LOW),
            shape((n_tok, width), WIDE),
            shape((3, chunk, width), WIDE),
            shape((chunk, width), WIDE),
            shape((chunk, hidden), WIDE),
            shape((4 * chunk, width), WIDE),
            shape((16, 128), WIDE),
        ),
        in_specs=[any_, vmem, smem, any_, vmem, any_, vmem, vmem, vmem, any_, vmem, any_, vmem, vmem, vmem, vmem, any_],
        out_specs=(any_, any_, vmem, vmem, vmem, vmem, vmem),
        scratch_shapes=[
            low(n_tok, width), low(n_tok, width), low(2, 3, width, half), wide(2, 2, half), low(width, width), low(width, hidden), low(hidden, width),
            low(n_tok, width), low(3, 2, n_tok, half), wide(n_tok, n_tok), wide(n_tok, width), wide(n_tok, 128), low(2, half, n_tok),
            wide(n_tok, width), low(n_tok, width), low(2, half, n_tok), low(2, 3, 16, 32, n_tok), low(n_tok, hidden),
            wide(n_tok, width), wide(n_tok, width), wide(2, n_tok, 512), low(2, n_tok, 512), low(n_tok, width), wide(16, width), wide(n_partners, 16, width),
            low(3, 16, 32, width), low(n_wide, 16, 48, half), low(2, 16, 32, width), low(2, 16, 48, half), low(3, 16, 32, width), low(n_wide, 16, 48, half),
            *(low(3, 16 >> k, 32, width) for k in range(1, 5)), *(low(n_wide, 16 >> k, 48, half) for k in range(1, 5)),
            dma(8), dma(2), dma(2), dma(N_MSG, 5), dma(N_MSG, 5), dma(n_partners), dma(n_partners),
        ],
        compiler_params=pltpu.CompilerParams(collective_id=0, has_side_effects=True, vmem_limit_bytes=64 * 2**20 - 2**16),
        cost_estimate=pl.CostEstimate(flops=25_000_000_000, bytes_accessed=24_000_000, transcendentals=12_000_000),
    )(
        tokens, seg_ids, fill_len, jnp.transpose(qkv_weight, (1, 0, 2)), qv_bias, out_weight, out_bias, norm1_gain,
        norm1_bias, in_weight, in_bias.reshape(1, hidden), down_weight, down_bias, norm2_gain,
        norm2_bias, act_range.reshape(1, 4), cotangent,
    )
    layer_out, grad_tokens, qkv_sum, sum_out, sum_in, sum_down, small = outs
    if n_low > 1:
        groups = [[top * n_low + low_ for low_ in range(n_low)] for top in range(16)]
        moves = [((top * n_low + i) * 2 + core, n_low * (2 * top + core) + i) for top in range(16) for i in range(n_low) for core in range(2)]

        def spread(v, dim):
            return lax.psum_scatter(v, "dp", scatter_dimension=dim, axis_index_groups=groups, tiled=True)

        qkv_sum = spread(qkv_sum, 1)
        sum_out, sum_in, sum_down = (lax.ppermute(spread(v, 0), ("dp", "mp"), moves) for v in (sum_out, sum_in, sum_down))
    per = width // (2 * n_dp)
    rows = (per, per, per, 4 * per, per, per, per)
    vectors = [shape((size,), WIDE) for size in rows]
    big = (layer_out, grad_tokens, qkv_sum, sum_out, sum_in, sum_down)
    done = pl.pallas_call(
        functools.partial(hand_out, per),
        out_shape=(*(shape(v.shape, v.dtype) for v in big), shape((2, per), WIDE), *vectors, shape((4,), WIDE)),
        in_specs=[any_] * len(big) + [vmem],
        out_specs=(*([any_] * len(big)), *([vmem] * 9)),
        scratch_shapes=[*(pltpu.VMEM(v.shape, v.dtype) for v in big), dma(2, len(big))],
        compiler_params=pltpu.CompilerParams(vmem_limit_bytes=64 * 2**20 - 2**16),
    )(*big, small)
    layer_out, grad_tokens, qkv_sum, sum_out, sum_in, sum_down, sum_qv, out_b, gain1, shift1, in_b, down_b, gain2, shift2, new_range = done
    qkv_sum = jnp.transpose(qkv_sum, (2, 0, 1))
    return (
        layer_out, grad_tokens, qkv_sum, sum_qv, sum_out, out_b, gain1, shift1, sum_in, in_b, sum_down, down_b, gain2, shift2, new_range,
    )


def solution(mesh):
    n_dp = mesh.shape["dp"]
    both, copies = P(("dp", "mp")), P()
    rows = P(("dp", "mp"), None)
    return jax.shard_map(
        functools.partial(per_device, n_dp),
        mesh=mesh,
        in_specs=(
            rows, P("dp", None), P("dp"), P(None, None, "mp"), P(None, "mp"),
            *([copies] * 11), rows,
        ),
        out_specs=(
            rows, rows, P(None, None, ("mp", "dp")), P(None, ("mp", "dp")), rows, both, both, both, rows, both, rows, both, both, both, copies,
        ),
        check_vma=False,
    )
```

```python
import functools
import math

import jax
import jax.numpy as jnp
from jax import lax
from jax.experimental import pallas as pl
from jax.experimental.pallas import tpu as pltpu
from jax.sharding import PartitionSpec as P

HD = 64
EPSILON = 1e-06
MOMENTUM = 0.9
SQRT_HALF = math.sqrt(0.5)
INV_SQRT_2PI = 1.0 / math.sqrt(2.0 * math.pi)
LOW = jnp.bfloat16
WIDE = jnp.float32
MESH = pl.DeviceIdType.MESH

MESSAGES = (
    ("down", 0, (0, 1, 2, 3)),
    ("down", 1, (2, 0, 1, 3)),
    ("down", 2, (1, 0, 2, 3)),
    ("wide", 0, (1, 0, 2, 3)),
    ("wide", 1, (2, 0, 1, 3)),
    ("wide", 2, (2, 0, 1, 3)),
    ("wide", 3, (1, 2, 0, 3)),
    ("wide", 4, (0, 2, 1, 3)),
    ("wide", 5, (0, 1, 2, 3)),
    ("wide", 6, (1, 2, 0, 3)),
    ("wide", 7, (0, 1, 2, 3)),
)
N_MSG = len(MESSAGES)
GROUPS = {"down": 0, "wide": 3}
SLOTS = {"down": 3, "wide": 2}


SCHEDULE = (
    (("Dp",), 3, (
    )),
    (("Do",), 3, (
        (("Do", 0), ((0, 0),)),
        (("Do", 1), ((1, 0),)),
    )),
    (("Ip", "Io", "In"), 4, (
        (("Ip", 0), ((2, 0),)),
        (("In", 0), ((3, 0),)),
        (("Io", 1), ((0, 1),)),
        (("In", 1), ((1, 1), (4, 0))),
        (("Ip", 2), ((2, 1),)),
        (("In", 2), ((5, 0),)),
    )),
    (1, 2), (6, 0), ("LN", 0), (4, 1), ("Op", 0), ("Oo", 0), ("dm", 0), (3, 1), (2, 2), (7, 0), ("cx", 0),
    (("ab",), 3, (
        (("ab", 1), ((4, 2),)),
    )),
    (5, 1), (0, 2),
    (("Qp",), 3, (
    )),
    (3, 2),
    (("am",), 3, (
        (("am", 0), ((1, 3), (2, 3))),
        (("am", 1), ((0, 3),)),
    )),
    (7, 1),
    (("Qo",), 3, (
        (("Qo", 0), ((8, 0), (3, 3), (6, 1))),
        (("Qo", 1), ((9, 0),)),
    )),
    (10, 0), ("hs", 0),
    (("dc",), 3, (
        (("dc", 0), (("sm", 0),)),
    )),
    ("tk", 0), (4, 3), (5, 2), (7, 2), (9, 1), (8, 1), (6, 2), (5, 3), ("sm", 1), (7, 3), (9, 2), (10, 1), (8, 2), ("sm", 2), (10, 2),
    (6, 3), (8, 3), (9, 3), (10, 3), ("sm", 3), (1, 4), (2, 4), (0, 4), (3, 4), (4, 4), (5, 4), (7, 4), ("sm", 4), (6, 4), (8, 4), (9, 4),
    (10, 4),
)


def dot(a, b):
    return lax.dot_general(a, b, (((1,), (0,)), ((), ())), preferred_element_type=WIDE)


def dot_nt(a, b):
    return lax.dot_general(a, b, (((1,), (1,)), ((), ())), preferred_element_type=WIDE)


def dot_tn(a, b):
    return lax.dot_general(a, b, (((0,), (0,)), ((), ())), preferred_element_type=WIDE)


def place(chunk, order):
    spot = 0
    for bit in order:
        spot = spot * 2 + (chunk >> bit) % 2
    return spot


class Scatter:
    def __init__(self, n_low, acc, csend, crecv, recvs, send_sem, recv_sem):
        self.acc, self.csend, self.crecv, self.recvs = acc, csend, crecv, recvs
        self.send_sem, self.recv_sem = send_sem, recv_sem
        self.dp, self.mp = lax.axis_index("dp"), lax.axis_index("mp")
        self.n_low = n_low
        self.pending = []
        self.next = dict.fromkeys(range(N_MSG), 0)

    def bit(self, bit):
        return (self.dp // (self.n_low << bit)) % 2

    def partner(self, bit):
        return (self.dp + (self.n_low << bit) * (1 - 2 * self.bit(bit)), self.mp)

    def core_copy(self, group, index):
        m = GROUPS[group] + index
        return pltpu.make_async_remote_copy(
            src_ref=self.csend[group].at[index % SLOTS[group]],
            dst_ref=self.crecv[group].at[index],
            send_sem=self.send_sem.at[m, 0, 0],
            recv_sem=self.recv_sem.at[m, 0, 0],
            device_id=(self.dp, 1 - self.mp),
            device_id_type=MESH,
        )

    def base(self, m, stage):
        order = MESSAGES[m][2]
        spot = 0
        for k in range(stage):
            spot = spot + self.bit(order[k]) * (8 >> k)
        return spot

    def copies(self, m, stage):
        group, index, order = MESSAGES[m]
        count = 16 >> stage
        bit = order[stage - 1]
        start = self.base(m, stage - 1) + (1 - self.bit(bit)) * count
        if stage == 4:
            parts = [(0, 1)]
        else:
            mine = self.bit(order[stage])
            parts = [((1 - mine) * (count // 2), count // 2), (mine * (count // 2), count // 2)]
        return [
            pltpu.make_async_remote_copy(
                src_ref=self.acc[group].at[index, pl.ds(start + first, size)],
                dst_ref=self.recvs[group][stage - 1].at[index, pl.ds(first, size)],
                send_sem=self.send_sem.at[m, stage, n],
                recv_sem=self.recv_sem.at[m, stage, n],
                device_id=self.partner(bit),
                device_id_type=MESH,
            )
            for n, (first, size) in enumerate(parts)
        ]

    def slot_free(self, group, index):
        old = index - SLOTS[group]
        if isinstance(index, int):
            if old >= 0:
                self.core_copy(group, old).wait_send()
        else:
            pl.when(old >= 0)(lambda: self.core_copy(group, old).wait_send())

    def add(self, m, received, from_, start, count):
        group, index, _ = MESSAGES[m]
        acc = self.acc[group]
        here = pl.ds(start, count)
        acc[index, here] = acc[index, here] + received[index, pl.ds(from_, count)]

    def add_half(self, m, stage, keep):
        group, index, order = MESSAGES[m]
        received = self.crecv[group] if stage == 0 else self.recvs[group][stage - 1]
        count = 8 >> stage
        mine = self.bit(order[stage])
        half = mine if keep else 1 - mine
        self.add(m, received, half * count, self.base(m, stage) + half * count, count)

    def step(self, m, stage, out=None):
        group, index, _ = MESSAGES[m]
        assert self.next[m] == stage
        self.next[m] = stage + 1
        if stage == 0:
            self.core_copy(group, index).wait_recv()
        else:
            if stage >= 2:
                self.copies(m, stage - 1)[1].wait_recv()
            self.add_half(m, stage - 1, True)
            self.copies(m, stage)[0].wait_recv()
        if stage == 4:
            total = self.acc[group][index, self.base(m, 4)].astype(WIDE) + self.recvs[group][3][index, 0].astype(WIDE)
            out(total)
            return
        self.add_half(m, stage, False)
        for copy in self.copies(m, stage + 1):
            copy.start()
        self.pending.append((m, stage + 1))

    def finish(self):
        for group, count in (("down", 3), ("wide", N_MSG - 3)):
            for index in range(count - SLOTS[group], count):
                self.core_copy(group, index).wait_send()
        for m, stage in self.pending:
            for copy in self.copies(m, stage):
                copy.wait_send()


def spot_of(group, index, chunk):
    if isinstance(index, int):
        return place(chunk, MESSAGES[GROUPS[group] + index][2])
    spot = 0
    for other, number, order in MESSAGES:
        if other == group:
            spot = jnp.where(index == number, place(chunk, order), spot)
    return spot


def store_chunks(ref, slot, group, index, result):
    for chunk in range(16):
        if group == "down":
            piece = result[32 * chunk : 32 * chunk + 32]
        else:
            rows, half = result[24 * chunk : 24 * chunk + 24], result.shape[1] // 2
            piece = jnp.concatenate([rows[:, :half], rows[:, half:]], axis=0)
        ref[slot, spot_of(group, index, chunk)] = piece.astype(LOW)


def interleave(ref, values):
    for part in range(2):
        flipped = values(part).T
        for core in range(2):
            groups = [flipped[24 * i : 24 * i + 24] for i in range(core, 16, 2)]
            ref[core, 192 * part : 192 * part + 192, :] = jnp.concatenate(groups, axis=0).astype(LOW)


def kernel(
    n_dp, n_low,
    tok_h, seg_v, fill_s, qkvw_h, qvb_v, outw_h, outb_v, g1_v, b1_v, inw_h, inb_v, downw_h, downb_v, g2_v, b2_v, act_v, range_s, cot_h,
    lay_h, gtok_h, gqkv_h, gout_h, gin_h, gdown_h, small_o,
    tok, cot, wqkv, qvb, wout, win, wdown, clip_in, qkv, bias, ctx, stats, mixed_t, xhat1, clip_mid, clip_mid_t, clip_act_t, slope_f, h2, d_h1, pre_b, act_a, act_b, vec_s, peak_s, sm, sm_r,
    acc_d, acc_w, cs_d, cs_w, cr_d, cr_w, rd1, rd2, rd3, rd4, rw1, rw2, rw3, rw4,
    gqkv, gout, gin, gdown, out_sem, loc_sem, wsend, wrecv, msend, mrecv, ssend, srecv,
):
    dp, mp = lax.axis_index("dp"), lax.axis_index("mp")
    for i, v in enumerate((outb_v, g1_v, b1_v, downb_v, g2_v, b2_v)):
        vec_s[i : i + 1, :] = v[...].reshape(1, -1)
    n_bits = n_dp.bit_length() - 1
    tokens, width = tok.shape
    hidden = win.shape[1]
    half = width // 2
    other = 1 - mp
    core_id = (dp, other)

    local = [
        pltpu.make_async_copy(src, dst, loc_sem.at[i])
        for i, (src, dst) in enumerate(
            ((tok_h, tok), (qkvw_h, wqkv.at[mp]), (outw_h, wout), (inw_h, win), (downw_h, wdown), (cot_h, cot))
        )
    ]
    for copy in local[:2]:
        copy.start()
    open_ = dict(enumerate(local))
    def take(i):
        open_.pop(i).wait()

    def dp_partner(b):
        return (dp + (1 << b) * (1 - 2 * ((dp // (1 << b)) % 2)), mp)

    barrier = pltpu.get_barrier_semaphore()
    partners = [core_id] + [dp_partner(b) for b in reversed(range(2, n_bits))] + [dp_partner(b) for b in range(2)]
    for there in partners:
        pl.semaphore_signal(barrier, inc=1, device_id=there, device_id_type=MESH)

    r0, r1, r2, r3 = (range_s[i] for i in range(4))
    i0, i1, i2, i3 = (1.0 / r for r in (r0, r1, r2, r3))

    qvb[mp] = qvb_v[...]
    take(0)
    rb = 256
    def rows_at(i, size=rb):
        return pl.ds(pl.multiple_of(i * size, size), size)

    def clip_rows(i, peak):
        v = tok[rows_at(i), :].astype(WIDE)
        clip_in[rows_at(i), :] = (r0 * jnp.tanh(v * i0)).astype(LOW)
        return jnp.maximum(peak, jnp.max(jnp.abs(v), axis=0, keepdims=True))

    peak_s[0:1, :] = lax.fori_loop(0, tokens // rb, clip_rows, jnp.zeros((1, width), WIDE), unroll=4)
    stats[...] = jnp.zeros_like(stats)
    lane = lax.broadcasted_iota(jnp.int32, (1, 128), 1)
    in_head = [lane < HD, lane >= HD]
    qb = 256

    def project(part):
        for j in range(3):
            out = dot(clip_in[...], wqkv[part, j])
            if j == 0:
                out = (out + qvb[part, 0:1, :]).astype(LOW).astype(WIDE) * (HD ** -0.5)
            elif j == 2:
                out = out + qvb[part, 1:2, :]
            qkv[j, part] = out.astype(LOW)

    def attend(part):
        def pair(t, carry):
            at = pl.ds(pl.multiple_of(t * 128, 128), 128)
            k, v = qkv[1, part, :, at], qkv[2, part, :, at]
            nil, one = jnp.zeros_like(v), jnp.ones_like(v)
            kz = [jnp.where(m, k, nil) for m in in_head]
            vz = [jnp.concatenate([jnp.where(m, v, nil), jnp.where(m, one, nil)], axis=1) for m in in_head]
            vz = jnp.concatenate(vz, axis=0)
            head = part * 6 + t * 2
            for i in range(tokens // qb):
                rows = pl.ds(i * qb, qb)
                q = qkv[0, part, rows, at]
                es, tops = [], []
                for h in range(2):
                    s = dot_nt(q, kz[h]) + bias[rows, :]
                    tops.append(jnp.max(s, axis=-1, keepdims=True))
                    es.append(jnp.exp(s - tops[h]).astype(LOW))
                both = dot(jnp.concatenate(es, axis=1), vz)
                norm = both[:, 128:]
                ctx[rows, pl.ds(pl.multiple_of(part * half + t * 128, 128), 128)] = both[:, :128] / norm
                total = jnp.where(in_head[0], tops[0], tops[1]) + jnp.log(norm)
                found = jnp.where(lane == head, total[:, 0:1], stats[rows, :])
                stats[rows, :] = jnp.where(lane == head + 1, total[:, HD : HD + 1], found)
            return carry

        lax.fori_loop(0, half // 128, pair, 0, unroll=True)

    take(1)
    project(mp)
    pl.semaphore_wait(barrier, len(partners))
    weight_copies = [
        pltpu.make_async_remote_copy(
            src_ref=src, dst_ref=dst, send_sem=wsend.at[i], recv_sem=wrecv.at[i], device_id=core_id, device_id_type=MESH
        )
        for i, (src, dst) in enumerate(((qkvw_h, wqkv.at[mp]), (qvb_v, qvb.at[mp])))
    ]
    for copy in weight_copies:
        copy.start()
    open_["w0"], open_["w1"] = weight_copies
    for copy in local[2:]:
        copy.start()
    row = jnp.sum(jnp.where(lax.broadcasted_iota(jnp.int32, seg_v.shape, 0) == mp, seg_v[...], 0), axis=0, keepdims=True).astype(WIDE)
    fill = fill_s[mp]
    seg_col = jnp.broadcast_to(row, (128, tokens)).T[:, 0:1]
    blk = 128

    for i in range(tokens // blk):
        kpos = lax.broadcasted_iota(jnp.int32, (blk, tokens), 1)
        qpos = lax.broadcasted_iota(jnp.int32, (blk, tokens), 0) + i * blk
        live = (kpos < fill) | (kpos == qpos)
        same = seg_col[i * blk : i * blk + blk] == row
        bias[i * blk : i * blk + blk, :] = jnp.where(same & live, 0.0, -1e30)

    attend(mp)
    take("w0")
    take("w1")
    project(other)
    attend(other)

    take(2)

    def mix_rows(i, peak):
        c = ctx[rows_at(i), :]
        clip_mid[rows_at(i), :] = (r1 * jnp.tanh(c * i1)).astype(LOW)
        return jnp.maximum(peak, jnp.max(jnp.abs(c), axis=0, keepdims=True))

    peak_s[1:2, :] = lax.fori_loop(0, tokens // rb, mix_rows, jnp.zeros((1, width), WIDE), unroll=4)
    interleave(mixed_t, lambda part: clip_mid[:, half * part : half * part + half].astype(WIDE))
    h2[...] = dot(clip_mid[...], wout[...])

    def norm(v):
        center = v - jnp.mean(v, axis=-1, keepdims=True)
        inv = lax.rsqrt(jnp.mean(center * center, axis=-1, keepdims=True) + EPSILON)
        return center * inv, inv

    def norm1_rows(i, peak):
        rows = rows_at(i)
        xhat, inv = norm(tok[rows, :].astype(WIDE) + (h2[rows, :] + vec_s[0:1, :]))
        xhat1[rows, :] = xhat
        stats[rows, :] = jnp.where(lane == 127, inv, stats[rows, :])
        normed = xhat * vec_s[1:2, :] + vec_s[2:3, :]
        h2[rows, :] = normed + vec_s[3:4, :]
        clip_mid[rows, :] = (r2 * jnp.tanh(normed * i2)).astype(LOW)
        return jnp.maximum(peak, jnp.max(jnp.abs(normed), axis=0, keepdims=True))

    peak_s[2:3, :] = lax.fori_loop(0, tokens // rb, norm1_rows, jnp.zeros((1, width), WIDE), unroll=1)
    interleave(clip_mid_t, lambda part: clip_mid[:, half * part : half * part + half].astype(WIDE))

    take(3)
    take(4)
    fb, fr = pre_b.shape[1], 64
    pre_s, act_s = (d_h1.at[:, 0:fb], pre_b), (act_a, act_b)
    n_fb = hidden // fb

    def feed_in(b):
        pre_s[b % 2][...] = dot(clip_mid[...], win[:, fb * b : fb * b + fb])

    def feed_act(b, peak):
        cols = slice(fb * b, fb * b + fb)
        for r in range(0, tokens, fr):
            rows = slice(r, r + fr)
            pre = pre_s[b % 2][rows, :] + inb_v[:, cols]
            cdf = 0.5 + 0.5 * lax.erf(pre * SQRT_HALF)
            act = pre * cdf
            th = jnp.tanh(act * i3)
            act_s[b % 2][rows, :] = (r3 * th).astype(LOW)
            bell = jnp.exp(pre * pre * -0.5) * INV_SQRT_2PI
            slope_f[rows, cols] = ((1.0 - th * th) * (cdf + pre * bell)).astype(LOW)
            peak = jnp.maximum(peak, jnp.max(jnp.abs(act), axis=0, keepdims=True))
        return peak

    def feed_out(b):
        out = act_s[b % 2][...]
        flipped = out.T
        for i in range(fb // 32):
            group = b * (fb // 32) + i
            owner = group // 3
            clip_act_t[owner % 2, group % 3, owner // 2] = flipped[32 * i : 32 * i + 32]
        h2[...] += dot(out, wdown[fb * b : fb * b + fb, :])

    peak3 = jnp.zeros((1, fb), WIDE)
    feed_in(0)
    for b in range(n_fb):
        if b + 1 < n_fb:
            feed_in(b + 1)
        peak3 = feed_act(b, peak3)
        if b > 0:
            feed_out(b - 1)
    feed_out(n_fb - 1)
    peak_s[3:4, :] = jnp.zeros_like(peak_s[3:4, :])
    peak_s[3:4, 0:fb] = peak3

    take(5)
    zero_row = jnp.zeros((1, width), WIDE)

    def norm2_rows(i, sums):
        rows = rows_at(i)
        xhat, inv = norm(h2[rows, :])
        e = cot[rows, :].astype(WIDE)
        clip_in_row = (xhat * vec_s[4:5, :] + vec_s[5:6, :]).astype(LOW)
        clip_mid[rows, :] = clip_in_row
        w = e * vec_s[4:5, :]
        d = inv * (w - jnp.mean(w, axis=-1, keepdims=True) - xhat * jnp.mean(w * xhat, axis=-1, keepdims=True))
        h2[rows, :] = d
        low = d.astype(LOW)
        cot[rows, :] = low
        return (
            sums[0] + jnp.sum(e * xhat, axis=0, keepdims=True),
            sums[1] + jnp.sum(e, axis=0, keepdims=True),
            sums[2] + jnp.sum(low.astype(WIDE), axis=0, keepdims=True),
        )

    gain2, shift2, down_bias = lax.fori_loop(0, tokens // rb, norm2_rows, (zero_row, zero_row, zero_row), unroll=1)
    lay_copy = pltpu.make_async_copy(clip_mid, lay_h, loc_sem.at[6])
    lay_copy.start()

    sm[...] = jnp.zeros_like(sm)
    sm[7:8, :] = down_bias
    sm[8:9, :] = gain2
    sm[9:10, :] = shift2
    lane_w = lax.broadcasted_iota(jnp.int32, (1, width), 1)
    peaks = zero_row
    for i in range(4):
        peaks = jnp.where(lane_w == i, jnp.max(peak_s[i : i + 1, :], axis=-1, keepdims=True), peaks)
    sm[12:13, :] = peaks

    scatter = Scatter(
        n_low,
        {"down": acc_d, "wide": acc_w},
        {"down": cs_d, "wide": cs_w},
        {"down": cr_d, "wide": cr_w},
        {"down": (rd1, rd2, rd3, rd4), "wide": (rw1, rw2, rw3, rw4)},
        msend,
        mrecv,
    )

    leaving = []

    def leave(src, dst):
        leaving.append(pltpu.make_async_copy(src, dst, out_sem.at[len(leaving)]))
        leaving[-1].start()

    def out_down(index):
        def write(total):
            rows = pl.ds(32 * index, 32)
            gdown[rows, :] = total
            leave(gdown.at[rows], gdown_h.at[rows])

        return write

    def out_wide(ref, there, at):
        def write(total):
            both = jnp.concatenate([total[:24], total[24:]], axis=1)
            if ref is gqkv:
                ref[at] = both
                leave(ref.at[at], there.at[at])
            else:
                cols = pl.ds(width * at, width)
                ref[:, cols] = both
                leave(ref.at[:, cols], there.at[:, cols])

        return write

    outs = [out_down(i) for i in range(3)] + [out_wide(gin, gin_h, i) for i in range(4)]
    outs += [out_wide(gout, gout_h, 0)] + [out_wide(gqkv, gqkv_h, i) for i in range(3)]

    def step(m, stage):
        scatter.step(m, stage, outs[m])

    def send_part(group, index, result):
        scatter.slot_free(group, index)
        store_chunks(cs_d if group == "down" else cs_w, index % SLOTS[group], group, index, result)
        scatter.core_copy(group, index).start()

    def own_part(group, index, result):
        store_chunks(acc_d if group == "down" else acc_w, index, group, index, result)

    def down_send(i):
        send_part("down", i, dot(clip_act_t[other, i].reshape(16 * 32, tokens), cot[...]))

    def down_own(i):
        own_part("down", i, dot(clip_act_t[mp, i].reshape(16 * 32, tokens), cot[...]))

    d_pre = clip_mid

    def block(i):
        return pl.ds(pl.multiple_of(i * width, width), width)

    def in_send(i):
        d_pre[...] = (dot_nt(cot[...], wdown[block(i), :]) * slope_f[:, block(i)].astype(WIDE)).astype(LOW)
        send_part("wide", i, dot(clip_mid_t[other], d_pre[...]))

    def in_own(i):
        own_part("wide", i, dot(clip_mid_t[mp], d_pre[...]))
        sm[pl.ds(3 + i, 1), :] = jnp.sum(d_pre[...].astype(WIDE), axis=0, keepdims=True)

    def in_back(i):
        d_h1[...] += dot_nt(d_pre[...], win[:, block(i)])

    def norm1_back(_):
        def some(i, sums):
            rows = rows_at(i)
            xhat = xhat1[rows, :]
            inv = stats[rows, 127:128]
            th = jnp.tanh((xhat * vec_s[1:2, :] + vec_s[2:3, :]) * i2)
            e = h2[rows, :] + d_h1[rows, :] * (1.0 - th * th)
            w = e * vec_s[1:2, :]
            d = inv * (w - jnp.mean(w, axis=-1, keepdims=True) - xhat * jnp.mean(w * xhat, axis=-1, keepdims=True))
            d_h1[rows, :] = d
            low = d.astype(LOW)
            cot[rows, :] = low
            return (
                sums[0] + jnp.sum(e * xhat, axis=0, keepdims=True),
                sums[1] + jnp.sum(e, axis=0, keepdims=True),
                sums[2] + jnp.sum(low.astype(WIDE), axis=0, keepdims=True),
            )

        gain1, shift1, out_bias = lax.fori_loop(0, tokens // rb, some, (zero_row, zero_row, zero_row), unroll=4)
        sm[0:1, :] = out_bias
        sm[1:2, :] = gain1
        sm[2:3, :] = shift1

    def out_send(_):
        send_part("wide", 4, dot(mixed_t[other], cot[...]))

    def out_own(_):
        own_part("wide", 4, dot(mixed_t[mp], cot[...]))

    def mixed_back(_):
        h2[...] = dot_nt(cot[...], wout[...])

    def context_back(_):
        def some(i, carry):
            rows = rows_at(i)
            th = jnp.tanh(ctx[rows, :] * i1)
            clip_mid[rows, :] = (h2[rows, :].astype(LOW).astype(WIDE) * (1.0 - th * th)).astype(LOW)
            return carry

        lax.fori_loop(0, tokens // rb, some, 0, unroll=4)

    def attend_back(part, t):
        at = pl.ds(pl.multiple_of(t * 128, 128), 128)
        wide_at = pl.ds(pl.multiple_of(part * half + t * 128, 128), 128)
        k, v = qkv[1, part, :, at], qkv[2, part, :, at]
        split = lambda v: [jnp.where(m, v, jnp.zeros_like(v)) for m in in_head]
        kz, vz = split(k), split(v)
        d_k, d_v = jnp.zeros((tokens, 128), WIDE), jnp.zeros((tokens, 128), WIDE)
        for i in range(tokens // qb):
            rows = pl.ds(i * qb, qb)
            q = qkv[0, part, rows, at]
            dc = clip_mid[rows, wide_at]
            prod = dc.astype(WIDE) * ctx[rows, wide_at]
            found = stats[rows, :]
            ps, ds = [], []
            for h in range(2):
                mean = jnp.sum(jnp.where(in_head[h], prod, 0.0), axis=-1, keepdims=True)
                total = jnp.sum(jnp.where(lane == (part * 6 + t * 2 + h), found, 0.0), axis=-1, keepdims=True)
                p = jnp.exp(dot_nt(q, kz[h]) + bias[rows, :] - total)
                ds.append((p * (dot_nt(dc, vz[h]) - mean)).astype(LOW))
                ps.append(p.astype(LOW))
            d_q = dot(jnp.concatenate(ds, axis=1), jnp.concatenate(kz, axis=0))
            d_k = d_k + dot_tn(jnp.concatenate(ds, axis=0), jnp.concatenate(split(q), axis=0))
            d_v = d_v + dot_tn(jnp.concatenate(ps, axis=0), jnp.concatenate(split(dc), axis=0))
            qkv[0, part, rows, at] = (d_q * (HD ** -0.5)).astype(LOW)
        qkv[1, part, :, at] = d_k.astype(LOW)
        qkv[2, part, :, at] = d_v.astype(LOW)

    def qkv_send(j):
        send_part("wide", 5 + j, dot_tn(qkv[j, other], clip_in[...]))

    def qkv_own(j):
        own_part("wide", 5 + j, dot_tn(qkv[j, mp], clip_in[...]))

    def head_sums(_):
        for r, j in ((10, 0), (11, 2)):
            for part in range(2):
                sm[r : r + 1, half * part : half * part + half] = jnp.sum(qkv[j, part].astype(WIDE), axis=0, keepdims=True)
        small_copy(0).start()
        h2[...] = jnp.zeros_like(h2)

    def in_tokens(j):
        both = jnp.concatenate([qkv[j, 0], qkv[j, 1]], axis=1)
        h2[...] += dot_nt(both, jnp.concatenate([wqkv[0, j], wqkv[1, j]], axis=1))

    def token_grad(_):
        def some(i, carry):
            rows = rows_at(i)
            th = jnp.tanh(tok[rows, :].astype(WIDE) * i0)
            d_h1[rows, :] += h2[rows, :] * (1.0 - th * th)
            return carry

        lax.fori_loop(0, tokens // rb, some, 0, unroll=4)
        tok_copy.start()

    tok_copy = pltpu.make_async_copy(d_h1, gtok_h, loc_sem.at[7])

    def small_copy(k):
        return pltpu.make_async_remote_copy(
            src_ref=sm,
            dst_ref=sm_r.at[k],
            send_sem=ssend.at[k],
            recv_sem=srecv.at[k],
            device_id=partners[k],
            device_id_type=MESH,
        )

    def small_end(k):
        small_copy(k).wait()
        is_peak = lax.broadcasted_iota(jnp.int32, sm.shape, 0) == 12
        sm[...] = jnp.where(is_peak, jnp.maximum(sm[...], sm_r[k]), sm[...] + sm_r[k])
        if k + 1 < len(partners):
            small_copy(k + 1).start()
        else:
            small_results()

    def small_results():
        per = width // (2 * n_dp)
        me = dp * 2 + mp
        sums = sm[...]
        out = pltpu.roll(sums, (width - per * me) % width, 1)[:, :128]
        qv_out = pltpu.roll(sums, (width - (mp * half + per * dp)) % width, 1)[:, :128]
        wide_at = 4 * per * me
        in_rows = pltpu.roll(sums, (width - wide_at % width) % width, 1)[:, :128]
        r_iota = lax.broadcasted_iota(jnp.int32, out.shape, 0)
        in_row = jnp.sum(jnp.where(r_iota == 3 + wide_at // width, in_rows, 0.0), axis=0, keepdims=True)
        out = jnp.where((r_iota == 10) | (r_iota == 11), qv_out, out)
        out = jnp.where(r_iota == 3, in_row, out)
        small_o[...] = out
        small_o[12:13, 0:4] = MOMENTUM * act_v[...] + (1.0 - MOMENTUM) * sums[12:13, 0:4]

    parts = {
        "Dp": down_send, "Do": down_own, "Ip": in_send, "Io": in_own, "In": in_back, "LN": norm1_back, "Op": out_send, "Oo": out_own,
        "dm": mixed_back, "cx": context_back, "ab": lambda t: attend_back(other, t), "am": lambda t: attend_back(mp, t),
        "Qp": qkv_send, "Qo": qkv_own, "hs": head_sums, "dc": in_tokens, "tk": token_grad, "sm": small_end,
    }
    d_h1[...] = jnp.zeros_like(d_h1)

    def run(which, n):
        if isinstance(which, str):
            parts[which](n)
        else:
            step(which, n)

    def loop(names, count, after):
        def round_(i, carry):
            for name in names:
                parts[name](i)
                for k in range(count):
                    todo = after.get((name, k), ())
                    if todo:
                        pl.when(i == k)(lambda todo=todo: [run(*which) for which in todo] and None)
            return carry

        lax.fori_loop(0, count, round_, 0)

    for entry in SCHEDULE:
        if len(entry) == 3:
            if "Ip" in entry[0]:
                lay_copy.wait()
            loop(entry[0], entry[1], dict(entry[2]))
        else:
            run(*entry)
    for k in range(5, len(partners)):
        small_end(k)
    scatter.finish()

    tok_copy.wait()
    for copy in leaving:
        copy.wait()


def hand_out(per, *refs):
    big, small, outs, held, sem = refs[:6], refs[6], refs[7:22], refs[22:28], refs[28]
    pieces = []
    for i, src in enumerate(big):
        size = src.shape[0] // (4 if i < 2 else 1)
        pieces += [(i, pl.ds(at, size)) for at in range(0, src.shape[0], size)]
    ins = [pltpu.make_async_copy(big[i].at[at], held[i].at[at], sem.at[0, n]) for n, (i, at) in enumerate(pieces)]
    away = [pltpu.make_async_copy(held[i].at[at], outs[i].at[at], sem.at[1, n]) for n, (i, at) in enumerate(pieces)]
    for copy in ins:
        copy.start()
    outs[6][...] = small[10:12, :per]
    for ref, row in zip(outs[7:], (0, 1, 2, 3, 7, 8, 9, 12)):
        ref[...] = small[row, : ref.shape[0]]
    for here, there in zip(ins, away):
        here.wait()
        there.start()
    for copy in away:
        copy.wait()


def per_device(n_dp, tokens, seg_ids, fill_len, qkv_weight, qv_bias, out_weight, out_bias, norm1_gain, norm1_bias, in_weight, in_bias,
               down_weight, down_bias, norm2_gain, norm2_bias, act_range, cotangent):
    n_tok, width = tokens.shape
    hidden = in_weight.shape[1]
    half = width // 2
    n_low = max(1, n_dp // 16)
    any_, vmem = pl.BlockSpec(memory_space=pl.ANY), pl.BlockSpec(memory_space=pltpu.VMEM)
    smem = pl.BlockSpec(memory_space=pltpu.SMEM)
    chunk = width // 32
    shape = jax.ShapeDtypeStruct
    low = lambda *s: pltpu.VMEM(s, LOW)
    wide = lambda *s: pltpu.VMEM(s, WIDE)
    dma = lambda *s: pltpu.SemaphoreType.DMA(s)
    n_partners = n_dp.bit_length()
    n_wide = N_MSG - 3
    outs = pl.pallas_call(
        functools.partial(kernel, n_dp, n_low),
        out_shape=(
            shape((n_tok, width), LOW),
            shape((n_tok, width), WIDE),
            shape((3, chunk, width), WIDE),
            shape((chunk, width), WIDE),
            shape((chunk, hidden), WIDE),
            shape((4 * chunk, width), WIDE),
            shape((16, 128), WIDE),
        ),
        in_specs=[any_, vmem, smem, any_, vmem, any_, vmem, vmem, vmem, any_, vmem, any_, vmem, vmem, vmem, vmem, smem, any_],
        out_specs=(any_, any_, any_, any_, any_, any_, vmem),
        scratch_shapes=[
            low(n_tok, width), low(n_tok, width), low(2, 3, width, half), wide(2, 2, half), low(width, width), low(width, hidden), low(hidden, width),
            low(n_tok, width), low(3, 2, n_tok, half), wide(n_tok, n_tok), wide(n_tok, width), wide(n_tok, 128), low(2, half, n_tok),
            wide(n_tok, width), low(n_tok, width), low(2, half, n_tok), low(2, 3, 16, 32, n_tok), low(n_tok, hidden),
            wide(n_tok, width), wide(n_tok, width), wide(n_tok, 512), low(n_tok, 512), low(n_tok, 512), wide(8, width), wide(8, width), wide(16, width), wide(n_partners, 16, width),
            low(3, 16, 32, width), low(n_wide, 16, 48, half), low(3, 16, 32, width), low(2, 16, 48, half), low(3, 16, 32, width), low(n_wide, 16, 48, half),
            *(low(3, 16 >> k, 32, width) for k in range(1, 5)), *(low(n_wide, 16 >> k, 48, half) for k in range(1, 5)),
            wide(3, chunk, width), wide(chunk, width), wide(chunk, hidden), wide(4 * chunk, width), dma(N_MSG),
            dma(8), dma(2), dma(2), dma(N_MSG, 5, 2), dma(N_MSG, 5, 2), dma(n_partners), dma(n_partners),
        ],
        compiler_params=pltpu.CompilerParams(collective_id=0, has_side_effects=True, vmem_limit_bytes=64 * 2**20 - 2**16),
        cost_estimate=pl.CostEstimate(flops=25_000_000_000, bytes_accessed=24_000_000, transcendentals=12_000_000),
    )(
        tokens, seg_ids, fill_len, jnp.transpose(qkv_weight, (1, 0, 2)), qv_bias, out_weight, out_bias, norm1_gain,
        norm1_bias, in_weight, in_bias.reshape(1, hidden), down_weight, down_bias, norm2_gain,
        norm2_bias, act_range.reshape(1, 4), act_range, cotangent,
    )
    layer_out, grad_tokens, qkv_sum, sum_out, sum_in, sum_down, small = outs
    if n_low > 1:
        groups = [[top * n_low + low_ for low_ in range(n_low)] for top in range(16)]
        moves = [((top * n_low + i) * 2 + core, n_low * (2 * top + core) + i) for top in range(16) for i in range(n_low) for core in range(2)]

        def spread(v, dim):
            return lax.psum_scatter(v, "dp", scatter_dimension=dim, axis_index_groups=groups, tiled=True)

        qkv_sum = spread(qkv_sum, 1)
        sum_out, sum_in, sum_down = (lax.ppermute(spread(v, 0), ("dp", "mp"), moves) for v in (sum_out, sum_in, sum_down))
    per = width // (2 * n_dp)
    rows = (per, per, per, 4 * per, per, per, per)
    vectors = [shape((size,), WIDE) for size in rows]
    big = (layer_out, grad_tokens, qkv_sum, sum_out, sum_in, sum_down)
    done = pl.pallas_call(
        functools.partial(hand_out, per),
        out_shape=(*(shape(v.shape, v.dtype) for v in big), shape((2, per), WIDE), *vectors, shape((4,), WIDE)),
        in_specs=[any_] * len(big) + [vmem],
        out_specs=(*([any_] * len(big)), *([vmem] * 9)),
        scratch_shapes=[*(pltpu.VMEM(v.shape, v.dtype) for v in big), dma(2, len(big) + 6)],
        compiler_params=pltpu.CompilerParams(vmem_limit_bytes=64 * 2**20 - 2**16),
    )(*big, small)
    layer_out, grad_tokens, qkv_sum, sum_out, sum_in, sum_down, sum_qv, out_b, gain1, shift1, in_b, down_b, gain2, shift2, new_range = done
    qkv_sum = jnp.transpose(qkv_sum, (2, 0, 1))
    return (
        layer_out, grad_tokens, qkv_sum, sum_qv, sum_out, out_b, gain1, shift1, sum_in, in_b, sum_down, down_b, gain2, shift2, new_range,
    )


def solution(mesh):
    n_dp = mesh.shape["dp"]
    both, copies = P(("dp", "mp")), P()
    rows = P(("dp", "mp"), None)
    return jax.shard_map(
        functools.partial(per_device, n_dp),
        mesh=mesh,
        in_specs=(
            rows, P("dp", None), P("dp"), P(None, None, "mp"), P(None, "mp"),
            *([copies] * 11), rows,
        ),
        out_specs=(
            rows, rows, P(None, None, ("mp", "dp")), P(None, ("mp", "dp")), rows, both, both, both, rows, both, rows, both, both, both, copies,
        ),
        check_vma=False,
    )
```

```python
import functools
import math

import jax
import jax.numpy as jnp
from jax import lax
from jax.experimental import pallas as pl
from jax.experimental.pallas import tpu as pltpu
from jax.sharding import PartitionSpec as P

HD = 64
EPSILON = 1e-06
MOMENTUM = 0.9
SQRT_HALF = math.sqrt(0.5)
INV_SQRT_2PI = 1.0 / math.sqrt(2.0 * math.pi)
LOW = jnp.bfloat16
WIDE = jnp.float32
MESH = pl.DeviceIdType.MESH

MESSAGES = (
    ("down", 0, (0, 1, 2, 3)),
    ("down", 1, (1, 2, 0, 3)),
    ("down", 2, (2, 0, 1, 3)),
    ("wide", 0, (1, 0, 2, 3)),
    ("wide", 1, (0, 1, 2, 3)),
    ("wide", 2, (1, 2, 0, 3)),
    ("wide", 3, (2, 1, 0, 3)),
    ("wide", 4, (0, 1, 2, 3)),
    ("wide", 5, (0, 2, 1, 3)),
    ("wide", 6, (1, 2, 0, 3)),
    ("wide", 7, (0, 1, 2, 3)),
)
N_MSG = len(MESSAGES)
GROUPS = {"down": 0, "wide": 3}
SLOTS = {"down": 3, "wide": 2}


SCHEDULE = (
    (("Dp",), 3, (
    )),
    (("Do",), 3, (
        (("Do", 0), ((0, 0),)),
        (("Do", 1), ((1, 0),)),
    )),
    (("Ip", "Io", "In"), 4, (
        (("Ip", 0), ((2, 0),)),
        (("In", 0), ((3, 0),)),
        (("Io", 1), ((0, 1),)),
        (("In", 1), ((1, 1), (4, 0))),
        (("Ip", 2), ((2, 1),)),
        (("In", 2), ((5, 0),)),
    )),
    (6, 0), ("LN", 0), (4, 1), (3, 1), ("Op", 0), (1, 2), ("Oo", 0), ("dm", 0), (7, 0), ("cx", 0),
    (("ab",), 3, (
        (("ab", 0), ((2, 2),)),
        (("ab", 1), ((0, 2), (6, 1))),
    )),
    (("Qp",), 3, (
        (("Qp", 0), ((3, 2),)),
    )),
    (("am",), 3, (
        (("am", 0), ((0, 3), (5, 1), (1, 3))),
        (("am", 1), ((3, 3),)),
    )),
    (("Qo",), 3, (
        (("Qo", 0), ((8, 0),)),
        (("Qo", 1), ((9, 0), (7, 1), (4, 2))),
    )),
    (10, 0), (5, 2), ("hs", 0),
    (("dc",), 3, (
        (("dc", 0), (("sm", 0),)),
    )),
    (2, 3), ("tk", 0), (4, 3), (6, 2), (8, 1), ("sm", 1), (8, 2), (9, 1), (10, 1), ("sm", 2), (9, 2), (7, 2), (5, 3), (8, 3), (7, 3),
    (6, 3), (10, 2), ("sm", 3), (9, 3), (10, 3), (0, 4), (1, 4), (3, 4), (2, 4), (4, 4), (5, 4), (8, 4), (7, 4), (6, 4), ("sm", 4),
    (9, 4), (10, 4),
)


def dot(a, b):
    return lax.dot_general(a, b, (((1,), (0,)), ((), ())), preferred_element_type=WIDE)


def dot_nt(a, b):
    return lax.dot_general(a, b, (((1,), (1,)), ((), ())), preferred_element_type=WIDE)


def dot_tn(a, b):
    return lax.dot_general(a, b, (((0,), (0,)), ((), ())), preferred_element_type=WIDE)


def place(chunk, order):
    spot = 0
    for bit in order:
        spot = spot * 2 + (chunk >> bit) % 2
    return spot


class Scatter:
    def __init__(self, n_low, acc, csend, crecv, recvs, send_sem, recv_sem):
        self.acc, self.csend, self.crecv, self.recvs = acc, csend, crecv, recvs
        self.send_sem, self.recv_sem = send_sem, recv_sem
        self.dp, self.mp = lax.axis_index("dp"), lax.axis_index("mp")
        self.n_low = n_low
        self.pending = []
        self.next = dict.fromkeys(range(N_MSG), 0)

    def bit(self, bit):
        return (self.dp // (self.n_low << bit)) % 2

    def partner(self, bit):
        return (self.dp + (self.n_low << bit) * (1 - 2 * self.bit(bit)), self.mp)

    def core_copy(self, group, index):
        m = GROUPS[group] + index
        return pltpu.make_async_remote_copy(
            src_ref=self.csend[group].at[index % SLOTS[group]],
            dst_ref=self.crecv[group].at[index],
            send_sem=self.send_sem.at[m, 0, 0],
            recv_sem=self.recv_sem.at[m, 0, 0],
            device_id=(self.dp, 1 - self.mp),
            device_id_type=MESH,
        )

    def base(self, m, stage):
        order = MESSAGES[m][2]
        spot = 0
        for k in range(stage):
            spot = spot + self.bit(order[k]) * (8 >> k)
        return spot

    def copies(self, m, stage):
        group, index, order = MESSAGES[m]
        count = 16 >> stage
        bit = order[stage - 1]
        start = self.base(m, stage - 1) + (1 - self.bit(bit)) * count
        if stage == 4:
            parts = [(0, 1)]
        else:
            mine = self.bit(order[stage])
            parts = [((1 - mine) * (count // 2), count // 2), (mine * (count // 2), count // 2)]
        return [
            pltpu.make_async_remote_copy(
                src_ref=self.acc[group].at[index, pl.ds(start + first, size)],
                dst_ref=self.recvs[group][stage - 1].at[index, pl.ds(first, size)],
                send_sem=self.send_sem.at[m, stage, n],
                recv_sem=self.recv_sem.at[m, stage, n],
                device_id=self.partner(bit),
                device_id_type=MESH,
            )
            for n, (first, size) in enumerate(parts)
        ]

    def slot_free(self, group, index):
        old = index - SLOTS[group]
        if isinstance(index, int):
            if old >= 0:
                self.core_copy(group, old).wait_send()
        else:
            pl.when(old >= 0)(lambda: self.core_copy(group, old).wait_send())

    def add(self, m, received, from_, start, count):
        group, index, _ = MESSAGES[m]
        acc = self.acc[group]
        here = pl.ds(start, count)
        acc[index, here] = acc[index, here] + received[index, pl.ds(from_, count)]

    def add_half(self, m, stage, keep):
        group, index, order = MESSAGES[m]
        received = self.crecv[group] if stage == 0 else self.recvs[group][stage - 1]
        count = 8 >> stage
        mine = self.bit(order[stage])
        half = mine if keep else 1 - mine
        self.add(m, received, half * count, self.base(m, stage) + half * count, count)

    def step(self, m, stage, out=None):
        group, index, _ = MESSAGES[m]
        assert self.next[m] == stage
        self.next[m] = stage + 1
        if stage == 0:
            self.core_copy(group, index).wait_recv()
        else:
            if stage >= 2:
                self.copies(m, stage - 1)[1].wait_recv()
            self.add_half(m, stage - 1, True)
            self.copies(m, stage)[0].wait_recv()
        if stage == 4:
            total = self.acc[group][index, self.base(m, 4)].astype(WIDE) + self.recvs[group][3][index, 0].astype(WIDE)
            out(total)
            return
        self.add_half(m, stage, False)
        for copy in self.copies(m, stage + 1):
            copy.start()
        self.pending.append((m, stage + 1))

    def finish(self):
        for group, count in (("down", 3), ("wide", N_MSG - 3)):
            for index in range(count - SLOTS[group], count):
                self.core_copy(group, index).wait_send()
        for m, stage in self.pending:
            for copy in self.copies(m, stage):
                copy.wait_send()


def spot_of(group, index, chunk):
    if isinstance(index, int):
        return place(chunk, MESSAGES[GROUPS[group] + index][2])
    spot = 0
    for other, number, order in MESSAGES:
        if other == group:
            spot = jnp.where(index == number, place(chunk, order), spot)
    return spot


def store_chunks(ref, slot, group, index, result):
    for chunk in range(16):
        if group == "down":
            piece = result[32 * chunk : 32 * chunk + 32]
        else:
            rows, half = result[24 * chunk : 24 * chunk + 24], result.shape[1] // 2
            piece = jnp.concatenate([rows[:, :half], rows[:, half:]], axis=0)
        ref[slot, spot_of(group, index, chunk)] = piece.astype(LOW)


def interleave(ref, values):
    for part in range(2):
        flipped = values(part).T
        for core in range(2):
            groups = [flipped[24 * i : 24 * i + 24] for i in range(core, 16, 2)]
            ref[core, 192 * part : 192 * part + 192, :] = jnp.concatenate(groups, axis=0).astype(LOW)


def kernel(
    n_dp, n_low,
    tok_h, seg_v, fill_s, qkvw_h, qvb_v, outw_h, outb_v, g1_v, b1_v, inw_h, inb_v, downw_h, downb_v, g2_v, b2_v, act_v, range_s, cot_h,
    lay_h, gtok_h, gqkv_h, gout_h, gin_h, gdown_h, small_h,
    tok, cot, wqkv, qvb, wout, win, wdown, clip_in, qkv, bias, ctx, stats, mixed_t, xhat1, clip_mid, clip_mid_t, clip_act_t, slope_f, h2, d_h1, pre_b, act_a, act_b, vec_s, peak_s, sm, sm_r,
    acc_d, acc_w, cs_d, cs_w, cr_d, cr_w, rd1, rd2, rd3, rd4, rw1, rw2, rw3, rw4,
    small_o, gqkv, gout, gin, gdown, out_sem, loc_sem, wsend, wrecv, msend, mrecv, ssend, srecv,
):
    dp, mp = lax.axis_index("dp"), lax.axis_index("mp")
    for i, v in enumerate((outb_v, g1_v, b1_v, downb_v, g2_v, b2_v)):
        vec_s[i : i + 1, :] = v[...].reshape(1, -1)
    n_bits = n_dp.bit_length() - 1
    tokens, width = tok.shape
    hidden = win.shape[1]
    half = width // 2
    other = 1 - mp
    core_id = (dp, other)

    local = [
        pltpu.make_async_copy(src, dst, loc_sem.at[i])
        for i, (src, dst) in enumerate(
            ((tok_h, tok), (qkvw_h, wqkv.at[mp]), (outw_h, wout), (inw_h, win), (downw_h, wdown), (cot_h, cot))
        )
    ]
    for copy in local[:2]:
        copy.start()
    open_ = dict(enumerate(local))
    def take(i):
        open_.pop(i).wait()

    def dp_partner(b):
        return (dp + (1 << b) * (1 - 2 * ((dp // (1 << b)) % 2)), mp)

    barrier = pltpu.get_barrier_semaphore()
    partners = [core_id] + [dp_partner(b) for b in reversed(range(2, n_bits))] + [dp_partner(b) for b in range(2)]
    for there in partners:
        pl.semaphore_signal(barrier, inc=1, device_id=there, device_id_type=MESH)

    r0, r1, r2, r3 = (range_s[i] for i in range(4))
    i0, i1, i2, i3 = (1.0 / r for r in (r0, r1, r2, r3))

    qvb[mp] = qvb_v[...]
    take(0)
    rb = 256
    def rows_at(i, size=rb):
        return pl.ds(pl.multiple_of(i * size, size), size)

    def clip_rows(i, peak):
        v = tok[rows_at(i), :].astype(WIDE)
        clip_in[rows_at(i), :] = (r0 * jnp.tanh(v * i0)).astype(LOW)
        return jnp.maximum(peak, jnp.max(jnp.abs(v), axis=0, keepdims=True))

    peak_s[0:1, :] = lax.fori_loop(0, tokens // rb, clip_rows, jnp.zeros((1, width), WIDE), unroll=4)
    stats[...] = jnp.zeros_like(stats)
    lane = lax.broadcasted_iota(jnp.int32, (1, 128), 1)
    in_head = [lane < HD, lane >= HD]
    qb = 256

    def project(part):
        for j in range(3):
            out = dot(clip_in[...], wqkv[part, j])
            if j == 0:
                out = (out + qvb[part, 0:1, :]).astype(LOW).astype(WIDE) * (HD ** -0.5)
            elif j == 2:
                out = out + qvb[part, 1:2, :]
            qkv[j, part] = out.astype(LOW)

    def attend(part):
        def pair(t, carry):
            at = pl.ds(pl.multiple_of(t * 128, 128), 128)
            k, v = qkv[1, part, :, at], qkv[2, part, :, at]
            nil, one = jnp.zeros_like(v), jnp.ones_like(v)
            kz = [jnp.where(m, k, nil) for m in in_head]
            vz = [jnp.concatenate([jnp.where(m, v, nil), jnp.where(m, one, nil)], axis=1) for m in in_head]
            vz = jnp.concatenate(vz, axis=0)
            head = part * 6 + t * 2
            for i in range(tokens // qb):
                rows = pl.ds(i * qb, qb)
                q = qkv[0, part, rows, at]
                es, tops = [], []
                for h in range(2):
                    s = dot_nt(q, kz[h]) + bias[rows, :]
                    tops.append(jnp.max(s, axis=-1, keepdims=True))
                    es.append(jnp.exp(s - tops[h]).astype(LOW))
                both = dot(jnp.concatenate(es, axis=1), vz)
                norm = both[:, 128:]
                ctx[rows, pl.ds(pl.multiple_of(part * half + t * 128, 128), 128)] = both[:, :128] / norm
                total = jnp.where(in_head[0], tops[0], tops[1]) + jnp.log(norm)
                found = jnp.where(lane == head, total[:, 0:1], stats[rows, :])
                stats[rows, :] = jnp.where(lane == head + 1, total[:, HD : HD + 1], found)
            return carry

        lax.fori_loop(0, half // 128, pair, 0, unroll=True)

    take(1)
    project(mp)
    pl.semaphore_wait(barrier, len(partners))
    weight_copies = [
        pltpu.make_async_remote_copy(
            src_ref=src, dst_ref=dst, send_sem=wsend.at[i], recv_sem=wrecv.at[i], device_id=core_id, device_id_type=MESH
        )
        for i, (src, dst) in enumerate(((qkvw_h, wqkv.at[mp]), (qvb_v, qvb.at[mp])))
    ]
    for copy in weight_copies:
        copy.start()
    open_["w0"], open_["w1"] = weight_copies
    for copy in local[2:]:
        copy.start()
    row = jnp.sum(jnp.where(lax.broadcasted_iota(jnp.int32, seg_v.shape, 0) == mp, seg_v[...], 0), axis=0, keepdims=True).astype(WIDE)
    fill = fill_s[mp]
    seg_col = jnp.broadcast_to(row, (128, tokens)).T[:, 0:1]
    blk = 128

    for i in range(tokens // blk):
        kpos = lax.broadcasted_iota(jnp.int32, (blk, tokens), 1)
        qpos = lax.broadcasted_iota(jnp.int32, (blk, tokens), 0) + i * blk
        live = (kpos < fill) | (kpos == qpos)
        same = seg_col[i * blk : i * blk + blk] == row
        bias[i * blk : i * blk + blk, :] = jnp.where(same & live, 0.0, -1e30)

    attend(mp)
    take("w0")
    take("w1")
    project(other)
    attend(other)

    take(2)

    def mix_rows(i, peak):
        c = ctx[rows_at(i), :]
        clip_mid[rows_at(i), :] = (r1 * jnp.tanh(c * i1)).astype(LOW)
        return jnp.maximum(peak, jnp.max(jnp.abs(c), axis=0, keepdims=True))

    peak_s[1:2, :] = lax.fori_loop(0, tokens // rb, mix_rows, jnp.zeros((1, width), WIDE), unroll=4)
    interleave(mixed_t, lambda part: clip_mid[:, half * part : half * part + half].astype(WIDE))
    h2[...] = dot(clip_mid[...], wout[...])

    def norm(v):
        center = v - jnp.mean(v, axis=-1, keepdims=True)
        inv = lax.rsqrt(jnp.mean(center * center, axis=-1, keepdims=True) + EPSILON)
        return center * inv, inv

    def norm1_rows(i, peak):
        rows = rows_at(i)
        xhat, inv = norm(tok[rows, :].astype(WIDE) + (h2[rows, :] + vec_s[0:1, :]))
        xhat1[rows, :] = xhat
        stats[rows, :] = jnp.where(lane == 127, inv, stats[rows, :])
        normed = xhat * vec_s[1:2, :] + vec_s[2:3, :]
        h2[rows, :] = normed + vec_s[3:4, :]
        clip_mid[rows, :] = (r2 * jnp.tanh(normed * i2)).astype(LOW)
        return jnp.maximum(peak, jnp.max(jnp.abs(normed), axis=0, keepdims=True))

    peak_s[2:3, :] = lax.fori_loop(0, tokens // rb, norm1_rows, jnp.zeros((1, width), WIDE), unroll=1)
    interleave(clip_mid_t, lambda part: clip_mid[:, half * part : half * part + half].astype(WIDE))

    take(3)
    take(4)
    fb, fr = pre_b.shape[1], 64
    pre_s, act_s = (d_h1.at[:, 0:fb], pre_b), (act_a, act_b)
    n_fb = hidden // fb

    def feed_in(b):
        pre_s[b % 2][...] = dot(clip_mid[...], win[:, fb * b : fb * b + fb])

    def feed_act(b, peak):
        cols = slice(fb * b, fb * b + fb)
        for r in range(0, tokens, fr):
            rows = slice(r, r + fr)
            pre = pre_s[b % 2][rows, :] + inb_v[:, cols]
            cdf = 0.5 + 0.5 * lax.erf(pre * SQRT_HALF)
            act = pre * cdf
            th = jnp.tanh(act * i3)
            act_s[b % 2][rows, :] = (r3 * th).astype(LOW)
            bell = jnp.exp(pre * pre * -0.5) * INV_SQRT_2PI
            slope_f[rows, cols] = ((1.0 - th * th) * (cdf + pre * bell)).astype(LOW)
            peak = jnp.maximum(peak, jnp.max(jnp.abs(act), axis=0, keepdims=True))
        return peak

    def feed_out(b):
        out = act_s[b % 2][...]
        flipped = out.T
        for i in range(fb // 32):
            group = b * (fb // 32) + i
            owner = group // 3
            clip_act_t[owner % 2, group % 3, owner // 2] = flipped[32 * i : 32 * i + 32]
        h2[...] += dot(out, wdown[fb * b : fb * b + fb, :])

    peak3 = jnp.zeros((1, fb), WIDE)
    feed_in(0)
    for b in range(n_fb):
        if b + 1 < n_fb:
            feed_in(b + 1)
        peak3 = feed_act(b, peak3)
        if b > 0:
            feed_out(b - 1)
    feed_out(n_fb - 1)
    peak_s[3:4, :] = jnp.zeros_like(peak_s[3:4, :])
    peak_s[3:4, 0:fb] = peak3

    take(5)
    zero_row = jnp.zeros((1, width), WIDE)

    def norm2_rows(i, sums):
        rows = rows_at(i)
        xhat, inv = norm(h2[rows, :])
        e = cot[rows, :].astype(WIDE)
        clip_in_row = (xhat * vec_s[4:5, :] + vec_s[5:6, :]).astype(LOW)
        clip_mid[rows, :] = clip_in_row
        w = e * vec_s[4:5, :]
        d = inv * (w - jnp.mean(w, axis=-1, keepdims=True) - xhat * jnp.mean(w * xhat, axis=-1, keepdims=True))
        h2[rows, :] = d
        low = d.astype(LOW)
        cot[rows, :] = low
        return (
            sums[0] + jnp.sum(e * xhat, axis=0, keepdims=True),
            sums[1] + jnp.sum(e, axis=0, keepdims=True),
            sums[2] + jnp.sum(low.astype(WIDE), axis=0, keepdims=True),
        )

    gain2, shift2, down_bias = lax.fori_loop(0, tokens // rb, norm2_rows, (zero_row, zero_row, zero_row), unroll=1)
    lay_copy = pltpu.make_async_copy(clip_mid, lay_h, loc_sem.at[6])
    lay_copy.start()

    sm[...] = jnp.zeros_like(sm)
    sm[7:8, :] = down_bias
    sm[8:9, :] = gain2
    sm[9:10, :] = shift2
    lane_w = lax.broadcasted_iota(jnp.int32, (1, width), 1)
    peaks = zero_row
    for i in range(4):
        peaks = jnp.where(lane_w == i, jnp.max(peak_s[i : i + 1, :], axis=-1, keepdims=True), peaks)
    sm[12:13, :] = peaks

    scatter = Scatter(
        n_low,
        {"down": acc_d, "wide": acc_w},
        {"down": cs_d, "wide": cs_w},
        {"down": cr_d, "wide": cr_w},
        {"down": (rd1, rd2, rd3, rd4), "wide": (rw1, rw2, rw3, rw4)},
        msend,
        mrecv,
    )

    leaving = []

    def leave(src, dst):
        leaving.append(pltpu.make_async_copy(src, dst, out_sem.at[len(leaving)]))
        leaving[-1].start()

    def out_down(index):
        def write(total):
            rows = pl.ds(32 * index, 32)
            gdown[rows, :] = total
            leave(gdown.at[rows], gdown_h.at[rows])

        return write

    def out_wide(ref, there, at):
        def write(total):
            both = jnp.concatenate([total[:24], total[24:]], axis=1)
            if ref is gqkv:
                ref[at] = both
                leave(ref.at[at], there.at[at])
            else:
                cols = pl.ds(width * at, width)
                ref[:, cols] = both
                leave(ref.at[:, cols], there.at[:, cols])

        return write

    outs = [out_down(i) for i in range(3)] + [out_wide(gin, gin_h, i) for i in range(4)]
    outs += [out_wide(gout, gout_h, 0)] + [out_wide(gqkv, gqkv_h, i) for i in range(3)]

    def step(m, stage):
        scatter.step(m, stage, outs[m])

    def send_part(group, index, result):
        scatter.slot_free(group, index)
        store_chunks(cs_d if group == "down" else cs_w, index % SLOTS[group], group, index, result)
        scatter.core_copy(group, index).start()

    def own_part(group, index, result):
        store_chunks(acc_d if group == "down" else acc_w, index, group, index, result)

    def down_send(i):
        send_part("down", i, dot(clip_act_t[other, i].reshape(16 * 32, tokens), cot[...]))

    def down_own(i):
        own_part("down", i, dot(clip_act_t[mp, i].reshape(16 * 32, tokens), cot[...]))

    d_pre = clip_mid

    def block(i):
        return pl.ds(pl.multiple_of(i * width, width), width)

    def in_send(i):
        d_pre[...] = (dot_nt(cot[...], wdown[block(i), :]) * slope_f[:, block(i)].astype(WIDE)).astype(LOW)
        send_part("wide", i, dot(clip_mid_t[other], d_pre[...]))

    def in_own(i):
        own_part("wide", i, dot(clip_mid_t[mp], d_pre[...]))
        sm[pl.ds(3 + i, 1), :] = jnp.sum(d_pre[...].astype(WIDE), axis=0, keepdims=True)

    def in_back(i):
        d_h1[...] += dot_nt(d_pre[...], win[:, block(i)])

    def norm1_back(_):
        def some(i, sums):
            rows = rows_at(i)
            xhat = xhat1[rows, :]
            inv = stats[rows, 127:128]
            th = jnp.tanh((xhat * vec_s[1:2, :] + vec_s[2:3, :]) * i2)
            e = h2[rows, :] + d_h1[rows, :] * (1.0 - th * th)
            w = e * vec_s[1:2, :]
            d = inv * (w - jnp.mean(w, axis=-1, keepdims=True) - xhat * jnp.mean(w * xhat, axis=-1, keepdims=True))
            d_h1[rows, :] = d
            low = d.astype(LOW)
            cot[rows, :] = low
            return (
                sums[0] + jnp.sum(e * xhat, axis=0, keepdims=True),
                sums[1] + jnp.sum(e, axis=0, keepdims=True),
                sums[2] + jnp.sum(low.astype(WIDE), axis=0, keepdims=True),
            )

        gain1, shift1, out_bias = lax.fori_loop(0, tokens // rb, some, (zero_row, zero_row, zero_row), unroll=4)
        sm[0:1, :] = out_bias
        sm[1:2, :] = gain1
        sm[2:3, :] = shift1

    def out_send(_):
        send_part("wide", 4, dot(mixed_t[other], cot[...]))

    def out_own(_):
        own_part("wide", 4, dot(mixed_t[mp], cot[...]))

    def mixed_back(_):
        h2[...] = dot_nt(cot[...], wout[...])

    def context_back(_):
        def some(i, carry):
            rows = rows_at(i)
            th = jnp.tanh(ctx[rows, :] * i1)
            clip_mid[rows, :] = (h2[rows, :].astype(LOW).astype(WIDE) * (1.0 - th * th)).astype(LOW)
            return carry

        lax.fori_loop(0, tokens // rb, some, 0, unroll=4)

    def attend_back(part, t):
        at = pl.ds(pl.multiple_of(t * 128, 128), 128)
        wide_at = pl.ds(pl.multiple_of(part * half + t * 128, 128), 128)
        k, v = qkv[1, part, :, at], qkv[2, part, :, at]
        split = lambda v: [jnp.where(m, v, jnp.zeros_like(v)) for m in in_head]
        kz, vz = split(k), split(v)
        d_k, d_v = jnp.zeros((tokens, 128), WIDE), jnp.zeros((tokens, 128), WIDE)
        for i in range(tokens // qb):
            rows = pl.ds(i * qb, qb)
            q = qkv[0, part, rows, at]
            dc = clip_mid[rows, wide_at]
            prod = dc.astype(WIDE) * ctx[rows, wide_at]
            found = stats[rows, :]
            ps, ds = [], []
            for h in range(2):
                mean = jnp.sum(jnp.where(in_head[h], prod, 0.0), axis=-1, keepdims=True)
                total = jnp.sum(jnp.where(lane == (part * 6 + t * 2 + h), found, 0.0), axis=-1, keepdims=True)
                p = jnp.exp(dot_nt(q, kz[h]) + bias[rows, :] - total)
                ds.append((p * (dot_nt(dc, vz[h]) - mean)).astype(LOW))
                ps.append(p.astype(LOW))
            d_q = dot(jnp.concatenate(ds, axis=1), jnp.concatenate(kz, axis=0))
            d_k = d_k + dot_tn(jnp.concatenate(ds, axis=0), jnp.concatenate(split(q), axis=0))
            d_v = d_v + dot_tn(jnp.concatenate(ps, axis=0), jnp.concatenate(split(dc), axis=0))
            qkv[0, part, rows, at] = (d_q * (HD ** -0.5)).astype(LOW)
        qkv[1, part, :, at] = d_k.astype(LOW)
        qkv[2, part, :, at] = d_v.astype(LOW)

    def qkv_send(j):
        send_part("wide", 5 + j, dot_tn(qkv[j, other], clip_in[...]))

    def qkv_own(j):
        own_part("wide", 5 + j, dot_tn(qkv[j, mp], clip_in[...]))

    def head_sums(_):
        for r, j in ((10, 0), (11, 2)):
            for part in range(2):
                sm[r : r + 1, half * part : half * part + half] = jnp.sum(qkv[j, part].astype(WIDE), axis=0, keepdims=True)
        small_copy(0).start()
        h2[...] = jnp.zeros_like(h2)

    def in_tokens(j):
        both = jnp.concatenate([qkv[j, 0], qkv[j, 1]], axis=1)
        h2[...] += dot_nt(both, jnp.concatenate([wqkv[0, j], wqkv[1, j]], axis=1))

    def token_grad(_):
        def some(i, carry):
            rows = rows_at(i)
            th = jnp.tanh(tok[rows, :].astype(WIDE) * i0)
            d_h1[rows, :] += h2[rows, :] * (1.0 - th * th)
            return carry

        lax.fori_loop(0, tokens // rb, some, 0, unroll=4)
        tok_copy.start()

    tok_copy = pltpu.make_async_copy(d_h1, gtok_h, loc_sem.at[7])

    def small_copy(k):
        return pltpu.make_async_remote_copy(
            src_ref=sm,
            dst_ref=sm_r.at[k],
            send_sem=ssend.at[k],
            recv_sem=srecv.at[k],
            device_id=partners[k],
            device_id_type=MESH,
        )

    def small_end(k):
        small_copy(k).wait()
        is_peak = lax.broadcasted_iota(jnp.int32, sm.shape, 0) == 12
        sm[...] = jnp.where(is_peak, jnp.maximum(sm[...], sm_r[k]), sm[...] + sm_r[k])
        if k + 1 < len(partners):
            small_copy(k + 1).start()
        else:
            small_results()

    def small_results():
        per = width // (2 * n_dp)
        me = dp * 2 + mp
        sums = sm[...]
        out = pltpu.roll(sums, (width - per * me) % width, 1)[:, :128]
        qv_out = pltpu.roll(sums, (width - (mp * half + per * dp)) % width, 1)[:, :128]
        wide_at = 4 * per * me
        in_rows = pltpu.roll(sums, (width - wide_at % width) % width, 1)[:, :128]
        r_iota = lax.broadcasted_iota(jnp.int32, out.shape, 0)
        in_row = jnp.sum(jnp.where(r_iota == 3 + wide_at // width, in_rows, 0.0), axis=0, keepdims=True)
        out = jnp.where((r_iota == 10) | (r_iota == 11), qv_out, out)
        out = jnp.where(r_iota == 3, in_row, out)
        small_o[...] = out
        small_o[12:13, 0:4] = MOMENTUM * act_v[...] + (1.0 - MOMENTUM) * sums[12:13, 0:4]
        leave(small_o, small_h)

    parts = {
        "Dp": down_send, "Do": down_own, "Ip": in_send, "Io": in_own, "In": in_back, "LN": norm1_back, "Op": out_send, "Oo": out_own,
        "dm": mixed_back, "cx": context_back, "ab": lambda t: attend_back(other, t), "am": lambda t: attend_back(mp, t),
        "Qp": qkv_send, "Qo": qkv_own, "hs": head_sums, "dc": in_tokens, "tk": token_grad, "sm": small_end,
    }
    d_h1[...] = jnp.zeros_like(d_h1)

    def run(which, n):
        if isinstance(which, str):
            parts[which](n)
        else:
            step(which, n)

    def loop(names, count, after):
        def round_(i, carry):
            for name in names:
                parts[name](i)
                for k in range(count):
                    todo = after.get((name, k), ())
                    if todo:
                        pl.when(i == k)(lambda todo=todo: [run(*which) for which in todo] and None)
            return carry

        lax.fori_loop(0, count, round_, 0)

    for entry in SCHEDULE:
        if len(entry) == 3:
            if "Ip" in entry[0]:
                lay_copy.wait()
            loop(entry[0], entry[1], dict(entry[2]))
        else:
            run(*entry)
    for k in range(5, len(partners)):
        small_end(k)
    scatter.finish()

    tok_copy.wait()
    for copy in leaving:
        copy.wait()


def hand_out(per, *refs):
    big, small_h, outs, held, short, small, sem = refs[:6], refs[6], refs[7:22], refs[22:28], refs[28:37], refs[37], refs[38]
    pieces = []
    for i, src in enumerate(big):
        size = src.shape[0] // (4 if i < 2 else 1)
        pieces += [(i, pl.ds(at, size)) for at in range(0, src.shape[0], size)]
    ins = [pltpu.make_async_copy(big[i].at[at], held[i].at[at], sem.at[0, n]) for n, (i, at) in enumerate(pieces)]
    away = [pltpu.make_async_copy(held[i].at[at], outs[i].at[at], sem.at[1, n]) for n, (i, at) in enumerate(pieces)]
    last = len(pieces)
    first = pltpu.make_async_copy(small_h, small, sem.at[0, last])
    first.start()
    for copy in ins:
        copy.start()
    away += [pltpu.make_async_copy(src, dst, sem.at[1, last + n]) for n, (src, dst) in enumerate(zip(short, outs[6:]))]
    first.wait()
    short[0][...] = small[10:12, :per]
    for ref, row in zip(short[1:], (0, 1, 2, 3, 7, 8, 9, 12)):
        ref[...] = small[row, : ref.shape[0]]
    for copy in away[last:]:
        copy.start()
    for here, there in zip(ins, away):
        here.wait()
        there.start()
    for copy in away:
        copy.wait()


def per_device(n_dp, tokens, seg_ids, fill_len, qkv_weight, qv_bias, out_weight, out_bias, norm1_gain, norm1_bias, in_weight, in_bias,
               down_weight, down_bias, norm2_gain, norm2_bias, act_range, cotangent):
    n_tok, width = tokens.shape
    hidden = in_weight.shape[1]
    half = width // 2
    n_low = max(1, n_dp // 16)
    any_, vmem = pl.BlockSpec(memory_space=pl.ANY), pl.BlockSpec(memory_space=pltpu.VMEM)
    smem = pl.BlockSpec(memory_space=pltpu.SMEM)
    chunk = width // 32
    shape = jax.ShapeDtypeStruct
    low = lambda *s: pltpu.VMEM(s, LOW)
    wide = lambda *s: pltpu.VMEM(s, WIDE)
    dma = lambda *s: pltpu.SemaphoreType.DMA(s)
    n_partners = n_dp.bit_length()
    n_wide = N_MSG - 3
    outs = pl.pallas_call(
        functools.partial(kernel, n_dp, n_low),
        out_shape=(
            shape((n_tok, width), LOW),
            shape((n_tok, width), WIDE),
            shape((3, chunk, width), WIDE),
            shape((chunk, width), WIDE),
            shape((chunk, hidden), WIDE),
            shape((4 * chunk, width), WIDE),
            shape((16, 128), WIDE),
        ),
        in_specs=[any_, vmem, smem, any_, vmem, any_, vmem, vmem, vmem, any_, vmem, any_, vmem, vmem, vmem, vmem, smem, any_],
        out_specs=(any_,) * 7,
        scratch_shapes=[
            low(n_tok, width), low(n_tok, width), low(2, 3, width, half), wide(2, 2, half), low(width, width), low(width, hidden), low(hidden, width),
            low(n_tok, width), low(3, 2, n_tok, half), wide(n_tok, n_tok), wide(n_tok, width), wide(n_tok, 128), low(2, half, n_tok),
            wide(n_tok, width), low(n_tok, width), low(2, half, n_tok), low(2, 3, 16, 32, n_tok), low(n_tok, hidden),
            wide(n_tok, width), wide(n_tok, width), wide(n_tok, 512), low(n_tok, 512), low(n_tok, 512), wide(8, width), wide(8, width), wide(16, width), wide(n_partners, 16, width),
            low(3, 16, 32, width), low(n_wide, 16, 48, half), low(3, 16, 32, width), low(2, 16, 48, half), low(3, 16, 32, width), low(n_wide, 16, 48, half),
            *(low(3, 16 >> k, 32, width) for k in range(1, 5)), *(low(n_wide, 16 >> k, 48, half) for k in range(1, 5)),
            wide(16, 128), wide(3, chunk, width), wide(chunk, width), wide(chunk, hidden), wide(4 * chunk, width), dma(N_MSG + 1),
            dma(8), dma(2), dma(2), dma(N_MSG, 5, 2), dma(N_MSG, 5, 2), dma(n_partners), dma(n_partners),
        ],
        compiler_params=pltpu.CompilerParams(collective_id=0, has_side_effects=True, vmem_limit_bytes=64 * 2**20 - 2**16),
        cost_estimate=pl.CostEstimate(flops=25_000_000_000, bytes_accessed=24_000_000, transcendentals=12_000_000),
    )(
        tokens, seg_ids, fill_len, jnp.transpose(qkv_weight, (1, 0, 2)), qv_bias, out_weight, out_bias, norm1_gain,
        norm1_bias, in_weight, in_bias.reshape(1, hidden), down_weight, down_bias, norm2_gain,
        norm2_bias, act_range.reshape(1, 4), act_range, cotangent,
    )
    layer_out, grad_tokens, qkv_sum, sum_out, sum_in, sum_down, small = outs
    if n_low > 1:
        groups = [[top * n_low + low_ for low_ in range(n_low)] for top in range(16)]
        moves = [((top * n_low + i) * 2 + core, n_low * (2 * top + core) + i) for top in range(16) for i in range(n_low) for core in range(2)]

        def spread(v, dim):
            return lax.psum_scatter(v, "dp", scatter_dimension=dim, axis_index_groups=groups, tiled=True)

        qkv_sum = spread(qkv_sum, 1)
        sum_out, sum_in, sum_down = (lax.ppermute(spread(v, 0), ("dp", "mp"), moves) for v in (sum_out, sum_in, sum_down))
    per = width // (2 * n_dp)
    rows = (per, per, per, 4 * per, per, per, per)
    vectors = [shape((size,), WIDE) for size in rows]
    big = (layer_out, grad_tokens, qkv_sum, sum_out, sum_in, sum_down)
    done = pl.pallas_call(
        functools.partial(hand_out, per),
        out_shape=(*(shape(v.shape, v.dtype) for v in big), shape((2, per), WIDE), *vectors, shape((4,), WIDE)),
        in_specs=[any_] * (len(big) + 1),
        out_specs=(any_,) * (len(big) + 9),
        scratch_shapes=[
            *(pltpu.VMEM(v.shape, v.dtype) for v in (*big, shape((2, per), WIDE), *vectors, shape((4,), WIDE), small)),
            dma(2, len(big) + 15),
        ],
        compiler_params=pltpu.CompilerParams(vmem_limit_bytes=64 * 2**20 - 2**16),
    )(*big, small)
    layer_out, grad_tokens, qkv_sum, sum_out, sum_in, sum_down, sum_qv, out_b, gain1, shift1, in_b, down_b, gain2, shift2, new_range = done
    qkv_sum = jnp.transpose(qkv_sum, (2, 0, 1))
    return (
        layer_out, grad_tokens, qkv_sum, sum_qv, sum_out, out_b, gain1, shift1, sum_in, in_b, sum_down, down_b, gain2, shift2, new_range,
    )


def solution(mesh):
    n_dp = mesh.shape["dp"]
    both, copies = P(("dp", "mp")), P()
    rows = P(("dp", "mp"), None)
    return jax.shard_map(
        functools.partial(per_device, n_dp),
        mesh=mesh,
        in_specs=(
            rows, P("dp", None), P("dp"), P(None, None, "mp"), P(None, "mp"),
            *([copies] * 11), rows,
        ),
        out_specs=(
            rows, rows, P(None, None, ("mp", "dp")), P(None, ("mp", "dp")), rows, both, both, both, rows, both, rows, both, both, both, copies,
        ),
        check_vma=False,
    )
```

```python
import functools
import math

import jax
import jax.numpy as jnp
from jax import lax
from jax.experimental import pallas as pl
from jax.experimental.pallas import tpu as pltpu
from jax.sharding import PartitionSpec as P

HD = 64
EPSILON = 1e-06
MOMENTUM = 0.9
SQRT_HALF = math.sqrt(0.5)
INV_SQRT_2PI = 1.0 / math.sqrt(2.0 * math.pi)
LOW = jnp.bfloat16
WIDE = jnp.float32
MESH = pl.DeviceIdType.MESH

MESSAGES = (
    ("down", 0, (2, 0, 1, 3)),
    ("down", 1, (0, 2, 1, 3)),
    ("down", 2, (1, 2, 0, 3)),
    ("wide", 0, (0, 1, 2, 3)),
    ("wide", 1, (1, 2, 0, 3)),
    ("wide", 2, (1, 0, 2, 3)),
    ("wide", 3, (1, 0, 2, 3)),
    ("wide", 4, (2, 0, 1, 3)),
    ("wide", 5, (0, 1, 2, 3)),
    ("wide", 6, (2, 0, 1, 3)),
    ("wide", 7, (0, 1, 2, 3)),
)
N_MSG = len(MESSAGES)
GROUPS = {"down": 0, "wide": 3}
SLOTS = {"down": 3, "wide": 2}


SCHEDULE = (
    (("Dp",), 3, (
    )),
    (("Do",), 3, (
        (("Do", 0), ((0, 0),)),
        (("Do", 1), ((1, 0),)),
    )),
    (("Ip", "Io", "In"), 4, (
        (("Ip", 0), ((2, 0),)),
        (("In", 0), ((3, 0),)),
        (("Io", 1), ((0, 1),)),
        (("In", 1), ((1, 1), (4, 0))),
        (("Io", 2), ((2, 1),)),
        (("In", 2), ((5, 0),)),
    )),
    (1, 2), (6, 0), ("LN", 0), (3, 1), ("Op", 0), ("Oo", 0), ("dm", 0), (4, 1), (7, 0), (2, 2), ("cx", 0),
    (("ab",), 3, (
        (("ab", 1), ((0, 2), (4, 2))),
    )),
    (("Qp",), 3, (
        (("Qp", 1), ((5, 1), (2, 3))),
    )),
    (("am",), 3, (
        (("am", 0), ((4, 3), (7, 1))),
        (("am", 1), ((1, 3),)),
    )),
    (5, 2),
    (("Qo",), 3, (
        (("Qo", 0), ((8, 0),)),
        (("Qo", 1), ((9, 0),)),
    )),
    (10, 0), (7, 2), ("hs", 0),
    (("dc",), 3, (
        (("dc", 0), ((6, 1), ("sm", 0))),
    )),
    (5, 3), ("tk", 0), (8, 1), (3, 2), (9, 1), (0, 3), (7, 3), (10, 1), ("sm", 1), (3, 3), (8, 2), ("sm", 2), (10, 2), (6, 2), (8, 3),
    (10, 3), (9, 2), (6, 3), (9, 3), ("sm", 3), (2, 4), (4, 4), (1, 4), (5, 4), (0, 4), (7, 4), (3, 4), ("sm", 4), (8, 4), (10, 4),
    (6, 4), (9, 4),
)


def dot(a, b):
    return lax.dot_general(a, b, (((1,), (0,)), ((), ())), preferred_element_type=WIDE)


def dot_nt(a, b):
    return lax.dot_general(a, b, (((1,), (1,)), ((), ())), preferred_element_type=WIDE)


def dot_tn(a, b):
    return lax.dot_general(a, b, (((0,), (0,)), ((), ())), preferred_element_type=WIDE)


def place(chunk, order):
    spot = 0
    for bit in order:
        spot = spot * 2 + (chunk >> bit) % 2
    return spot


class Scatter:
    def __init__(self, n_low, acc, csend, crecv, recvs, send_sem, recv_sem):
        self.acc, self.csend, self.crecv, self.recvs = acc, csend, crecv, recvs
        self.send_sem, self.recv_sem = send_sem, recv_sem
        self.dp, self.mp = lax.axis_index("dp"), lax.axis_index("mp")
        self.n_low = n_low
        self.pending = []
        self.next = dict.fromkeys(range(N_MSG), 0)

    def bit(self, bit):
        return (self.dp // (self.n_low << bit)) % 2

    def partner(self, bit):
        return (self.dp + (self.n_low << bit) * (1 - 2 * self.bit(bit)), self.mp)

    def core_copy(self, group, index):
        m = GROUPS[group] + index
        return pltpu.make_async_remote_copy(
            src_ref=self.csend[group].at[index % SLOTS[group]],
            dst_ref=self.crecv[group].at[index],
            send_sem=self.send_sem.at[m, 0, 0],
            recv_sem=self.recv_sem.at[m, 0, 0],
            device_id=(self.dp, 1 - self.mp),
            device_id_type=MESH,
        )

    def base(self, m, stage):
        order = MESSAGES[m][2]
        spot = 0
        for k in range(stage):
            spot = spot + self.bit(order[k]) * (8 >> k)
        return spot

    def copies(self, m, stage):
        group, index, order = MESSAGES[m]
        count = 16 >> stage
        bit = order[stage - 1]
        start = self.base(m, stage - 1) + (1 - self.bit(bit)) * count
        if stage == 4:
            parts = [(0, 1)]
        else:
            mine = self.bit(order[stage])
            parts = [((1 - mine) * (count // 2), count // 2), (mine * (count // 2), count // 2)]
        return [
            pltpu.make_async_remote_copy(
                src_ref=self.acc[group].at[index, pl.ds(start + first, size)],
                dst_ref=self.recvs[group][stage - 1].at[index, pl.ds(first, size)],
                send_sem=self.send_sem.at[m, stage, n],
                recv_sem=self.recv_sem.at[m, stage, n],
                device_id=self.partner(bit),
                device_id_type=MESH,
            )
            for n, (first, size) in enumerate(parts)
        ]

    def slot_free(self, group, index):
        old = index - SLOTS[group]
        if isinstance(index, int):
            if old >= 0:
                self.core_copy(group, old).wait_send()
        else:
            pl.when(old >= 0)(lambda: self.core_copy(group, old).wait_send())

    def add(self, m, received, from_, start, count):
        group, index, _ = MESSAGES[m]
        acc = self.acc[group]
        here = pl.ds(start, count)
        acc[index, here] = acc[index, here] + received[index, pl.ds(from_, count)]

    def add_half(self, m, stage, keep):
        group, index, order = MESSAGES[m]
        received = self.crecv[group] if stage == 0 else self.recvs[group][stage - 1]
        count = 8 >> stage
        mine = self.bit(order[stage])
        half = mine if keep else 1 - mine
        self.add(m, received, half * count, self.base(m, stage) + half * count, count)

    def step(self, m, stage, out=None):
        group, index, _ = MESSAGES[m]
        assert self.next[m] == stage
        self.next[m] = stage + 1
        if stage == 0:
            self.core_copy(group, index).wait_recv()
        else:
            if stage >= 2:
                self.copies(m, stage - 1)[1].wait_recv()
            self.add_half(m, stage - 1, True)
            self.copies(m, stage)[0].wait_recv()
        if stage == 4:
            total = self.acc[group][index, self.base(m, 4)].astype(WIDE) + self.recvs[group][3][index, 0].astype(WIDE)
            out(total)
            return
        self.add_half(m, stage, False)
        for copy in self.copies(m, stage + 1):
            copy.start()
        self.pending.append((m, stage + 1))

    def finish(self):
        for group, count in (("down", 3), ("wide", N_MSG - 3)):
            for index in range(count - SLOTS[group], count):
                self.core_copy(group, index).wait_send()
        for m, stage in self.pending:
            for copy in self.copies(m, stage):
                copy.wait_send()


def spot_of(group, index, chunk):
    if isinstance(index, int):
        return place(chunk, MESSAGES[GROUPS[group] + index][2])
    spot = 0
    for other, number, order in MESSAGES:
        if other == group:
            spot = jnp.where(index == number, place(chunk, order), spot)
    return spot


def store_chunks(ref, slot, group, index, result):
    for chunk in range(16):
        if group == "down":
            piece = result[32 * chunk : 32 * chunk + 32]
        else:
            rows, half = result[24 * chunk : 24 * chunk + 24], result.shape[1] // 2
            piece = jnp.concatenate([rows[:, :half], rows[:, half:]], axis=0)
        ref[slot, spot_of(group, index, chunk)] = piece.astype(LOW)


def interleave(ref, values):
    for part in range(2):
        flipped = values(part).T
        for core in range(2):
            groups = [flipped[24 * i : 24 * i + 24] for i in range(core, 16, 2)]
            ref[core, 192 * part : 192 * part + 192, :] = jnp.concatenate(groups, axis=0).astype(LOW)


def kernel(
    n_dp, n_low,
    tok_h, seg_v, fill_s, qkvw_h, qvb_v, outw_h, outb_v, g1_v, b1_v, inw_h, inb_v, downw_h, downb_v, g2_v, b2_v, act_v, range_s, cot_h,
    lay_h, gtok_h, gqkv_h, gout_h, gin_h, gdown_h, small_h,
    tok, cot, wqkv, qvb, wout, win, wdown, clip_in, qkv, bias, ctx, stats, mixed_t, xhat1, clip_mid, clip_mid_t, clip_act_t, slope_f, h2, d_h1, pre_b, act_a, act_b, vec_s, peak_s, sm, sm_r,
    acc_d, acc_w, cs_d, cs_w, cr_d, cr_w, rd1, rd2, rd3, rd4, rw1, rw2, rw3, rw4,
    small_o, gqkv, gout, gin, gdown, out_sem, loc_sem, wsend, wrecv, msend, mrecv, ssend, srecv,
):
    dp, mp = lax.axis_index("dp"), lax.axis_index("mp")
    for i, v in enumerate((outb_v, g1_v, b1_v, downb_v, g2_v, b2_v)):
        vec_s[i : i + 1, :] = v[...].reshape(1, -1)
    n_bits = n_dp.bit_length() - 1
    tokens, width = tok.shape
    hidden = win.shape[1]
    half = width // 2
    other = 1 - mp
    core_id = (dp, other)

    local = [
        pltpu.make_async_copy(src, dst, loc_sem.at[i])
        for i, (src, dst) in enumerate(
            ((tok_h, tok), (qkvw_h, wqkv.at[mp]), (outw_h, wout), (inw_h, win), (downw_h, wdown), (cot_h, cot))
        )
    ]
    for copy in local[:2]:
        copy.start()
    open_ = dict(enumerate(local))
    def take(i):
        open_.pop(i).wait()

    def dp_partner(b):
        return (dp + (1 << b) * (1 - 2 * ((dp // (1 << b)) % 2)), mp)

    barrier = pltpu.get_barrier_semaphore()
    partners = [core_id] + [dp_partner(b) for b in reversed(range(2, n_bits))] + [dp_partner(b) for b in range(2)]
    for there in partners:
        pl.semaphore_signal(barrier, inc=1, device_id=there, device_id_type=MESH)

    r0, r1, r2, r3 = (range_s[i] for i in range(4))
    i0, i1, i2, i3 = (1.0 / r for r in (r0, r1, r2, r3))

    qvb[mp] = qvb_v[...]
    take(0)
    rb = 256
    def rows_at(i, size=rb):
        return pl.ds(pl.multiple_of(i * size, size), size)

    def clip_rows(i, peak):
        v = tok[rows_at(i), :].astype(WIDE)
        clip_in[rows_at(i), :] = (r0 * jnp.tanh(v * i0)).astype(LOW)
        return jnp.maximum(peak, jnp.max(jnp.abs(v), axis=0, keepdims=True))

    peak_s[0:1, :] = lax.fori_loop(0, tokens // rb, clip_rows, jnp.zeros((1, width), WIDE), unroll=4)
    stats[...] = jnp.zeros_like(stats)
    lane = lax.broadcasted_iota(jnp.int32, (1, 128), 1)
    in_head = [lane < HD, lane >= HD]
    qb = 256

    def project(part):
        for j in range(3):
            out = dot(clip_in[...], wqkv[part, j])
            if j == 0:
                out = (out + qvb[part, 0:1, :]).astype(LOW).astype(WIDE) * (HD ** -0.5)
            elif j == 2:
                out = out + qvb[part, 1:2, :]
            qkv[j, part] = out.astype(LOW)

    def attend(part):
        def pair(t, carry):
            at = pl.ds(pl.multiple_of(t * 128, 128), 128)
            k, v = qkv[1, part, :, at], qkv[2, part, :, at]
            nil, one = jnp.zeros_like(v), jnp.ones_like(v)
            kz = [jnp.where(m, k, nil) for m in in_head]
            vz = [jnp.concatenate([jnp.where(m, v, nil), jnp.where(m, one, nil)], axis=1) for m in in_head]
            vz = jnp.concatenate(vz, axis=0)
            head = part * 6 + t * 2
            for i in range(tokens // qb):
                rows = pl.ds(i * qb, qb)
                q = qkv[0, part, rows, at]
                es, tops = [], []
                for h in range(2):
                    s = dot_nt(q, kz[h]) + bias[rows, :]
                    tops.append(jnp.max(s, axis=-1, keepdims=True))
                    es.append(jnp.exp(s - tops[h]).astype(LOW))
                both = dot(jnp.concatenate(es, axis=1), vz)
                norm = both[:, 128:]
                ctx[rows, pl.ds(pl.multiple_of(part * half + t * 128, 128), 128)] = both[:, :128] / norm
                total = jnp.where(in_head[0], tops[0], tops[1]) + jnp.log(norm)
                found = jnp.where(lane == head, total[:, 0:1], stats[rows, :])
                stats[rows, :] = jnp.where(lane == head + 1, total[:, HD : HD + 1], found)
            return carry

        lax.fori_loop(0, half // 128, pair, 0, unroll=True)

    take(1)
    project(mp)
    pl.semaphore_wait(barrier, len(partners))
    weight_copies = [
        pltpu.make_async_remote_copy(
            src_ref=src, dst_ref=dst, send_sem=wsend.at[i], recv_sem=wrecv.at[i], device_id=core_id, device_id_type=MESH
        )
        for i, (src, dst) in enumerate(((qkvw_h, wqkv.at[mp]), (qvb_v, qvb.at[mp])))
    ]
    for copy in weight_copies:
        copy.start()
    open_["w0"], open_["w1"] = weight_copies
    for copy in local[2:]:
        copy.start()
    row = jnp.sum(jnp.where(lax.broadcasted_iota(jnp.int32, seg_v.shape, 0) == mp, seg_v[...], 0), axis=0, keepdims=True).astype(WIDE)
    fill = fill_s[mp]
    seg_col = jnp.broadcast_to(row, (128, tokens)).T[:, 0:1]
    blk = 128

    for i in range(tokens // blk):
        kpos = lax.broadcasted_iota(jnp.int32, (blk, tokens), 1)
        qpos = lax.broadcasted_iota(jnp.int32, (blk, tokens), 0) + i * blk
        live = (kpos < fill) | (kpos == qpos)
        same = seg_col[i * blk : i * blk + blk] == row
        bias[i * blk : i * blk + blk, :] = jnp.where(same & live, 0.0, -1e30)

    attend(mp)
    take("w0")
    take("w1")
    project(other)
    attend(other)

    take(2)

    def mix_rows(i, peak):
        c = ctx[rows_at(i), :]
        clip_mid[rows_at(i), :] = (r1 * jnp.tanh(c * i1)).astype(LOW)
        return jnp.maximum(peak, jnp.max(jnp.abs(c), axis=0, keepdims=True))

    peak_s[1:2, :] = lax.fori_loop(0, tokens // rb, mix_rows, jnp.zeros((1, width), WIDE), unroll=4)
    interleave(mixed_t, lambda part: clip_mid[:, half * part : half * part + half].astype(WIDE))
    h2[...] = dot(clip_mid[...], wout[...])

    def norm(v):
        center = v - jnp.mean(v, axis=-1, keepdims=True)
        inv = lax.rsqrt(jnp.mean(center * center, axis=-1, keepdims=True) + EPSILON)
        return center * inv, inv

    def norm1_rows(i, peak):
        rows = rows_at(i)
        xhat, inv = norm(tok[rows, :].astype(WIDE) + (h2[rows, :] + vec_s[0:1, :]))
        xhat1[rows, :] = xhat
        stats[rows, :] = jnp.where(lane == 127, inv, stats[rows, :])
        normed = xhat * vec_s[1:2, :] + vec_s[2:3, :]
        h2[rows, :] = normed + vec_s[3:4, :]
        clip_mid[rows, :] = (r2 * jnp.tanh(normed * i2)).astype(LOW)
        return jnp.maximum(peak, jnp.max(jnp.abs(normed), axis=0, keepdims=True))

    peak_s[2:3, :] = lax.fori_loop(0, tokens // rb, norm1_rows, jnp.zeros((1, width), WIDE), unroll=1)
    interleave(clip_mid_t, lambda part: clip_mid[:, half * part : half * part + half].astype(WIDE))

    take(3)
    take(4)
    fb, fr = pre_b.shape[1], 64
    pre_s, act_s = (d_h1.at[:, 0:fb], pre_b), (act_a, act_b)
    n_fb = hidden // fb

    def feed_in(b):
        pre_s[b % 2][...] = dot(clip_mid[...], win[:, fb * b : fb * b + fb])

    def feed_act(b, peak):
        cols = slice(fb * b, fb * b + fb)
        for r in range(0, tokens, fr):
            rows = slice(r, r + fr)
            pre = pre_s[b % 2][rows, :] + inb_v[:, cols]
            cdf = 0.5 + 0.5 * lax.erf(pre * SQRT_HALF)
            act = pre * cdf
            th = jnp.tanh(act * i3)
            act_s[b % 2][rows, :] = (r3 * th).astype(LOW)
            bell = jnp.exp(pre * pre * -0.5) * INV_SQRT_2PI
            slope_f[rows, cols] = ((1.0 - th * th) * (cdf + pre * bell)).astype(LOW)
            peak = jnp.maximum(peak, jnp.max(jnp.abs(act), axis=0, keepdims=True))
        return peak

    def feed_out(b):
        out = act_s[b % 2][...]
        flipped = out.T
        for i in range(fb // 32):
            group = b * (fb // 32) + i
            owner = group // 3
            clip_act_t[owner % 2, group % 3, owner // 2] = flipped[32 * i : 32 * i + 32]
        h2[...] += dot(out, wdown[fb * b : fb * b + fb, :])

    peak3 = jnp.zeros((1, fb), WIDE)
    feed_in(0)
    for b in range(n_fb):
        if b + 1 < n_fb:
            feed_in(b + 1)
        peak3 = feed_act(b, peak3)
        if b > 0:
            feed_out(b - 1)
    feed_out(n_fb - 1)
    peak_s[3:4, :] = jnp.zeros_like(peak_s[3:4, :])
    peak_s[3:4, 0:fb] = peak3

    take(5)
    zero_row = jnp.zeros((1, width), WIDE)

    def norm2_rows(i, sums):
        rows = rows_at(i)
        xhat, inv = norm(h2[rows, :])
        e = cot[rows, :].astype(WIDE)
        clip_in_row = (xhat * vec_s[4:5, :] + vec_s[5:6, :]).astype(LOW)
        clip_mid[rows, :] = clip_in_row
        w = e * vec_s[4:5, :]
        d = inv * (w - jnp.mean(w, axis=-1, keepdims=True) - xhat * jnp.mean(w * xhat, axis=-1, keepdims=True))
        h2[rows, :] = d
        low = d.astype(LOW)
        cot[rows, :] = low
        return (
            sums[0] + jnp.sum(e * xhat, axis=0, keepdims=True),
            sums[1] + jnp.sum(e, axis=0, keepdims=True),
            sums[2] + jnp.sum(low.astype(WIDE), axis=0, keepdims=True),
        )

    gain2, shift2, down_bias = lax.fori_loop(0, tokens // rb, norm2_rows, (zero_row, zero_row, zero_row), unroll=1)
    lay_copy = pltpu.make_async_copy(clip_mid, lay_h, loc_sem.at[6])
    lay_copy.start()

    sm[...] = jnp.zeros_like(sm)
    sm[7:8, :] = down_bias
    sm[8:9, :] = gain2
    sm[9:10, :] = shift2
    lane_w = lax.broadcasted_iota(jnp.int32, (1, width), 1)
    peaks = zero_row
    for i in range(4):
        peaks = jnp.where(lane_w == i, jnp.max(peak_s[i : i + 1, :], axis=-1, keepdims=True), peaks)
    sm[12:13, :] = peaks

    scatter = Scatter(
        n_low,
        {"down": acc_d, "wide": acc_w},
        {"down": cs_d, "wide": cs_w},
        {"down": cr_d, "wide": cr_w},
        {"down": (rd1, rd2, rd3, rd4), "wide": (rw1, rw2, rw3, rw4)},
        msend,
        mrecv,
    )

    leaving = []

    def leave(src, dst):
        leaving.append(pltpu.make_async_copy(src, dst, out_sem.at[len(leaving)]))
        leaving[-1].start()

    def out_down(index):
        def write(total):
            rows = pl.ds(32 * index, 32)
            gdown[rows, :] = total
            leave(gdown.at[rows], gdown_h.at[rows])

        return write

    def out_wide(ref, there, at):
        def write(total):
            both = jnp.concatenate([total[:24], total[24:]], axis=1)
            if ref is gqkv:
                ref[at] = both
                leave(ref.at[at], there.at[at])
            else:
                cols = pl.ds(width * at, width)
                ref[:, cols] = both
                leave(ref.at[:, cols], there.at[:, cols])

        return write

    outs = [out_down(i) for i in range(3)] + [out_wide(gin, gin_h, i) for i in range(4)]
    outs += [out_wide(gout, gout_h, 0)] + [out_wide(gqkv, gqkv_h, i) for i in range(3)]

    def step(m, stage):
        scatter.step(m, stage, outs[m])

    def send_part(group, index, result):
        scatter.slot_free(group, index)
        store_chunks(cs_d if group == "down" else cs_w, index % SLOTS[group], group, index, result)
        scatter.core_copy(group, index).start()

    def own_part(group, index, result):
        store_chunks(acc_d if group == "down" else acc_w, index, group, index, result)

    def down_send(i):
        send_part("down", i, dot(clip_act_t[other, i].reshape(16 * 32, tokens), cot[...]))

    def down_own(i):
        own_part("down", i, dot(clip_act_t[mp, i].reshape(16 * 32, tokens), cot[...]))

    d_pre = clip_mid

    def block(i):
        return pl.ds(pl.multiple_of(i * width, width), width)

    def in_send(i):
        d_pre[...] = (dot_nt(cot[...], wdown[block(i), :]) * slope_f[:, block(i)].astype(WIDE)).astype(LOW)
        send_part("wide", i, dot(clip_mid_t[other], d_pre[...]))

    def in_own(i):
        own_part("wide", i, dot(clip_mid_t[mp], d_pre[...]))
        sm[pl.ds(3 + i, 1), :] = jnp.sum(d_pre[...].astype(WIDE), axis=0, keepdims=True)

    def in_back(i):
        d_h1[...] += dot_nt(d_pre[...], win[:, block(i)])

    def norm1_back(_):
        def some(i, sums):
            rows = rows_at(i)
            xhat = xhat1[rows, :]
            inv = stats[rows, 127:128]
            th = jnp.tanh((xhat * vec_s[1:2, :] + vec_s[2:3, :]) * i2)
            e = h2[rows, :] + d_h1[rows, :] * (1.0 - th * th)
            w = e * vec_s[1:2, :]
            d = inv * (w - jnp.mean(w, axis=-1, keepdims=True) - xhat * jnp.mean(w * xhat, axis=-1, keepdims=True))
            d_h1[rows, :] = d
            low = d.astype(LOW)
            cot[rows, :] = low
            return (
                sums[0] + jnp.sum(e * xhat, axis=0, keepdims=True),
                sums[1] + jnp.sum(e, axis=0, keepdims=True),
                sums[2] + jnp.sum(low.astype(WIDE), axis=0, keepdims=True),
            )

        gain1, shift1, out_bias = lax.fori_loop(0, tokens // rb, some, (zero_row, zero_row, zero_row), unroll=4)
        sm[0:1, :] = out_bias
        sm[1:2, :] = gain1
        sm[2:3, :] = shift1

    def out_send(_):
        send_part("wide", 4, dot(mixed_t[other], cot[...]))

    def out_own(_):
        own_part("wide", 4, dot(mixed_t[mp], cot[...]))

    def mixed_back(_):
        h2[...] = dot_nt(cot[...], wout[...])

    def context_back(_):
        def some(i, carry):
            rows = rows_at(i)
            th = jnp.tanh(ctx[rows, :] * i1)
            clip_mid[rows, :] = (h2[rows, :].astype(LOW).astype(WIDE) * (1.0 - th * th)).astype(LOW)
            return carry

        lax.fori_loop(0, tokens // rb, some, 0, unroll=4)

    def attend_back(part, t):
        at = pl.ds(pl.multiple_of(t * 128, 128), 128)
        wide_at = pl.ds(pl.multiple_of(part * half + t * 128, 128), 128)
        k, v = qkv[1, part, :, at], qkv[2, part, :, at]
        split = lambda v: [jnp.where(m, v, jnp.zeros_like(v)) for m in in_head]
        kz, vz = split(k), split(v)
        d_k, d_v = jnp.zeros((tokens, 128), WIDE), jnp.zeros((tokens, 128), WIDE)
        for i in range(tokens // qb):
            rows = pl.ds(i * qb, qb)
            q = qkv[0, part, rows, at]
            dc = clip_mid[rows, wide_at]
            prod = dc.astype(WIDE) * ctx[rows, wide_at]
            found = stats[rows, :]
            ps, ds = [], []
            for h in range(2):
                mean = jnp.sum(jnp.where(in_head[h], prod, 0.0), axis=-1, keepdims=True)
                total = jnp.sum(jnp.where(lane == (part * 6 + t * 2 + h), found, 0.0), axis=-1, keepdims=True)
                p = jnp.exp(dot_nt(q, kz[h]) + bias[rows, :] - total)
                ds.append((p * (dot_nt(dc, vz[h]) - mean)).astype(LOW))
                ps.append(p.astype(LOW))
            d_q = dot(jnp.concatenate(ds, axis=1), jnp.concatenate(kz, axis=0))
            d_k = d_k + dot_tn(jnp.concatenate(ds, axis=0), jnp.concatenate(split(q), axis=0))
            d_v = d_v + dot_tn(jnp.concatenate(ps, axis=0), jnp.concatenate(split(dc), axis=0))
            qkv[0, part, rows, at] = (d_q * (HD ** -0.5)).astype(LOW)
        qkv[1, part, :, at] = d_k.astype(LOW)
        qkv[2, part, :, at] = d_v.astype(LOW)

    def qkv_send(j):
        send_part("wide", 5 + j, dot_tn(qkv[j, other], clip_in[...]))

    def qkv_own(j):
        own_part("wide", 5 + j, dot_tn(qkv[j, mp], clip_in[...]))

    def head_sums(_):
        for r, j in ((10, 0), (11, 2)):
            for part in range(2):
                sm[r : r + 1, half * part : half * part + half] = jnp.sum(qkv[j, part].astype(WIDE), axis=0, keepdims=True)
        small_copy(0).start()
        h2[...] = jnp.zeros_like(h2)

    def in_tokens(j):
        both = jnp.concatenate([qkv[j, 0], qkv[j, 1]], axis=1)
        h2[...] += dot_nt(both, jnp.concatenate([wqkv[0, j], wqkv[1, j]], axis=1))

    def token_grad(_):
        def some(i, carry):
            rows = rows_at(i)
            th = jnp.tanh(tok[rows, :].astype(WIDE) * i0)
            d_h1[rows, :] += h2[rows, :] * (1.0 - th * th)
            return carry

        lax.fori_loop(0, tokens // rb, some, 0, unroll=4)
        tok_copy.start()

    tok_copy = pltpu.make_async_copy(d_h1, gtok_h, loc_sem.at[7])

    def small_copy(k):
        return pltpu.make_async_remote_copy(
            src_ref=sm,
            dst_ref=sm_r.at[k],
            send_sem=ssend.at[k],
            recv_sem=srecv.at[k],
            device_id=partners[k],
            device_id_type=MESH,
        )

    def small_end(k):
        small_copy(k).wait()
        is_peak = lax.broadcasted_iota(jnp.int32, sm.shape, 0) == 12
        sm[...] = jnp.where(is_peak, jnp.maximum(sm[...], sm_r[k]), sm[...] + sm_r[k])
        if k + 1 < len(partners):
            small_copy(k + 1).start()
        else:
            small_results()

    def small_results():
        per = width // (2 * n_dp)
        me = dp * 2 + mp
        sums = sm[...]
        out = pltpu.roll(sums, (width - per * me) % width, 1)[:, :128]
        qv_out = pltpu.roll(sums, (width - (mp * half + per * dp)) % width, 1)[:, :128]
        wide_at = 4 * per * me
        in_rows = pltpu.roll(sums, (width - wide_at % width) % width, 1)[:, :128]
        r_iota = lax.broadcasted_iota(jnp.int32, out.shape, 0)
        in_row = jnp.sum(jnp.where(r_iota == 3 + wide_at // width, in_rows, 0.0), axis=0, keepdims=True)
        out = jnp.where((r_iota == 10) | (r_iota == 11), qv_out, out)
        out = jnp.where(r_iota == 3, in_row, out)
        small_o[...] = out
        small_o[12:13, 0:4] = MOMENTUM * act_v[...] + (1.0 - MOMENTUM) * sums[12:13, 0:4]
        leave(small_o, small_h)

    parts = {
        "Dp": down_send, "Do": down_own, "Ip": in_send, "Io": in_own, "In": in_back, "LN": norm1_back, "Op": out_send, "Oo": out_own,
        "dm": mixed_back, "cx": context_back, "ab": lambda t: attend_back(other, t), "am": lambda t: attend_back(mp, t),
        "Qp": qkv_send, "Qo": qkv_own, "hs": head_sums, "dc": in_tokens, "tk": token_grad, "sm": small_end,
    }
    d_h1[...] = jnp.zeros_like(d_h1)

    def run(which, n):
        if isinstance(which, str):
            parts[which](n)
        else:
            step(which, n)

    def loop(names, count, after):
        def round_(i, carry):
            for name in names:
                parts[name](i)
                for k in range(count):
                    todo = after.get((name, k), ())
                    if todo:
                        pl.when(i == k)(lambda todo=todo: [run(*which) for which in todo] and None)
            return carry

        lax.fori_loop(0, count, round_, 0)

    for entry in SCHEDULE:
        if len(entry) == 3:
            if "Ip" in entry[0]:
                lay_copy.wait()
            loop(entry[0], entry[1], dict(entry[2]))
        else:
            run(*entry)
    for k in range(5, len(partners)):
        small_end(k)
    scatter.finish()

    tok_copy.wait()
    for copy in leaving:
        copy.wait()


def hand_out(per, *refs):
    big, small_h, outs, held, short, small, sem = refs[:6], refs[6], refs[7:22], refs[22:28], refs[28:37], refs[37], refs[38]
    pieces = []
    for i, src in enumerate(big):
        size = src.shape[0] // (4 if i < 2 else 1)
        pieces += [(i, pl.ds(at, size)) for at in range(0, src.shape[0], size)]
    ins = [pltpu.make_async_copy(big[i].at[at], held[i].at[at], sem.at[0, n]) for n, (i, at) in enumerate(pieces)]
    away = [pltpu.make_async_copy(held[i].at[at], outs[i].at[at], sem.at[1, n]) for n, (i, at) in enumerate(pieces)]
    last = len(pieces)
    first = pltpu.make_async_copy(small_h, small, sem.at[0, last])
    first.start()
    for copy in ins:
        copy.start()
    away += [pltpu.make_async_copy(src, dst, sem.at[1, last + n]) for n, (src, dst) in enumerate(zip(short, outs[6:]))]
    first.wait()
    short[0][...] = small[10:12, :per]
    for ref, row in zip(short[1:], (0, 1, 2, 3, 7, 8, 9, 12)):
        ref[...] = small[row, : ref.shape[0]]
    for copy in away[last:]:
        copy.start()
    for here, there in zip(ins, away):
        here.wait()
        there.start()
    for copy in away:
        copy.wait()


def per_device(n_dp, tokens, seg_ids, fill_len, qkv_weight, qv_bias, out_weight, out_bias, norm1_gain, norm1_bias, in_weight, in_bias,
               down_weight, down_bias, norm2_gain, norm2_bias, act_range, cotangent):
    n_tok, width = tokens.shape
    hidden = in_weight.shape[1]
    half = width // 2
    n_low = max(1, n_dp // 16)
    any_, vmem = pl.BlockSpec(memory_space=pl.ANY), pl.BlockSpec(memory_space=pltpu.VMEM)
    smem = pl.BlockSpec(memory_space=pltpu.SMEM)
    chunk = width // 32
    shape = jax.ShapeDtypeStruct
    low = lambda *s: pltpu.VMEM(s, LOW)
    wide = lambda *s: pltpu.VMEM(s, WIDE)
    dma = lambda *s: pltpu.SemaphoreType.DMA(s)
    n_partners = n_dp.bit_length()
    n_wide = N_MSG - 3
    outs = pl.pallas_call(
        functools.partial(kernel, n_dp, n_low),
        out_shape=(
            shape((n_tok, width), LOW),
            shape((n_tok, width), WIDE),
            shape((3, chunk, width), WIDE),
            shape((chunk, width), WIDE),
            shape((chunk, hidden), WIDE),
            shape((4 * chunk, width), WIDE),
            shape((16, 128), WIDE),
        ),
        in_specs=[any_, vmem, smem, any_, vmem, any_, vmem, vmem, vmem, any_, vmem, any_, vmem, vmem, vmem, vmem, smem, any_],
        out_specs=(any_,) * 7,
        scratch_shapes=[
            low(n_tok, width), low(n_tok, width), low(2, 3, width, half), wide(2, 2, half), low(width, width), low(width, hidden), low(hidden, width),
            low(n_tok, width), low(3, 2, n_tok, half), wide(n_tok, n_tok), wide(n_tok, width), wide(n_tok, 128), low(2, half, n_tok),
            wide(n_tok, width), low(n_tok, width), low(2, half, n_tok), low(2, 3, 16, 32, n_tok), low(n_tok, hidden),
            wide(n_tok, width), wide(n_tok, width), wide(n_tok, 512), low(n_tok, 512), low(n_tok, 512), wide(8, width), wide(8, width), wide(16, width), wide(n_partners, 16, width),
            low(3, 16, 32, width), low(n_wide, 16, 48, half), low(3, 16, 32, width), low(2, 16, 48, half), low(3, 16, 32, width), low(n_wide, 16, 48, half),
            *(low(3, 16 >> k, 32, width) for k in range(1, 5)), *(low(n_wide, 16 >> k, 48, half) for k in range(1, 5)),
            wide(16, 128), wide(3, chunk, width), wide(chunk, width), wide(chunk, hidden), wide(4 * chunk, width), dma(N_MSG + 1),
            dma(8), dma(2), dma(2), dma(N_MSG, 5, 2), dma(N_MSG, 5, 2), dma(n_partners), dma(n_partners),
        ],
        compiler_params=pltpu.CompilerParams(collective_id=0, has_side_effects=True, vmem_limit_bytes=64 * 2**20 - 2**16),
        cost_estimate=pl.CostEstimate(flops=25_000_000_000, bytes_accessed=24_000_000, transcendentals=12_000_000),
    )(
        tokens, seg_ids, fill_len, jnp.transpose(qkv_weight, (1, 0, 2)), qv_bias, out_weight, out_bias, norm1_gain,
        norm1_bias, in_weight, in_bias.reshape(1, hidden), down_weight, down_bias, norm2_gain,
        norm2_bias, act_range.reshape(1, 4), act_range, cotangent,
    )
    layer_out, grad_tokens, qkv_sum, sum_out, sum_in, sum_down, small = outs
    if n_low > 1:
        groups = [[top * n_low + low_ for low_ in range(n_low)] for top in range(16)]
        moves = [((top * n_low + i) * 2 + core, n_low * (2 * top + core) + i) for top in range(16) for i in range(n_low) for core in range(2)]

        def spread(v, dim):
            return lax.psum_scatter(v, "dp", scatter_dimension=dim, axis_index_groups=groups, tiled=True)

        qkv_sum = spread(qkv_sum, 1)
        sum_out, sum_in, sum_down = (lax.ppermute(spread(v, 0), ("dp", "mp"), moves) for v in (sum_out, sum_in, sum_down))
    per = width // (2 * n_dp)
    rows = (per, per, per, 4 * per, per, per, per)
    vectors = [shape((size,), WIDE) for size in rows]
    big = (layer_out, grad_tokens, qkv_sum, sum_out, sum_in, sum_down)
    done = pl.pallas_call(
        functools.partial(hand_out, per),
        out_shape=(*(shape(v.shape, v.dtype) for v in big), shape((2, per), WIDE), *vectors, shape((4,), WIDE)),
        in_specs=[any_] * (len(big) + 1),
        out_specs=(any_,) * (len(big) + 9),
        scratch_shapes=[
            *(pltpu.VMEM(v.shape, v.dtype) for v in (*big, shape((2, per), WIDE), *vectors, shape((4,), WIDE), small)),
            dma(2, len(big) + 15),
        ],
        compiler_params=pltpu.CompilerParams(vmem_limit_bytes=64 * 2**20 - 2**16),
    )(*big, small)
    layer_out, grad_tokens, qkv_sum, sum_out, sum_in, sum_down, sum_qv, out_b, gain1, shift1, in_b, down_b, gain2, shift2, new_range = done
    qkv_sum = jnp.transpose(qkv_sum, (2, 0, 1))
    return (
        layer_out, grad_tokens, qkv_sum, sum_qv, sum_out, out_b, gain1, shift1, sum_in, in_b, sum_down, down_b, gain2, shift2, new_range,
    )


def solution(mesh):
    n_dp = mesh.shape["dp"]
    both, copies = P(("dp", "mp")), P()
    rows = P(("dp", "mp"), None)
    return jax.shard_map(
        functools.partial(per_device, n_dp),
        mesh=mesh,
        in_specs=(
            rows, P("dp", None), P("dp"), P(None, None, "mp"), P(None, "mp"),
            *([copies] * 11), rows,
        ),
        out_specs=(
            rows, rows, P(None, None, ("mp", "dp")), P(None, ("mp", "dp")), rows, both, both, both, rows, both, rows, both, both, both, copies,
        ),
        check_vma=False,
    )
```
